32 devices in a mesh: shot: 8 (over y, x, core), slab: 4 (over z).
Axes of the slice: x: 2, y: 2, z: 4, core: 2. Of those that a mesh axis runs over, the one named last changes fastest.
Arguments:
- velocity: float32 [64, 64, 128], P('slab', 'shot'), may hold values from 1.5 to 4.5
- aperture_start: int32 [8], P('shot'), may hold values from 0 to 4, as said below
- aperture_count: int32 [8], P('shot'), may hold values from 1 to 4
- wave_prev: float32 [8, 64, 32, 128], P('shot', 'slab'), may hold values from -6 to 6
- wave_now: float32 [8, 64, 32, 128], P('shot', 'slab'), may hold values from -6 to 6
- adjoint_prev: float32 [8, 64, 32, 128], P('shot', 'slab'), may hold values from -6 to 6
- adjoint_now: float32 [8, 64, 32, 128], P('shot', 'slab'), may hold values from -6 to 6
- source_cells: int32 [8, 4, 3], P('shot'), may hold values from 0 to 127, as said below
- wavelet: float32 [8, 4, 4], P('shot'), may hold values from -6 to 6
- receiver_cells: int32 [8, 16, 3], P('shot'), may hold values from 0 to 127, as said below
- trace: float32 [8, 4, 16], P('shot'), may hold values from -6 to 6
Outputs:
- wave_final: float32 [8, 64, 32, 128], P('shot', 'slab')
- adjoint_final: float32 [8, 64, 32, 128], P('shot', 'slab')
- gradient: float32 [64, 64, 128], P('slab', 'shot')
The draws below stay inside these ranges and needn't reach their ends.
Inputs may be any that keep to these rules, and one draw needn't show every extreme that they name: aperture_start[g] lies between g - 3 and g, and at most 4. `source_cells`: x below 64, window y below 8, z below 128. `receiver_cells`: x below 64, window y below 8, z below 128.
All inputs are finite; a program needn't handle non-finite values.
Results may differ from the reference program's by a relative error of at most 0.0003.
Values sent between devices are 32-bit elements; how exact they have to be, the bound alone decides.
No kernel may reach another device: no remote copies, remote signals or barrier semaphores. Data moves between devices by JAX's collectives and lax.ppermute only.
A program may use at most 64 MiB of HBM per device.

```python
import jax
import jax.numpy as jnp
from jax import lax

BY = 8
NZ = 128
APER = 4
STEPS = 4
SRC = 4
REC = 16
GROUPS = 8
NX = 64
NY = 64
WY = 32


def cell_list(key, count):
    key_x, key_y, key_z = jax.random.split(key, 3)
    across = jax.random.randint(key_x, (GROUPS, count), 0, NX)
    inward = jax.random.randint(key_y, (GROUPS, count), 0, BY)
    downward = jax.random.randint(key_z, (GROUPS, count), 0, NZ)
    across = across.at[0, 0].set(NX - 1)
    across = across.at[0, count - 1].set(0)
    downward = downward.at[0, 0].set(NZ - 1)
    return jnp.stack([across, inward, downward], -1).astype(jnp.int32)


def draw_aperture_start(key, part):
    key = jax.random.fold_in(key, 11)
    jitter = jax.random.randint(key, (GROUPS,), 0, APER)
    centre = jnp.arange(GROUPS, dtype=jnp.int32) - (APER - 1) + jitter
    return jnp.clip(centre, 0, GROUPS - APER).astype(jnp.int32)


def draw_aperture_count(key, part):
    key = jax.random.fold_in(key, 12)
    counts = jax.random.randint(key, (GROUPS,), 1, APER + 1)
    return counts.at[0].set(APER).astype(jnp.int32)


def draw_source_cells(key, part):
    key = jax.random.fold_in(key, 13)
    return cell_list(key, SRC)


def draw_receiver_cells(key, part):
    key = jax.random.fold_in(key, 14)
    return cell_list(key, REC)


def level_of(rng, shape, shards, low, largest):
    gain = 1.0
    for axis_at, blocks in shards:
        heights = jax.random.uniform(jax.random.fold_in(jax.random.fold_in(rng, 6), axis_at), (blocks,), jnp.float32, low / len(shards), largest / len(shards))
        gain = gain * jnp.repeat(jnp.exp(heights), shape[axis_at] // blocks).reshape((-1,) + (1,) * (len(shape) - 1 - axis_at))
    return gain


def scatter_about(own_key, dims, width, bound, shards=(), kind=jnp.bfloat16):
    values = width * jax.random.normal(own_key, dims, jnp.float32)
    if shards:
        values = values * level_of(own_key, dims, shards, -0.22, 0.18)
    return jnp.clip(values, -bound, bound).astype(kind)


def setup_inputs(seed: int = 0) -> dict:
    splits = jax.random.split(jax.random.key(seed), 12)
    return {
        "velocity": jnp.clip(1.5 + 3.0 * jax.random.uniform(splits[0], (NX, NY, NZ), jnp.float32) ** level_of(splits[0], (NX, NY, NZ), ((0, 4), (1, 8)), -0.2, 0.2), 1.5, 4.5),
        "aperture_start": draw_aperture_start(jax.random.fold_in(splits[11], 71), 0),
        "aperture_count": draw_aperture_count(jax.random.fold_in(splits[11], 71), 0),
        "wave_prev": scatter_about(splits[3], (GROUPS, NX, WY, NZ), 1.0, 6.0, ((0, 8), (1, 4)), jnp.float32),
        "wave_now": scatter_about(splits[4], (GROUPS, NX, WY, NZ), 1.0, 6.0, ((0, 8), (1, 4)), jnp.float32),
        "adjoint_prev": scatter_about(splits[5], (GROUPS, NX, WY, NZ), 1.0, 6.0, ((0, 8), (1, 4)), jnp.float32),
        "adjoint_now": scatter_about(splits[6], (GROUPS, NX, WY, NZ), 1.0, 6.0, ((0, 8), (1, 4)), jnp.float32),
        "source_cells": draw_source_cells(jax.random.fold_in(splits[11], 71), 0),
        "wavelet": scatter_about(splits[8], (GROUPS, STEPS, SRC), 1.0, 6.0, ((0, 8),), jnp.float32),
        "receiver_cells": draw_receiver_cells(jax.random.fold_in(splits[11], 71), 0),
        "trace": scatter_about(splits[10], (GROUPS, STEPS, REC), 1.0, 6.0, ((0, 8),), jnp.float32),
    }


stencil_weights = (-205.0 / 72.0, 8.0 / 5.0, -1.0 / 5.0, 8.0 / 315.0, -1.0 / 560.0)
time_step = 0.09


def stencil(padded):
    size_x = padded.shape[-3] - 8
    size_y = padded.shape[-2] - 8
    size_z = padded.shape[-1] - 8
    center = padded[..., 4:4 + size_x, 4:4 + size_y, 4:4 + size_z]
    total = (3.0 * stencil_weights[0]) * center
    for k in range(1, 5):
        near = padded[..., 4 + k:4 + k + size_x, 4:4 + size_y, 4:4 + size_z]
        near = near + padded[..., 4 - k:4 - k + size_x, 4:4 + size_y, 4:4 + size_z]
        near = near + padded[..., 4:4 + size_x, 4 + k:4 + k + size_y, 4:4 + size_z]
        near = near + padded[..., 4:4 + size_x, 4 - k:4 - k + size_y, 4:4 + size_z]
        near = near + padded[..., 4:4 + size_x, 4:4 + size_y, 4 + k:4 + k + size_z]
        near = near + padded[..., 4:4 + size_x, 4:4 + size_y, 4 - k:4 - k + size_z]
        total = total + stencil_weights[k] * near
    return total


def inject(cells, amps, x_cells, rows, depth):
    along_x = (x_cells[:, None] == cells[None, :, 0]).astype(jnp.float32) * amps[None, :]
    along_y = (jnp.arange(rows)[:, None] == cells[None, :, 1]).astype(jnp.float32)
    along_z = (jnp.arange(depth)[:, None] == cells[None, :, 2]).astype(jnp.float32)
    return jnp.einsum("xs,ys,zs->xyz", along_x, along_y, along_z, precision=lax.Precision.HIGHEST)


def reference(velocity, aperture_start, aperture_count, wave_prev, wave_now, adjoint_prev, adjoint_now, source_cells, wavelet, receiver_cells, trace):
    rows = APER * BY
    x_cells = jnp.arange(NX)
    zero = jnp.zeros((), jnp.int32)

    def one_group(total, items):
        start_block, live_count, w_prev, w_now, j_prev, j_now, sources, amps, receivers, recorded = items
        anchor = (start_block * BY).astype(jnp.int32)
        window = lax.dynamic_slice(velocity, (zero, anchor, zero), (NX, rows, NZ))
        live = (jnp.arange(rows) < live_count * BY).astype(jnp.float32)[None, :, None]
        courant = window * window * (time_step * time_step)
        imaging = (2.0 * time_step * time_step) * window
        w_prev = w_prev * live
        w_now = w_now * live
        j_prev = j_prev * live
        j_now = j_now * live
        grad = jnp.zeros((NX, rows, NZ), jnp.float32)
        for step in range(STEPS):
            stacked = jnp.stack([w_now, j_now])
            padded = jnp.pad(stacked, ((0, 0), (4, 4), (4, 4), (4, 4)))
            lapl = stencil(padded)
            grad = grad + imaging * j_now * lapl[0]
            w_next = (2.0 * w_now - w_prev + courant * lapl[0] + inject(sources, amps[step], x_cells, rows, NZ)) * live
            j_next = (2.0 * j_now - j_prev + courant * lapl[1] + inject(receivers, recorded[step], x_cells, rows, NZ)) * live
            w_prev, w_now = w_now, w_next
            j_prev, j_now = j_now, j_next
        current = lax.dynamic_slice(total, (zero, anchor, zero), (NX, rows, NZ))
        total = lax.dynamic_update_slice(total, current + grad, (zero, anchor, zero))
        return total, (w_now, j_now)

    begin = jnp.zeros((NX, NY, NZ), jnp.float32)
    gradient, finals = lax.scan(one_group, begin, (aperture_start, aperture_count, wave_prev, wave_now, adjoint_prev, adjoint_now, source_cells, wavelet, receiver_cells, trace))
    return finals[0], finals[1], gradient
```

```python
import jax
import jax.numpy as jnp
import numpy as np
from jax import lax
from jax.experimental import pallas as pl
from jax.experimental.pallas import tpu as pltpu
from jax.sharding import PartitionSpec as P


SCALE = 5040.0
scaled_weights = (-14350.0, 8064.0, -1008.0, 128.0, -9.0)
time_step = 0.09
REACH = 4
TILE = 8


def swap_pairs(block, axis, first):
    count = lax.axis_size(axis)
    route = []
    for i in range(first, count - 1, 2):
        route += [(i, i + 1), (i + 1, i)]
    return lax.ppermute(block, axis, route)


def any_space():
    return pl.BlockSpec(memory_space=pl.ANY)


def in_hbm(array):
    return pltpu.with_memory_space_constraint(array, pltpu.HBM)


def packing_kernel(now_w, now_j, prev_w, prev_j, to_a, to_b, sems):
    cells = now_w.shape[1]
    deep_now = (to_a.shape[0] // 2 + REACH) // 2
    deep_prev = deep_now - REACH
    odd = lax.axis_index("slab") % 2
    copies = []
    for out, side in ((to_a, 1 - odd), (to_b, odd)):
        at = 0
        for field, deep in ((now_w, deep_now), (now_j, deep_now), (prev_w, deep_prev), (prev_j, deep_prev)):
            source = field.at[0, pl.ds(side * (cells - deep), deep)]
            copies.append(pltpu.make_async_copy(source, out.at[pl.ds(at, deep)], sems.at[len(copies)]))
            at += deep
    for copy in copies:
        copy.start()
    for copy in copies:
        copy.wait()


def pack(now_w, now_j, prev_w, prev_j, deep):
    rows, depth = now_w.shape[2:]
    out = pltpu.VMEM((4 * deep - 2 * REACH, rows, depth), jnp.float32)
    return pl.pallas_call(
        packing_kernel,
        out_shape=(out, out),
        in_specs=[pl.BlockSpec(memory_space=pltpu.HBM)] * 4,
        out_specs=(any_space(), any_space()),
        scratch_shapes=[pltpu.SemaphoreType.DMA((8,))],
        compiler_params=pltpu.CompilerParams(vmem_limit_bytes=1 << 20),
        cost_estimate=pl.CostEstimate(flops=0, bytes_accessed=4 << 20, transcendentals=0),
    )(*map(in_hbm, (now_w, now_j, prev_w, prev_j)))


def window_kernel(start, cells_w, cells_j, amps_w, amps_j, speeds, to_a, to_b, drops, sems):
    cells = speeds.shape[1]
    tiles, deep_prev = to_a.shape[:2]
    wide, depth = drops.shape[2], drops.shape[4]
    deep = deep_prev + REACH
    slab = lax.axis_index("slab")
    odd = slab % 2
    steps = amps_w.shape[1]
    start_block = start[0]
    copies = []
    for out, side in ((to_a, 1 - odd), (to_b, odd)):
        for tile in range(tiles):
            source = speeds.at[start_block + tile, pl.ds(side * (cells - deep_prev), deep_prev)]
            copies.append(pltpu.make_async_copy(source, out.at[tile], sems.at[len(copies)]))
    for copy in copies:
        copy.start()

    def clear(x, carry):
        for step in range(steps):
            for field in range(2):
                drops[step, field, x] = jnp.zeros((TILE, depth), jnp.float32)
        return carry

    lax.fori_loop(0, wide, clear, 0)
    row = lax.broadcasted_iota(jnp.int32, (TILE, depth), 0)
    col = lax.broadcasted_iota(jnp.int32, (TILE, depth), 1)

    def inject(field, places, amps):
        def one_cell(s, carry):
            x = places[0, 0, s] - (slab * cells - deep)

            @pl.when((x >= 0) & (x < wide))
            def _():
                here = (row == places[1, 0, s]) & (col == places[2, 0, s])
                for step in range(steps):
                    drops[step, field, x] = drops[step, field, x] + jnp.where(here, amps[0, step, s], 0.0)

            return carry

        lax.fori_loop(0, places.shape[2], one_cell, 0)

    inject(0, cells_w, amps_w)
    inject(1, cells_j, amps_j)
    for copy in copies:
        copy.wait()


def cut_window(start, cells_w, cells_j, amps_w, amps_j, speeds, tiles):
    cells, depth = speeds.shape[1], speeds.shape[3]
    steps = amps_w.shape[1]
    deep = steps * REACH
    out = pltpu.VMEM((tiles, deep - REACH, TILE, depth), jnp.float32)
    smem = pl.BlockSpec(memory_space=pltpu.SMEM)
    return pl.pallas_call(
        window_kernel,
        out_shape=(out, out, pltpu.VMEM((steps, 2, cells + 2 * deep, TILE, depth), jnp.float32)),
        in_specs=[smem] * 5 + [any_space()],
        out_specs=(any_space(), any_space(), pl.BlockSpec(memory_space=pltpu.VMEM)),
        scratch_shapes=[pltpu.SemaphoreType.DMA((2 * tiles,))],
        compiler_params=pltpu.CompilerParams(vmem_limit_bytes=8 << 20),
        cost_estimate=pl.CostEstimate(flops=1 << 20, bytes_accessed=2 << 20, transcendentals=0),
    )(start, cells_w, cells_j, amps_w, amps_j, in_hbm(speeds))


def steps_kernel(
    steps,
    start,
    count,
    now_w,
    now_j,
    prev_w,
    prev_j,
    from_a,
    from_b,
    speeds,
    speed_a,
    speed_b,
    drops,
    band,
    final_w,
    final_j,
    parts,
    one,
    two,
    model,
    grad,
    sems,
):
    cells, rows, depth = now_w.shape[1:]
    deep = steps * REACH
    deep_prev = deep - REACH
    wide = cells + 2 * deep
    tiles = rows // TILE
    odd = lax.axis_index("slab") % 2
    start_block = start[0]
    live = count[0]

    left_of_a = odd
    copies = []

    def bring(source, target):
        copy = pltpu.make_async_copy(source, target, sems.at[len(copies)])
        copy.start()
        copies.append(copy)

    inner = pl.ds(TILE, rows)
    for field, (now, prev) in enumerate(((now_w, prev_w), (now_j, prev_j))):
        bring(now.at[0], one.at[field, pl.ds(deep, cells), inner])
        bring(prev.at[0], two.at[field, pl.ds(deep, cells), inner])
        for buffer, on_left in ((from_a, left_of_a), (from_b, 1 - left_of_a)):
            at = (1 - on_left) * (deep + cells)
            bring(buffer.at[pl.ds(field * deep, deep)], one.at[field, pl.ds(at, deep), inner])
            at = on_left * REACH + (1 - on_left) * (deep + cells)
            bring(
                buffer.at[pl.ds(2 * deep + field * deep_prev, deep_prev)],
                two.at[field, pl.ds(at, deep_prev), inner],
            )
    for tile in range(tiles):
        bring(speeds.at[start_block + tile], model.at[tile, pl.ds(deep, cells)])
        for buffer, on_left in ((speed_a, left_of_a), (speed_b, 1 - left_of_a)):
            at = on_left * REACH + (1 - on_left) * (deep + cells)
            bring(buffer.at[tile], model.at[tile, pl.ds(at, deep_prev)])

    zero_tile = jnp.zeros((TILE, depth), jnp.float32)

    def clear_edges(x, carry):
        for buffer in (one, two):
            for field in range(2):
                buffer[field, x, pl.ds(0, TILE), :] = zero_tile
                buffer[field, x, pl.ds(TILE + rows, TILE), :] = zero_tile
        return carry

    lax.fori_loop(0, wide, clear_edges, 0)

    def clear_parts(b, carry):
        parts[b] = jnp.zeros(parts.shape[1:], jnp.float32)
        return carry

    lax.fori_loop(0, parts.shape[0], clear_parts, 0)

    for copy in copies:
        copy.wait()

    for tile in range(1, tiles):

        @pl.when(tile >= live)
        def _():
            def clear(x, carry):
                for buffer in (one, two):
                    for field in range(2):
                        buffer[field, x, pl.ds(TILE + tile * TILE, TILE), :] = zero_tile
                model[tile, x] = zero_tile
                return carry

            lax.fori_loop(0, wide, clear, 0)

    group = REACH

    def along_z(now, x):
        fields = [now[field, pl.ds(x, group), inner, :].reshape(group * rows, depth) for field in range(2)]
        cells_in = jnp.concatenate(fields, axis=0)
        high = cells_in.astype(jnp.bfloat16)
        low = (cells_in - high.astype(jnp.float32)).astype(jnp.bfloat16)
        return jnp.dot(
            jnp.concatenate([high, low], axis=1), band[...], preferred_element_type=jnp.float32
        )

    def advance(now, other, step, x_first, imaged):
        spread = along_z(now, x_first)
        for i in range(group):
            x = x_first + i
            speed = jnp.concatenate([model[tile, x] for tile in range(tiles)], axis=0)
            courant = speed * speed * (time_step * time_step / SCALE)
            pair = []
            for field in range(2):
                center = now[field, x, inner, :]
                lap = (3.0 * scaled_weights[0]) * center
                for k in range(1, REACH + 1):
                    near = now[field, x + k, inner, :] + now[field, x - k, inner, :]
                    near = near + now[field, x, pl.ds(TILE + k, rows), :]
                    near = near + now[field, x, pl.ds(TILE - k, rows), :]
                    lap = lap + scaled_weights[k] * near
                at = (field * group + i) * rows
                lap = lap + spread[at : at + rows]
                pair.append((center, lap))
                ahead = 2.0 * center - other[field, x, inner, :] + courant * lap
                other[field, x, pl.ds(TILE, TILE), :] = ahead[:TILE] + drops[step, field, x]
                other[field, x, pl.ds(2 * TILE, rows - TILE), :] = ahead[TILE:]
            if imaged:
                term = pair[1][0] * pair[0][1]
                if step == 0:
                    grad[x - deep] = term
                else:
                    grad[x - deep] = grad[x - deep] + term

    now, other = one, two
    for step in range(steps):
        margin = REACH * (step + 1)
        half = (deep - margin) // group

        def outside(i, carry):
            advance(now, other, step, margin + i * group + jnp.where(i >= half, cells, 0), False)
            return carry

        def inside(i, carry):
            advance(now, other, step, deep + i * group, True)
            return carry

        if half:
            lax.fori_loop(0, 2 * half, outside, 0)
        lax.fori_loop(0, cells // group, inside, 0)
        now, other = other, now

    out = []
    for field, final in ((0, final_w), (1, final_j)):
        out.append(pltpu.make_async_copy(now.at[field, pl.ds(deep, cells), inner], final.at[0], sems.at[field]))
        out[-1].start()

    def place(x, carry):
        for tile in range(tiles):
            speed = model[tile, deep + x]
            piece = grad[x, pl.ds(tile * TILE, TILE), :]
            parts[start_block + tile, x] = (2.0 * time_step * time_step / SCALE) * speed * piece
        return carry

    lax.fori_loop(0, cells, place, 0)
    for copy in out:
        copy.wait()


def run_steps(steps, start, count, fields, from_a, from_b, speeds, speed_a, speed_b, drops, groups):
    now = fields[0]
    cells, rows, depth = now.shape[1:]
    deep = steps * REACH
    wide = cells + 2 * deep
    tiles = rows // TILE
    copies = 12 + 3 * tiles
    final = jax.ShapeDtypeStruct(now.shape, jnp.float32)
    away = np.abs(np.subtract.outer(np.arange(depth), np.arange(depth)))
    band = np.zeros((depth, depth), np.float32)
    for k in range(1, REACH + 1):
        band[away == k] = scaled_weights[k]
    band = jnp.asarray(np.concatenate([band, band], axis=0), jnp.bfloat16)

    def kernel(*refs):
        steps_kernel(steps, *refs)

    field_buffer = pltpu.VMEM((2, wide, rows + 2 * TILE, depth), jnp.float32)
    hbm = pl.BlockSpec(memory_space=pltpu.HBM)
    vmem = pl.BlockSpec(memory_space=pltpu.VMEM)
    return pl.pallas_call(
        kernel,
        out_shape=(final, final, jax.ShapeDtypeStruct((groups, cells, TILE, depth), jnp.float32)),
        in_specs=[pl.BlockSpec(memory_space=pltpu.SMEM)] * 2 + [hbm] * 4 + [any_space()] * 5 + [vmem, vmem],
        out_specs=(any_space(), any_space(), vmem),
        scratch_shapes=[
            field_buffer,
            field_buffer,
            pltpu.VMEM((tiles, wide, TILE, depth), jnp.float32),
            pltpu.VMEM((cells, rows, depth), jnp.float32),
            pltpu.SemaphoreType.DMA((copies,)),
        ],
        compiler_params=pltpu.CompilerParams(vmem_limit_bytes=24 << 20),
        cost_estimate=pl.CostEstimate(flops=40 << 20, bytes_accessed=6 << 20, transcendentals=0),
    )(start, count, *map(in_hbm, fields), from_a, from_b, in_hbm(speeds), speed_a, speed_b, drops, band)


def per_device(
    velocity,
    aperture_start,
    aperture_count,
    wave_prev,
    wave_now,
    adjoint_prev,
    adjoint_now,
    source_cells,
    wavelet,
    receiver_cells,
    trace,
):
    steps = wavelet.shape[1]
    deep = steps * REACH
    tiles = wave_now.shape[2] // TILE

    to_a, to_b = pack(wave_now, adjoint_now, wave_prev, adjoint_prev, deep)
    from_a = swap_pairs(to_a, "slab", 0)
    from_b = swap_pairs(to_b, "slab", 1)
    speeds = lax.all_gather(velocity, "shot")

    cells_w, cells_j = (jnp.transpose(places, (2, 0, 1)) for places in (source_cells, receiver_cells))
    to_a, to_b, drops = cut_window(aperture_start, cells_w, cells_j, wavelet, trace, speeds, tiles)
    speed_a = swap_pairs(to_a, "slab", 0)
    speed_b = swap_pairs(to_b, "slab", 1)
    fields = (wave_now, adjoint_now, wave_prev, adjoint_prev)
    groups = lax.axis_size("shot")
    final_w, final_j, parts = run_steps(
        steps, aperture_start, aperture_count, fields, from_a, from_b, speeds, speed_a, speed_b, drops, groups
    )
    shares = lax.all_to_all(parts, "shot", 0, 0, tiled=True)
    return final_w, final_j, jnp.sum(shares, axis=0)


def solution(mesh):
    return jax.shard_map(
        per_device,
        mesh=mesh,
        in_specs=(
            P("slab", "shot", None),
            P("shot"),
            P("shot"),
            P("shot", "slab", None, None),
            P("shot", "slab", None, None),
            P("shot", "slab", None, None),
            P("shot", "slab", None, None),
            P("shot", None, None),
            P("shot", None, None),
            P("shot", None, None),
            P("shot", None, None),
        ),
        out_specs=(
            P("shot", "slab", None, None),
            P("shot", "slab", None, None),
            P("slab", "shot", None),
        ),
        check_vma=False,
    )
```

```python
import jax
import jax.numpy as jnp
import numpy as np
from jax import lax
from jax.experimental import pallas as pl
from jax.experimental.pallas import tpu as pltpu
from jax.sharding import PartitionSpec as P


SCALE = 5040.0
scaled_weights = (-14350.0, 8064.0, -1008.0, 128.0, -9.0)
time_step = 0.09
REACH = 4
TILE = 8


def swap_pairs(block, axis, first):
    count = lax.axis_size(axis)
    route = []
    for i in range(first, count - 1, 2):
        route += [(i, i + 1), (i + 1, i)]
    return lax.ppermute(block, axis, route)


def any_space():
    return pl.BlockSpec(memory_space=pl.ANY)


def in_hbm(array):
    return pltpu.with_memory_space_constraint(array, pltpu.HBM)


def packing_kernel(now_w, now_j, prev_w, prev_j, to_a, to_b, sems):
    cells = now_w.shape[1]
    deep_now = (to_a.shape[0] // 2 + REACH) // 2
    deep_prev = deep_now - REACH
    odd = lax.axis_index("slab") % 2
    copies = []
    for out, side in ((to_a, 1 - odd), (to_b, odd)):
        at = 0
        for field, deep in ((now_w, deep_now), (now_j, deep_now), (prev_w, deep_prev), (prev_j, deep_prev)):
            source = field.at[0, pl.ds(side * (cells - deep), deep)]
            copies.append(pltpu.make_async_copy(source, out.at[pl.ds(at, deep)], sems.at[len(copies)]))
            at += deep
    for copy in copies:
        copy.start()
    for copy in copies:
        copy.wait()


def pack(now_w, now_j, prev_w, prev_j, deep):
    rows, depth = now_w.shape[2:]
    out = pltpu.VMEM((4 * deep - 2 * REACH, rows, depth), jnp.float32)
    return pl.pallas_call(
        packing_kernel,
        out_shape=(out, out),
        in_specs=[pl.BlockSpec(memory_space=pltpu.HBM)] * 4,
        out_specs=(any_space(), any_space()),
        scratch_shapes=[pltpu.SemaphoreType.DMA((8,))],
        compiler_params=pltpu.CompilerParams(vmem_limit_bytes=1 << 20),
        cost_estimate=pl.CostEstimate(flops=0, bytes_accessed=4 << 20, transcendentals=0),
    )(*map(in_hbm, (now_w, now_j, prev_w, prev_j)))


def window_kernel(start, cells_w, cells_j, amps_w, amps_j, speeds, to_a, to_b, drops, sems):
    cells = speeds.shape[1]
    tiles, deep_prev = to_a.shape[:2]
    wide, depth = drops.shape[2], drops.shape[4]
    deep = deep_prev + REACH
    slab = lax.axis_index("slab")
    odd = slab % 2
    steps = amps_w.shape[1]
    start_block = start[0]
    copies = []
    for out, side in ((to_a, 1 - odd), (to_b, odd)):
        for tile in range(tiles):
            source = speeds.at[start_block + tile, pl.ds(side * (cells - deep_prev), deep_prev)]
            copies.append(pltpu.make_async_copy(source, out.at[tile], sems.at[len(copies)]))
    for copy in copies:
        copy.start()

    def clear(x, carry):
        for step in range(steps):
            for field in range(2):
                drops[step, field, x] = jnp.zeros((TILE, depth), jnp.float32)
        return carry

    lax.fori_loop(0, wide, clear, 0)
    row = lax.broadcasted_iota(jnp.int32, (TILE, depth), 0)
    col = lax.broadcasted_iota(jnp.int32, (TILE, depth), 1)

    def inject(field, places, amps):
        def one_cell(s, carry):
            x = places[0, 0, s] - (slab * cells - deep)

            @pl.when((x >= 0) & (x < wide))
            def _():
                here = (row == places[1, 0, s]) & (col == places[2, 0, s])
                for step in range(steps):
                    drops[step, field, x] = drops[step, field, x] + jnp.where(here, amps[0, step, s], 0.0)

            return carry

        lax.fori_loop(0, places.shape[2], one_cell, 0)

    inject(0, cells_w, amps_w)
    inject(1, cells_j, amps_j)
    for copy in copies:
        copy.wait()


def cut_window(start, cells_w, cells_j, amps_w, amps_j, speeds, tiles):
    cells, depth = speeds.shape[1], speeds.shape[3]
    steps = amps_w.shape[1]
    deep = steps * REACH
    out = pltpu.VMEM((tiles, deep - REACH, TILE, depth), jnp.float32)
    smem = pl.BlockSpec(memory_space=pltpu.SMEM)
    return pl.pallas_call(
        window_kernel,
        out_shape=(out, out, pltpu.VMEM((steps, 2, cells + 2 * deep, TILE, depth), jnp.float32)),
        in_specs=[smem] * 5 + [any_space()],
        out_specs=(any_space(), any_space(), pl.BlockSpec(memory_space=pltpu.VMEM)),
        scratch_shapes=[pltpu.SemaphoreType.DMA((2 * tiles,))],
        compiler_params=pltpu.CompilerParams(vmem_limit_bytes=8 << 20),
        cost_estimate=pl.CostEstimate(flops=1 << 20, bytes_accessed=2 << 20, transcendentals=0),
    )(start, cells_w, cells_j, amps_w, amps_j, in_hbm(speeds))


def along_z(now, band, x):
    rows, depth = now.shape[2] - 2 * TILE, now.shape[3]
    inner = pl.ds(TILE, rows)
    fields = [now[field, pl.ds(x, REACH), inner, :].reshape(REACH * rows, depth) for field in range(2)]
    cells = jnp.concatenate(fields, axis=0)
    high = cells.astype(jnp.bfloat16)
    low = (cells - high.astype(jnp.float32)).astype(jnp.bfloat16)
    return jnp.dot(jnp.concatenate([high, low], axis=1), band[...], preferred_element_type=jnp.float32)


def laplacian(now, spread, field, i, x):
    rows = now.shape[2] - 2 * TILE
    inner = pl.ds(TILE, rows)
    center = now[field, x, inner, :]
    lap = (3.0 * scaled_weights[0]) * center
    for k in range(1, REACH + 1):
        near = now[field, x + k, inner, :] + now[field, x - k, inner, :]
        near = near + now[field, x, pl.ds(TILE + k, rows), :]
        near = near + now[field, x, pl.ds(TILE - k, rows), :]
        lap = lap + scaled_weights[k] * near
    at = (field * REACH + i) * rows
    return center, lap + spread[at : at + rows]


def store_layer(buffer, field, x, values, drop):
    rows = values.shape[0]
    buffer[field, x, pl.ds(TILE, TILE), :] = values[:TILE] + drop
    buffer[field, x, pl.ds(2 * TILE, rows - TILE), :] = values[TILE:]


def advance(now, other, courant, drops, band, step, x_first, grad, fresh, deep):
    rows = now.shape[2] - 2 * TILE
    inner = pl.ds(TILE, rows)
    spread = along_z(now, band, x_first)
    for i in range(REACH):
        x = x_first + i
        pair = []
        for field in range(2):
            center, lap = laplacian(now, spread, field, i, x)
            pair.append((center, lap))
            ahead = 2.0 * center - other[field, x, inner, :] + courant[x] * lap
            store_layer(other, field, x, ahead, drops[step, field, x])
        if grad is not None:
            term = pair[1][0] * pair[0][1]
            grad[x - deep] = term if fresh else grad[x - deep] + term


def early_kernel(
    steps,
    start,
    count,
    now_w,
    now_j,
    prev_w,
    prev_j,
    from_a,
    from_b,
    speeds,
    drops,
    band,
    one,
    two,
    courant,
    image,
    grad,
    waiting,
    model,
    sems,
):
    cells, rows, depth = now_w.shape[1:]
    deep = steps * REACH
    deep_prev = deep - REACH
    wide = cells + 2 * deep
    tiles = rows // TILE
    odd = lax.axis_index("slab") % 2
    start_block = start[0]
    live = count[0]

    left_of_a = odd
    copies = []

    def bring(source, target):
        copy = pltpu.make_async_copy(source, target, sems.at[len(copies)])
        copy.start()
        copies.append(copy)

    inner = pl.ds(TILE, rows)
    for field, (now, prev) in enumerate(((now_w, prev_w), (now_j, prev_j))):
        bring(now.at[0], one.at[field, pl.ds(deep, cells), inner])
        bring(prev.at[0], two.at[field, pl.ds(deep, cells), inner])
        for buffer, on_left in ((from_a, left_of_a), (from_b, 1 - left_of_a)):
            at = (1 - on_left) * (deep + cells)
            bring(buffer.at[pl.ds(field * deep, deep)], one.at[field, pl.ds(at, deep), inner])
            at = on_left * REACH + (1 - on_left) * (deep + cells)
            bring(
                buffer.at[pl.ds(2 * deep + field * deep_prev, deep_prev)],
                two.at[field, pl.ds(at, deep_prev), inner],
            )
    for tile in range(tiles):
        bring(speeds.at[start_block + tile], model.at[tile])

    zero_tile = jnp.zeros((TILE, depth), jnp.float32)

    def clear_edges(x, carry):
        for buffer in (one, two):
            for field in range(2):
                buffer[field, x, pl.ds(0, TILE), :] = zero_tile
                buffer[field, x, pl.ds(TILE + rows, TILE), :] = zero_tile
        return carry

    lax.fori_loop(0, wide, clear_edges, 0)
    for copy in copies:
        copy.wait()

    def factors(x, carry):
        for tile in range(tiles):
            alive = jnp.where(tile < live, time_step * time_step / SCALE, 0.0)
            speed = model[tile, x]
            at = pl.ds(tile * TILE, TILE)
            courant[deep + x, at, :] = alive * (speed * speed)
            image[x, at, :] = (2.0 * time_step * time_step / SCALE) * speed
        return carry

    lax.fori_loop(0, cells, factors, 0)

    for tile in range(1, tiles):

        @pl.when(tile >= live)
        def _():
            def clear(x, carry):
                for buffer in (one, two):
                    for field in range(2):
                        buffer[field, x, pl.ds(TILE + tile * TILE, TILE), :] = zero_tile
                return carry

            lax.fori_loop(0, wide, clear, 0)

    half = deep_prev // REACH

    def outside(c, carry):
        x_first = REACH + c * REACH + jnp.where(c >= half, cells, 0)
        spread = along_z(one, band, x_first)
        for i in range(REACH):
            x = x_first + i
            for field in range(2):
                center, lap = laplacian(one, spread, field, i, x)
                waiting[field, c * REACH + i] = lap
                store_layer(two, field, x, 2.0 * center - two[field, x, inner, :], drops[0, field, x])
        return carry

    def inside(c, carry):
        advance(one, two, courant, drops, band, 0, deep + c * REACH, grad, True, deep)
        return carry

    def core(c, carry):
        advance(two, one, courant, drops, band, 1, deep + REACH + c * REACH, grad, False, deep)
        return carry

    lax.fori_loop(0, cells // REACH, inside, 0)
    lax.fori_loop(0, cells // REACH - 2, core, 0)
    lax.fori_loop(0, 2 * half, outside, 0)


def late_kernel(
    steps,
    start,
    count,
    speed_a,
    speed_b,
    drops,
    band,
    image,
    waiting,
    one_in,
    two_in,
    courant_in,
    grad_in,
    final_w,
    final_j,
    parts,
    one,
    two,
    courant,
    grad,
    sems,
):
    cells, rows, depth = image.shape
    deep = steps * REACH
    deep_prev = deep - REACH
    tiles = rows // TILE
    odd = lax.axis_index("slab") % 2
    start_block = start[0]
    live = count[0]
    inner = pl.ds(TILE, rows)

    def finish(h, carry):
        right = h >= deep_prev
        layer = jnp.where(right, h - deep_prev, h)
        x = jnp.where(right, deep + cells, REACH) + layer
        use_a = jnp.where(right, 1 - odd, odd) == 1
        for tile in range(tiles):
            alive = jnp.where(tile < live, time_step * time_step / SCALE, 0.0)
            speed = jnp.where(use_a, speed_a[tile, layer], speed_b[tile, layer])
            factor = alive * (speed * speed)
            courant[x, pl.ds(tile * TILE, TILE), :] = factor
            for field in range(2):
                at = pl.ds(TILE + tile * TILE, TILE)
                change = factor * waiting[field, h, pl.ds(tile * TILE, TILE), :]
                two[field, x, at, :] = two[field, x, at, :] + change
        return carry

    lax.fori_loop(0, 2 * deep_prev, finish, 0)

    now, other = two, one
    for step in range(1, steps):
        margin = REACH * (step + 1)
        half = (deep - margin) // REACH

        def outside(c, carry):
            x = margin + c * REACH + jnp.where(c >= half, cells, 0)
            advance(now, other, courant, drops, band, step, x, None, False, deep)
            return carry

        stride = cells - REACH if step == 1 else REACH

        def inside(c, carry):
            advance(now, other, courant, drops, band, step, deep + c * stride, grad, False, deep)
            return carry

        if half:
            lax.fori_loop(0, 2 * half, outside, 0)
        lax.fori_loop(0, 2 if step == 1 else cells // REACH, inside, 0)
        now, other = other, now

    out = []
    for field, final in ((0, final_w), (1, final_j)):
        out.append(pltpu.make_async_copy(now.at[field, pl.ds(deep, cells), inner], final.at[0], sems.at[field]))
        out[-1].start()

    def clear_parts(b, carry):
        parts[b] = jnp.zeros(parts.shape[1:], jnp.float32)
        return carry

    lax.fori_loop(0, parts.shape[0], clear_parts, 0)

    def place(x, carry):
        for tile in range(tiles):
            at = pl.ds(tile * TILE, TILE)
            parts[start_block + tile, x] = image[x, at, :] * grad[x, at, :]
        return carry

    lax.fori_loop(0, cells, place, 0)
    for copy in out:
        copy.wait()


def run_steps(steps, start, count, fields, from_a, from_b, speeds, speed_a, speed_b, drops, groups):
    now = fields[0]
    cells, rows, depth = now.shape[1:]
    deep = steps * REACH
    deep_prev = deep - REACH
    wide = cells + 2 * deep
    tiles = rows // TILE
    copies = 12 + tiles
    away = np.abs(np.subtract.outer(np.arange(depth), np.arange(depth)))
    band = np.zeros((depth, depth), np.float32)
    for k in range(1, REACH + 1):
        band[away == k] = scaled_weights[k]
    band = jnp.asarray(np.concatenate([band, band], axis=0), jnp.bfloat16)

    smem = pl.BlockSpec(memory_space=pltpu.SMEM)
    hbm = pl.BlockSpec(memory_space=pltpu.HBM)
    vmem = pl.BlockSpec(memory_space=pltpu.VMEM)
    buffer = pltpu.VMEM((2, wide, rows + 2 * TILE, depth), jnp.float32)
    factors = pltpu.VMEM((wide, rows, depth), jnp.float32)
    layers = pltpu.VMEM((cells, rows, depth), jnp.float32)
    waiting = pltpu.VMEM((2, 2 * deep_prev, rows, depth), jnp.float32)

    def early(*refs):
        early_kernel(steps, *refs)

    def late(*refs):
        late_kernel(steps, *refs)

    one, two, courant, image, grad, waiting = pl.pallas_call(
        early,
        out_shape=(buffer, buffer, factors, layers, layers, waiting),
        in_specs=[smem] * 2 + [hbm] * 4 + [any_space()] * 3 + [vmem, vmem],
        out_specs=(vmem,) * 6,
        scratch_shapes=[
            pltpu.VMEM((tiles, cells, TILE, depth), jnp.float32),
            pltpu.SemaphoreType.DMA((copies,)),
        ],
        compiler_params=pltpu.CompilerParams(vmem_limit_bytes=8 << 20),
        cost_estimate=pl.CostEstimate(flops=40 << 20, bytes_accessed=6 << 20, transcendentals=0),
    )(start, count, *map(in_hbm, fields), from_a, from_b, in_hbm(speeds), drops, band)
    final = jax.ShapeDtypeStruct(now.shape, jnp.float32)
    parts = pltpu.VMEM((groups, cells, TILE, depth), jnp.float32)
    results = pl.pallas_call(
        late,
        out_shape=(final, final, parts, buffer, buffer, factors, layers),
        in_specs=[smem] * 2 + [vmem] * 10,
        out_specs=(any_space(), any_space()) + (vmem,) * 5,
        input_output_aliases={8: 3, 9: 4, 10: 5, 11: 6},
        scratch_shapes=[pltpu.SemaphoreType.DMA((2,))],
        compiler_params=pltpu.CompilerParams(vmem_limit_bytes=8 << 20),
        cost_estimate=pl.CostEstimate(flops=40 << 20, bytes_accessed=6 << 20, transcendentals=0),
    )(start, count, speed_a, speed_b, drops, band, image, waiting, one, two, courant, grad)
    return results[:3]


def per_device(
    velocity,
    aperture_start,
    aperture_count,
    wave_prev,
    wave_now,
    adjoint_prev,
    adjoint_now,
    source_cells,
    wavelet,
    receiver_cells,
    trace,
):
    steps = wavelet.shape[1]
    deep = steps * REACH
    tiles = wave_now.shape[2] // TILE

    to_a, to_b = pack(wave_now, adjoint_now, wave_prev, adjoint_prev, deep)
    from_b = swap_pairs(to_b, "slab", 1)
    from_a = swap_pairs(to_a, "slab", 0)
    speeds = lax.all_gather(velocity, "shot")

    cells_w, cells_j = (jnp.transpose(places, (2, 0, 1)) for places in (source_cells, receiver_cells))
    to_a, to_b, drops = cut_window(aperture_start, cells_w, cells_j, wavelet, trace, speeds, tiles)
    speed_b = swap_pairs(to_b, "slab", 1)
    speed_a = swap_pairs(to_a, "slab", 0)
    fields = (wave_now, adjoint_now, wave_prev, adjoint_prev)
    groups = lax.axis_size("shot")
    final_w, final_j, parts = run_steps(
        steps, aperture_start, aperture_count, fields, from_a, from_b, speeds, speed_a, speed_b, drops, groups
    )
    shares = lax.all_to_all(parts, "shot", 0, 0, tiled=True)
    return final_w, final_j, jnp.sum(shares, axis=0)


def solution(mesh):
    return jax.shard_map(
        per_device,
        mesh=mesh,
        in_specs=(
            P("slab", "shot", None),
            P("shot"),
            P("shot"),
            P("shot", "slab", None, None),
            P("shot", "slab", None, None),
            P("shot", "slab", None, None),
            P("shot", "slab", None, None),
            P("shot", None, None),
            P("shot", None, None),
            P("shot", None, None),
            P("shot", None, None),
        ),
        out_specs=(
            P("shot", "slab", None, None),
            P("shot", "slab", None, None),
            P("slab", "shot", None),
        ),
        check_vma=False,
    )
```

```python
import jax
import jax.numpy as jnp
from jax import lax
from jax.experimental import pallas as pl
from jax.experimental.pallas import tpu as pltpu
from jax.sharding import PartitionSpec as P


SCALE = 5040.0
scaled_weights = (-14350.0, 8064.0, -1008.0, 128.0, -9.0)
time_step = 0.09
REACH = 4
TILE = 8


def swap_pairs(block, axis, first):
    count = lax.axis_size(axis)
    route = []
    for i in range(first, count - 1, 2):
        route += [(i, i + 1), (i + 1, i)]
    return lax.ppermute(block, axis, route)


def any_space():
    return pl.BlockSpec(memory_space=pl.ANY)


def in_hbm(array):
    return pltpu.with_memory_space_constraint(array, pltpu.HBM)


def packing_kernel(now_w, now_j, prev_w, prev_j, to_a, to_b, sems):
    cells = now_w.shape[1]
    deep_now = (to_a.shape[0] // 2 + REACH) // 2
    deep_prev = deep_now - REACH
    odd = lax.axis_index("slab") % 2
    copies, bring = bringing(sems)
    for out, side in ((to_a, 1 - odd), (to_b, odd)):
        at = 0
        for field, deep in ((now_w, deep_now), (now_j, deep_now), (prev_w, deep_prev), (prev_j, deep_prev)):
            bring(field.at[0, pl.ds(side * (cells - deep), deep)], out.at[pl.ds(at, deep)])
            at += deep
    for copy in copies:
        copy.wait()


def pack(fields, deep):
    rows, depth = fields[0].shape[2:]
    out = pltpu.VMEM((4 * deep - 2 * REACH, rows, depth), jnp.float32)
    return pl.pallas_call(
        packing_kernel,
        out_shape=(out, out),
        in_specs=[pl.BlockSpec(memory_space=pltpu.HBM)] * 4,
        out_specs=(any_space(), any_space()),
        scratch_shapes=[pltpu.SemaphoreType.DMA((8,))],
        compiler_params=pltpu.CompilerParams(vmem_limit_bytes=1 << 20),
        cost_estimate=pl.CostEstimate(flops=0, bytes_accessed=4 << 20, transcendentals=0),
    )(*map(in_hbm, fields))


def bringing(sems):
    copies = []

    def bring(source, target):
        copy = pltpu.make_async_copy(source, target, sems.at[len(copies)])
        copy.start()
        copies.append(copy)

    return copies, bring


def opening_kernel(
    start,
    count,
    cells_w_in,
    cells_j_in,
    amps_w_in,
    amps_j_in,
    now_w,
    now_j,
    prev_w,
    prev_j,
    speeds,
    to_a,
    to_b,
    drops,
    band,
    one,
    two,
    courant,
    image,
    grad,
    cells_w,
    cells_j,
    amps_w,
    amps_j,
    model,
    sems,
):
    cells, rows, depth = image.shape
    tiles, deep_prev = to_a.shape[:2]
    wide = drops.shape[2]
    steps = drops.shape[0]
    deep = deep_prev + REACH
    slab = lax.axis_index("slab")
    odd = slab % 2
    start_block = start[0]
    live = count[0]
    copies, bring = bringing(sems)
    for out, side in ((to_a, 1 - odd), (to_b, odd)):
        for tile in range(tiles):
            bring(speeds.at[start_block + tile, pl.ds(side * (cells - deep_prev), deep_prev)], out.at[tile])
    for source, target in ((cells_w_in, cells_w), (cells_j_in, cells_j), (amps_w_in, amps_w), (amps_j_in, amps_j)):
        bring(source, target)
    for tile in range(tiles):
        bring(speeds.at[start_block + tile], model.at[tile])
    inner = pl.ds(TILE, rows)
    for field, (now, prev) in enumerate(((now_w, prev_w), (now_j, prev_j))):
        bring(now.at[0], one.at[field, pl.ds(deep, cells), inner])
        bring(prev.at[0], two.at[field, pl.ds(deep, cells), inner])

    zero_tile = jnp.zeros((TILE, depth), jnp.float32)

    def clear(x, carry):
        for step in range(steps):
            for field in range(2):
                drops[step, field, x] = zero_tile
        for buffer in (one, two):
            for field in range(2):
                buffer[field, x, pl.ds(0, TILE), :] = zero_tile
                buffer[field, x, pl.ds(TILE + rows, TILE), :] = zero_tile
        return carry

    lax.fori_loop(0, wide, clear, 0)
    away = lax.broadcasted_iota(jnp.int32, (depth, depth), 0) - lax.broadcasted_iota(jnp.int32, (depth, depth), 1)
    matrix = jnp.zeros((depth, depth), jnp.float32)
    for k in range(1, REACH + 1):
        matrix = jnp.where((away == k) | (away == -k), scaled_weights[k], matrix)
    band[pl.ds(0, depth), :] = matrix.astype(jnp.bfloat16)
    band[pl.ds(depth, depth), :] = matrix.astype(jnp.bfloat16)
    for copy in copies:
        copy.wait()

    row = lax.broadcasted_iota(jnp.int32, (TILE, depth), 0)
    col = lax.broadcasted_iota(jnp.int32, (TILE, depth), 1)

    def inject(field, places, amps):
        def one_cell(s, carry):
            x = places[0, 0, s] - (slab * cells - deep)

            @pl.when((x >= 0) & (x < wide))
            def _():
                here = (row == places[1, 0, s]) & (col == places[2, 0, s])
                for step in range(steps):
                    drops[step, field, x] = drops[step, field, x] + jnp.where(here, amps[0, step, s], 0.0)

            return carry

        lax.fori_loop(0, places.shape[2], one_cell, 0)

    inject(0, cells_w, amps_w)
    inject(1, cells_j, amps_j)

    def factors(x, carry):
        for tile in range(tiles):
            alive = jnp.where(tile < live, time_step * time_step / SCALE, 0.0)
            speed = model[tile, x]
            at = pl.ds(tile * TILE, TILE)
            courant[deep + x, at, :] = alive * (speed * speed)
            image[x, at, :] = (2.0 * time_step * time_step / SCALE) * speed
        return carry

    lax.fori_loop(0, cells, factors, 0)
    clear_dead(one, two, live, deep, deep + cells)

    def core(c, carry):
        advance(one, two, courant, drops, band, 0, deep + REACH + c * REACH, grad, True, deep)
        return carry

    lax.fori_loop(0, cells // REACH - 2, core, 0, unroll=2)


def clear_dead(one, two, live, first, last):
    tiles = one.shape[2] // TILE - 2
    for tile in range(1, tiles):

        @pl.when(tile >= live)
        def _():
            def clear(x, carry):
                for buffer in (one, two):
                    for field in range(2):
                        buffer[field, x, pl.ds(TILE + tile * TILE, TILE), :] = jnp.zeros(
                            (TILE, one.shape[3]), jnp.float32
                        )
                return carry

            lax.fori_loop(first, last, clear, 0)


def opening(start, count, small, fields, speeds, steps):
    groups, cells, _, depth = speeds.shape
    rows = fields[0].shape[2]
    tiles = rows // TILE
    deep = steps * REACH
    wide = cells + 2 * deep
    halo = pltpu.VMEM((tiles, deep - REACH, TILE, depth), jnp.float32)
    drops = pltpu.VMEM((steps, 2, wide, TILE, depth), jnp.float32)
    band = pltpu.VMEM((2 * depth, depth), jnp.bfloat16)
    buffer = pltpu.VMEM((2, wide, rows + 2 * TILE, depth), jnp.float32)
    courant = pltpu.VMEM((wide, rows, depth), jnp.float32)
    layers = pltpu.VMEM((cells, rows, depth), jnp.float32)
    vmem = pl.BlockSpec(memory_space=pltpu.VMEM)
    return pl.pallas_call(
        opening_kernel,
        out_shape=(halo, halo, drops, band, buffer, buffer, courant, layers, layers),
        in_specs=[pl.BlockSpec(memory_space=pltpu.SMEM)] * 2 + [pl.BlockSpec(memory_space=pltpu.HBM)] * 9,
        out_specs=(vmem,) * 9,
        scratch_shapes=[pltpu.SMEM(array.shape, array.dtype) for array in small]
        + [
            pltpu.VMEM((tiles, cells, TILE, depth), jnp.float32),
            pltpu.SemaphoreType.DMA((3 * tiles + 8,)),
        ],
        compiler_params=pltpu.CompilerParams(vmem_limit_bytes=8 << 20),
        cost_estimate=pl.CostEstimate(flops=4 << 20, bytes_accessed=4 << 20, transcendentals=0),
    )(start, count, *map(in_hbm, small), *map(in_hbm, fields), in_hbm(speeds))


def along_z(now, band, x):
    rows, depth = now.shape[2] - 2 * TILE, now.shape[3]
    inner = pl.ds(TILE, rows)
    fields = [now[field, pl.ds(x, REACH), inner, :].reshape(REACH * rows, depth) for field in range(2)]
    cells = jnp.concatenate(fields, axis=0)
    high = cells.astype(jnp.bfloat16)
    low = (cells - high.astype(jnp.float32)).astype(jnp.bfloat16)
    return jnp.dot(jnp.concatenate([high, low], axis=1), band[...], preferred_element_type=jnp.float32)


def laplacian(now, spread, field, i, x):
    rows = now.shape[2] - 2 * TILE
    inner = pl.ds(TILE, rows)
    center = now[field, x, inner, :]
    lap = (3.0 * scaled_weights[0]) * center
    for k in range(1, REACH + 1):
        near = now[field, x + k, inner, :] + now[field, x - k, inner, :]
        near = near + now[field, x, pl.ds(TILE + k, rows), :]
        near = near + now[field, x, pl.ds(TILE - k, rows), :]
        lap = lap + scaled_weights[k] * near
    at = (field * REACH + i) * rows
    return center, lap + spread[at : at + rows]


def store_layer(buffer, field, x, values, drop):
    rows = values.shape[0]
    buffer[field, x, pl.ds(TILE, TILE), :] = values[:TILE] + drop
    buffer[field, x, pl.ds(2 * TILE, rows - TILE), :] = values[TILE:]


def advance(now, other, courant, drops, band, step, x_first, grad, fresh, deep):
    rows = now.shape[2] - 2 * TILE
    inner = pl.ds(TILE, rows)
    spread = along_z(now, band, x_first)
    for i in range(REACH):
        x = x_first + i
        pair = []
        for field in range(2):
            center, lap = laplacian(now, spread, field, i, x)
            pair.append((center, lap))
            ahead = 2.0 * center - other[field, x, inner, :] + courant[x] * lap
            store_layer(other, field, x, ahead, drops[step, field, x])
        if grad is not None:
            term = pair[1][0] * pair[0][1]
            grad[x - deep] = term if fresh else grad[x - deep] + term


def early_kernel(steps, count, from_a, from_b, courant, drops, band, one_in, two_in, grad_in, one, two, grad, waiting, sems):
    cells, rows, depth = grad.shape
    deep = steps * REACH
    deep_prev = deep - REACH
    wide = cells + 2 * deep
    odd = lax.axis_index("slab") % 2

    left_of_a = odd
    copies, bring = bringing(sems)
    inner = pl.ds(TILE, rows)
    for field in range(2):
        for buffer, on_left in ((from_a, left_of_a), (from_b, 1 - left_of_a)):
            at = (1 - on_left) * (deep + cells)
            bring(buffer.at[pl.ds(field * deep, deep)], one.at[field, pl.ds(at, deep), inner])
            at = on_left * REACH + (1 - on_left) * (deep + cells)
            bring(
                buffer.at[pl.ds(2 * deep + field * deep_prev, deep_prev)],
                two.at[field, pl.ds(at, deep_prev), inner],
            )
    for copy in copies:
        copy.wait()
    clear_dead(one, two, count[0], 0, deep)
    clear_dead(one, two, count[0], deep + cells, wide)

    half = deep_prev // REACH

    def outside(c, carry):
        x_first = REACH + c * REACH + jnp.where(c >= half, cells, 0)
        spread = along_z(one, band, x_first)
        for i in range(REACH):
            x = x_first + i
            for field in range(2):
                center, lap = laplacian(one, spread, field, i, x)
                waiting[field, c * REACH + i] = lap
                store_layer(two, field, x, 2.0 * center - two[field, x, inner, :], drops[0, field, x])
        return carry

    def inside(c, carry):
        advance(one, two, courant, drops, band, 0, deep + c * (cells - REACH), grad, True, deep)
        return carry

    def core(c, carry):
        advance(two, one, courant, drops, band, 1, deep + REACH + c * REACH, grad, False, deep)
        return carry

    lax.fori_loop(0, 2, inside, 0, unroll=2)
    lax.fori_loop(0, 2 * half, outside, 0, unroll=2)
    lax.fori_loop(0, cells // REACH - 2, core, 0, unroll=2)


def late_kernel(
    steps,
    start,
    count,
    speed_a,
    speed_b,
    drops,
    band,
    image,
    waiting,
    one_in,
    two_in,
    courant_in,
    grad_in,
    final_w,
    final_j,
    parts,
    one,
    two,
    courant,
    grad,
    sems,
):
    cells, rows, depth = image.shape
    deep = steps * REACH
    deep_prev = deep - REACH
    tiles = rows // TILE
    odd = lax.axis_index("slab") % 2
    start_block = start[0]
    live = count[0]
    inner = pl.ds(TILE, rows)

    def finish(h, carry):
        right = h >= deep_prev
        layer = jnp.where(right, h - deep_prev, h)
        x = jnp.where(right, deep + cells, REACH) + layer
        use_a = jnp.where(right, 1 - odd, odd) == 1
        for tile in range(tiles):
            alive = jnp.where(tile < live, time_step * time_step / SCALE, 0.0)
            speed = jnp.where(use_a, speed_a[tile, layer], speed_b[tile, layer])
            factor = alive * (speed * speed)
            courant[x, pl.ds(tile * TILE, TILE), :] = factor
            for field in range(2):
                at = pl.ds(TILE + tile * TILE, TILE)
                change = factor * waiting[field, h, pl.ds(tile * TILE, TILE), :]
                two[field, x, at, :] = two[field, x, at, :] + change
        return carry

    lax.fori_loop(0, 2 * deep_prev, finish, 0)

    now, other = two, one
    for step in range(1, steps):
        margin = REACH * (step + 1)
        half = (deep - margin) // REACH

        def outside(c, carry):
            x = margin + c * REACH + jnp.where(c >= half, cells, 0)
            advance(now, other, courant, drops, band, step, x, None, False, deep)
            return carry

        stride = cells - REACH if step == 1 else REACH

        def inside(c, carry):
            advance(now, other, courant, drops, band, step, deep + c * stride, grad, False, deep)
            return carry

        if half:
            lax.fori_loop(0, 2 * half, outside, 0, unroll=2)
        lax.fori_loop(0, 2 if step == 1 else cells // REACH, inside, 0, unroll=2)
        now, other = other, now

    out = []
    for field, final in ((0, final_w), (1, final_j)):
        out.append(pltpu.make_async_copy(now.at[field, pl.ds(deep, cells), inner], final.at[0], sems.at[field]))
        out[-1].start()

    def clear_parts(b, carry):
        parts[b] = jnp.zeros(parts.shape[1:], jnp.float32)
        return carry

    lax.fori_loop(0, parts.shape[0], clear_parts, 0)

    def place(x, carry):
        for tile in range(tiles):
            at = pl.ds(tile * TILE, TILE)
            parts[start_block + tile, x] = image[x, at, :] * grad[x, at, :]
        return carry

    lax.fori_loop(0, cells, place, 0)
    for copy in out:
        copy.wait()


def early_steps(steps, count, from_a, from_b, courant, drops, band, one, two, grad):
    rows, depth = grad.shape[1:]
    deep_prev = (steps - 1) * REACH
    smem = pl.BlockSpec(memory_space=pltpu.SMEM)
    vmem = pl.BlockSpec(memory_space=pltpu.VMEM)
    same = [pltpu.VMEM(array.shape, array.dtype) for array in (one, two, grad)]

    def kernel(*refs):
        early_kernel(steps, *refs)

    return pl.pallas_call(
        kernel,
        out_shape=(*same, pltpu.VMEM((2, 2 * deep_prev, rows, depth), jnp.float32)),
        in_specs=[smem, any_space(), any_space()] + [vmem] * 6,
        out_specs=(vmem,) * 4,
        input_output_aliases={6: 0, 7: 1, 8: 2},
        scratch_shapes=[pltpu.SemaphoreType.DMA((8,))],
        compiler_params=pltpu.CompilerParams(vmem_limit_bytes=8 << 20),
        cost_estimate=pl.CostEstimate(flops=20 << 20, bytes_accessed=4 << 20, transcendentals=0),
    )(count, from_a, from_b, courant, drops, band, one, two, grad)


def late_steps(steps, start, count, speed_a, speed_b, drops, band, image, waiting, one, two, courant, grad, groups):
    cells, rows, depth = image.shape
    smem = pl.BlockSpec(memory_space=pltpu.SMEM)
    vmem = pl.BlockSpec(memory_space=pltpu.VMEM)
    final = jax.ShapeDtypeStruct((1, cells, rows, depth), jnp.float32)
    parts = pltpu.VMEM((groups, cells, TILE, depth), jnp.float32)
    same = [pltpu.VMEM(array.shape, array.dtype) for array in (one, two, courant, grad)]

    def kernel(*refs):
        late_kernel(steps, *refs)

    return pl.pallas_call(
        kernel,
        out_shape=(final, final, parts, *same),
        in_specs=[smem] * 2 + [vmem] * 10,
        out_specs=(any_space(), any_space()) + (vmem,) * 5,
        input_output_aliases={8: 3, 9: 4, 10: 5, 11: 6},
        scratch_shapes=[pltpu.SemaphoreType.DMA((2,))],
        compiler_params=pltpu.CompilerParams(vmem_limit_bytes=8 << 20),
        cost_estimate=pl.CostEstimate(flops=40 << 20, bytes_accessed=6 << 20, transcendentals=0),
    )(start, count, speed_a, speed_b, drops, band, image, waiting, one, two, courant, grad)[:3]


def per_device(
    velocity,
    aperture_start,
    aperture_count,
    wave_prev,
    wave_now,
    adjoint_prev,
    adjoint_now,
    source_cells,
    wavelet,
    receiver_cells,
    trace,
):
    steps = wavelet.shape[1]
    deep = steps * REACH
    fields = (wave_now, adjoint_now, wave_prev, adjoint_prev)

    to_a, to_b = pack(fields, deep)
    from_a = swap_pairs(to_a, "slab", 0)
    from_b = swap_pairs(to_b, "slab", 1)
    speeds = lax.all_gather(velocity, "shot")

    cells_w, cells_j = (jnp.transpose(places, (2, 0, 1)) for places in (source_cells, receiver_cells))
    small = (cells_w, cells_j, wavelet, trace)
    to_a, to_b, drops, band, one, two, courant, image, grad = opening(
        aperture_start, aperture_count, small, fields, speeds, steps
    )
    speed_a = swap_pairs(to_a, "slab", 0)
    speed_b = swap_pairs(to_b, "slab", 1)
    one, two, grad, waiting = early_steps(
        steps, aperture_count, from_a, from_b, courant, drops, band, one, two, grad
    )
    final_w, final_j, parts = late_steps(
        steps,
        aperture_start,
        aperture_count,
        speed_a,
        speed_b,
        drops,
        band,
        image,
        waiting,
        one,
        two,
        courant,
        grad,
        lax.axis_size("shot"),
    )
    shares = lax.all_to_all(parts, "shot", 0, 0, tiled=True)
    return final_w, final_j, jnp.sum(shares, axis=0)


def solution(mesh):
    return jax.shard_map(
        per_device,
        mesh=mesh,
        in_specs=(
            P("slab", "shot", None),
            P("shot"),
            P("shot"),
            P("shot", "slab", None, None),
            P("shot", "slab", None, None),
            P("shot", "slab", None, None),
            P("shot", "slab", None, None),
            P("shot", None, None),
            P("shot", None, None),
            P("shot", None, None),
            P("shot", None, None),
        ),
        out_specs=(
            P("shot", "slab", None, None),
            P("shot", "slab", None, None),
            P("slab", "shot", None),
        ),
        check_vma=False,
    )
```

```python
import jax
import jax.numpy as jnp
from jax import lax
from jax.experimental import pallas as pl
from jax.experimental.pallas import tpu as pltpu
from jax.sharding import PartitionSpec as P


SCALE = 5040.0
scaled_weights = (-14350.0, 8064.0, -1008.0, 128.0, -9.0)
time_step = 0.09
REACH = 4
TILE = 8


def swap_pairs(block, axis, first):
    count = lax.axis_size(axis)
    route = []
    for i in range(first, count - 1, 2):
        route += [(i, i + 1), (i + 1, i)]
    return lax.ppermute(block, axis, route)


def any_space():
    return pl.BlockSpec(memory_space=pl.ANY)


def in_hbm(array):
    return pltpu.with_memory_space_constraint(array, pltpu.HBM)


def packing_kernel(now_w, now_j, prev_w, prev_j, to_a, to_b, sems):
    cells = now_w.shape[1]
    deep_now = (to_a.shape[0] // 2 + REACH) // 2
    deep_prev = deep_now - REACH
    odd = lax.axis_index("slab") % 2
    copies, bring = bringing(sems)
    for out, side in ((to_a, 1 - odd), (to_b, odd)):
        at = 0
        for field, deep in ((now_w, deep_now), (now_j, deep_now), (prev_w, deep_prev), (prev_j, deep_prev)):
            bring(field.at[0, pl.ds(side * (cells - deep), deep)], out.at[pl.ds(at, deep)])
            at += deep
    for copy in copies:
        copy.wait()


def pack(fields, deep):
    rows, depth = fields[0].shape[2:]
    out = pltpu.VMEM((4 * deep - 2 * REACH, rows, depth), jnp.float32)
    return pl.pallas_call(
        packing_kernel,
        out_shape=(out, out),
        in_specs=[pl.BlockSpec(memory_space=pltpu.HBM)] * 4,
        out_specs=(any_space(), any_space()),
        scratch_shapes=[pltpu.SemaphoreType.DMA((8,))],
        compiler_params=pltpu.CompilerParams(vmem_limit_bytes=1 << 20),
        cost_estimate=pl.CostEstimate(flops=0, bytes_accessed=4 << 20, transcendentals=0),
    )(*map(in_hbm, fields))


def bringing(sems):
    copies = []

    def bring(source, target):
        copy = pltpu.make_async_copy(source, target, sems.at[len(copies)])
        copy.start()
        copies.append(copy)

    return copies, bring


def opening_kernel(
    start,
    count,
    cells_w_in,
    cells_j_in,
    amps_w_in,
    amps_j_in,
    now_w,
    now_j,
    prev_w,
    prev_j,
    speeds,
    to_a,
    to_b,
    drops,
    band,
    one,
    two,
    courant,
    image,
    grad,
    cells_w,
    cells_j,
    amps_w,
    amps_j,
    model,
    sems,
):
    cells, rows, depth = image.shape
    tiles, deep_prev = to_a.shape[:2]
    wide = drops.shape[2]
    steps = drops.shape[0]
    deep = deep_prev + REACH
    slab = lax.axis_index("slab")
    odd = slab % 2
    start_block = start[0]
    live = count[0]
    copies, bring = bringing(sems)
    for out, side in ((to_a, 1 - odd), (to_b, odd)):
        for tile in range(tiles):
            bring(speeds.at[start_block + tile, pl.ds(side * (cells - deep_prev), deep_prev)], out.at[tile])
    for source, target in ((cells_w_in, cells_w), (cells_j_in, cells_j), (amps_w_in, amps_w), (amps_j_in, amps_j)):
        bring(source, target)
    for tile in range(tiles):
        bring(speeds.at[start_block + tile], model.at[tile])
    inner = pl.ds(TILE, rows)
    for field, (now, prev) in enumerate(((now_w, prev_w), (now_j, prev_j))):
        bring(now.at[0], one.at[field, pl.ds(deep, cells), inner])
        bring(prev.at[0], two.at[field, pl.ds(deep, cells), inner])

    zero_tile = jnp.zeros((TILE, depth), jnp.float32)

    def clear(x, carry):
        for step in range(steps):
            for field in range(2):
                drops[step, field, x] = zero_tile
        for buffer in (one, two):
            for field in range(2):
                buffer[field, x, pl.ds(0, TILE), :] = zero_tile
                buffer[field, x, pl.ds(TILE + rows, TILE), :] = zero_tile
        return carry

    lax.fori_loop(0, wide, clear, 0)
    away = lax.broadcasted_iota(jnp.int32, (depth, depth), 0) - lax.broadcasted_iota(jnp.int32, (depth, depth), 1)
    matrix = jnp.zeros((depth, depth), jnp.float32)
    for k in range(1, REACH + 1):
        matrix = jnp.where((away == k) | (away == -k), scaled_weights[k], matrix)
    band[pl.ds(0, depth), :] = matrix.astype(jnp.bfloat16)
    band[pl.ds(depth, depth), :] = matrix.astype(jnp.bfloat16)
    for copy in copies:
        copy.wait()

    row = lax.broadcasted_iota(jnp.int32, (TILE, depth), 0)
    col = lax.broadcasted_iota(jnp.int32, (TILE, depth), 1)

    def inject(field, places, amps):
        def one_cell(s, carry):
            x = places[0, 0, s] - (slab * cells - deep)

            @pl.when((x >= 0) & (x < wide))
            def _():
                here = (row == places[1, 0, s]) & (col == places[2, 0, s])
                for step in range(steps):
                    drops[step, field, x] = drops[step, field, x] + jnp.where(here, amps[0, step, s], 0.0)

            return carry

        lax.fori_loop(0, places.shape[2], one_cell, 0)

    inject(0, cells_w, amps_w)
    inject(1, cells_j, amps_j)

    def factors(x, carry):
        for tile in range(tiles):
            alive = jnp.where(tile < live, time_step * time_step / SCALE, 0.0)
            speed = model[tile, x]
            at = pl.ds(tile * TILE, TILE)
            courant[deep + x, at, :] = alive * (speed * speed)
            image[x, at, :] = (2.0 * time_step * time_step / SCALE) * speed
        return carry

    lax.fori_loop(0, cells, factors, 0)
    clear_dead(one, two, live, deep, deep + cells)

    def core(c, carry):
        advance(one, two, courant, drops, band, 0, deep + REACH + c * REACH, grad, True, deep)
        return carry

    lax.fori_loop(0, cells // REACH - 2, core, 0, unroll=2)


def clear_dead(one, two, live, first, last):
    tiles = one.shape[2] // TILE - 2
    for tile in range(1, tiles):

        @pl.when(tile >= live)
        def _():
            def clear(x, carry):
                for buffer in (one, two):
                    for field in range(2):
                        buffer[field, x, pl.ds(TILE + tile * TILE, TILE), :] = jnp.zeros(
                            (TILE, one.shape[3]), jnp.float32
                        )
                return carry

            lax.fori_loop(first, last, clear, 0)


def opening(start, count, small, fields, speeds, steps):
    groups, cells, _, depth = speeds.shape
    rows = fields[0].shape[2]
    tiles = rows // TILE
    deep = steps * REACH
    wide = cells + 2 * deep
    halo = pltpu.VMEM((tiles, deep - REACH, TILE, depth), jnp.float32)
    drops = pltpu.VMEM((steps, 2, wide, TILE, depth), jnp.float32)
    band = pltpu.VMEM((2 * depth, depth), jnp.bfloat16)
    buffer = pltpu.VMEM((2, wide, rows + 2 * TILE, depth), jnp.float32)
    courant = pltpu.VMEM((wide, rows, depth), jnp.float32)
    layers = pltpu.VMEM((cells, rows, depth), jnp.float32)
    vmem = pl.BlockSpec(memory_space=pltpu.VMEM)
    return pl.pallas_call(
        opening_kernel,
        out_shape=(halo, halo, drops, band, buffer, buffer, courant, layers, layers),
        in_specs=[pl.BlockSpec(memory_space=pltpu.SMEM)] * 2 + [pl.BlockSpec(memory_space=pltpu.HBM)] * 9,
        out_specs=(vmem,) * 9,
        scratch_shapes=[pltpu.SMEM(array.shape, array.dtype) for array in small]
        + [
            pltpu.VMEM((tiles, cells, TILE, depth), jnp.float32),
            pltpu.SemaphoreType.DMA((3 * tiles + 8,)),
        ],
        compiler_params=pltpu.CompilerParams(vmem_limit_bytes=8 << 20),
        cost_estimate=pl.CostEstimate(flops=4 << 20, bytes_accessed=4 << 20, transcendentals=0),
    )(start, count, *map(in_hbm, small), *map(in_hbm, fields), in_hbm(speeds))


def along_z(now, band, x):
    rows, depth = now.shape[2] - 2 * TILE, now.shape[3]
    inner = pl.ds(TILE, rows)
    fields = [now[field, pl.ds(x, REACH), inner, :].reshape(REACH * rows, depth) for field in range(2)]
    cells = jnp.concatenate(fields, axis=0)
    high = cells.astype(jnp.bfloat16)
    low = (cells - high.astype(jnp.float32)).astype(jnp.bfloat16)
    return jnp.dot(jnp.concatenate([high, low], axis=1), band[...], preferred_element_type=jnp.float32)


def laplacian(now, spread, field, i, x):
    rows = now.shape[2] - 2 * TILE
    inner = pl.ds(TILE, rows)
    center = now[field, x, inner, :]
    lap = (3.0 * scaled_weights[0]) * center
    for k in range(1, REACH + 1):
        near = now[field, x + k, inner, :] + now[field, x - k, inner, :]
        near = near + now[field, x, pl.ds(TILE + k, rows), :]
        near = near + now[field, x, pl.ds(TILE - k, rows), :]
        lap = lap + scaled_weights[k] * near
    at = (field * REACH + i) * rows
    return center, lap + spread[at : at + rows]


def store_layer(buffer, field, x, values, drop):
    rows = values.shape[0]
    buffer[field, x, pl.ds(TILE, TILE), :] = values[:TILE] + drop
    buffer[field, x, pl.ds(2 * TILE, rows - TILE), :] = values[TILE:]


def advance(now, other, courant, drops, band, step, x_first, grad, fresh, deep, finals=None):
    rows = now.shape[2] - 2 * TILE
    inner = pl.ds(TILE, rows)
    spread = along_z(now, band, x_first)
    for i in range(REACH):
        x = x_first + i
        pair = []
        for field in range(2):
            center, lap = laplacian(now, spread, field, i, x)
            pair.append((center, lap))
            ahead = 2.0 * center - other[field, x, inner, :] + courant[x] * lap
            if finals is None:
                store_layer(other, field, x, ahead, drops[step, field, x])
            else:
                finals[field, x - deep, pl.ds(0, TILE), :] = ahead[:TILE] + drops[step, field, x]
                finals[field, x - deep, pl.ds(TILE, rows - TILE), :] = ahead[TILE:]
        if grad is not None:
            term = pair[1][0] * pair[0][1]
            grad[x - deep] = term if fresh else grad[x - deep] + term


def early_kernel(steps, count, from_a, from_b, courant, drops, band, one_in, two_in, grad_in, one, two, grad, waiting, parts, sems):
    cells, rows, depth = grad.shape
    deep = steps * REACH
    deep_prev = deep - REACH
    wide = cells + 2 * deep
    odd = lax.axis_index("slab") % 2

    left_of_a = odd
    copies, bring = bringing(sems)
    inner = pl.ds(TILE, rows)
    for field in range(2):
        for buffer, on_left in ((from_a, left_of_a), (from_b, 1 - left_of_a)):
            at = (1 - on_left) * (deep + cells)
            bring(buffer.at[pl.ds(field * deep, deep)], one.at[field, pl.ds(at, deep), inner])
            at = on_left * REACH + (1 - on_left) * (deep + cells)
            bring(
                buffer.at[pl.ds(2 * deep + field * deep_prev, deep_prev)],
                two.at[field, pl.ds(at, deep_prev), inner],
            )
    def clear_parts(b, carry):
        parts[b] = jnp.zeros(parts.shape[1:], jnp.float32)
        return carry

    lax.fori_loop(0, parts.shape[0], clear_parts, 0)
    for copy in copies:
        copy.wait()
    clear_dead(one, two, count[0], 0, deep)
    clear_dead(one, two, count[0], deep + cells, wide)

    half = deep_prev // REACH

    def outside(c, carry):
        x_first = REACH + c * REACH + jnp.where(c >= half, cells, 0)
        spread = along_z(one, band, x_first)
        for i in range(REACH):
            x = x_first + i
            for field in range(2):
                center, lap = laplacian(one, spread, field, i, x)
                waiting[field, c * REACH + i] = lap
                store_layer(two, field, x, 2.0 * center - two[field, x, inner, :], drops[0, field, x])
        return carry

    def inside(c, carry):
        advance(one, two, courant, drops, band, 0, deep + c * (cells - REACH), grad, True, deep)
        return carry

    def core(c, carry):
        advance(two, one, courant, drops, band, 1, deep + REACH + c * REACH, grad, False, deep)
        return carry

    lax.fori_loop(0, 2, inside, 0, unroll=2)
    lax.fori_loop(0, 2 * half, outside, 0, unroll=2)
    lax.fori_loop(0, cells // REACH - 2, core, 0, unroll=2)


def late_kernel(
    steps,
    start,
    count,
    speed_a,
    speed_b,
    drops,
    band,
    image,
    waiting,
    one_in,
    two_in,
    courant_in,
    grad_in,
    parts_in,
    final_w,
    final_j,
    one,
    two,
    courant,
    grad,
    parts,
    finals,
    sems,
):
    cells, rows, depth = image.shape
    deep = steps * REACH
    deep_prev = deep - REACH
    tiles = rows // TILE
    odd = lax.axis_index("slab") % 2
    start_block = start[0]
    live = count[0]
    inner = pl.ds(TILE, rows)

    copies, bring = bringing(sems)

    def finish(h, carry):
        right = h >= deep_prev
        layer = jnp.where(right, h - deep_prev, h)
        x = jnp.where(right, deep + cells, REACH) + layer
        use_a = jnp.where(right, 1 - odd, odd) == 1
        for tile in range(tiles):
            alive = jnp.where(tile < live, time_step * time_step / SCALE, 0.0)
            speed = jnp.where(use_a, speed_a[tile, layer], speed_b[tile, layer])
            factor = alive * (speed * speed)
            courant[x, pl.ds(tile * TILE, TILE), :] = factor
            for field in range(2):
                at = pl.ds(TILE + tile * TILE, TILE)
                change = factor * waiting[field, h, pl.ds(tile * TILE, TILE), :]
                two[field, x, at, :] = two[field, x, at, :] + change
        return carry

    lax.fori_loop(0, 2 * deep_prev, finish, 0, unroll=4)

    now, other = two, one
    for step in range(1, steps):
        margin = REACH * (step + 1)
        half = (deep - margin) // REACH

        def outside(c, carry):
            x = margin + c * REACH + jnp.where(c >= half, cells, 0)
            advance(now, other, courant, drops, band, step, x, None, False, deep)
            return carry

        stride = cells - REACH if step == 1 else REACH

        def inside(c, carry):
            last = finals if step == steps - 1 else None
            advance(now, other, courant, drops, band, step, deep + c * stride, grad, False, deep, last)
            return carry

        if half:
            lax.fori_loop(0, 2 * half, outside, 0, unroll=2)
        groups = 2 if step == 1 else cells // REACH
        for first in range(0, groups, 2):
            lax.fori_loop(first, min(first + 2, groups), inside, 0, unroll=2)
            if step == steps - 1:
                done = pl.ds(first * REACH, min(2, groups - first) * REACH)
                bring(finals.at[0, done], final_w.at[0, done])
                bring(finals.at[1, done], final_j.at[0, done])
        now, other = other, now

    def place(x, carry):
        for tile in range(tiles):
            at = pl.ds(tile * TILE, TILE)
            parts[start_block + tile, x] = image[x, at, :] * grad[x, at, :]
        return carry

    lax.fori_loop(0, cells, place, 0, unroll=4)
    for copy in copies:
        copy.wait()


def early_steps(steps, count, from_a, from_b, courant, drops, band, one, two, grad, groups):
    cells, rows, depth = grad.shape
    deep_prev = (steps - 1) * REACH
    waiting = pltpu.VMEM((2, 2 * deep_prev, rows, depth), jnp.float32)
    parts = pltpu.VMEM((groups, cells, TILE, depth), jnp.float32)
    smem = pl.BlockSpec(memory_space=pltpu.SMEM)
    vmem = pl.BlockSpec(memory_space=pltpu.VMEM)
    same = [pltpu.VMEM(array.shape, array.dtype) for array in (one, two, grad)]

    def kernel(*refs):
        early_kernel(steps, *refs)

    return pl.pallas_call(
        kernel,
        out_shape=(*same, waiting, parts),
        in_specs=[smem, any_space(), any_space()] + [vmem] * 6,
        out_specs=(vmem,) * 5,
        input_output_aliases={6: 0, 7: 1, 8: 2},
        scratch_shapes=[pltpu.SemaphoreType.DMA((8,))],
        compiler_params=pltpu.CompilerParams(vmem_limit_bytes=8 << 20),
        cost_estimate=pl.CostEstimate(flops=20 << 20, bytes_accessed=4 << 20, transcendentals=0),
    )(count, from_a, from_b, courant, drops, band, one, two, grad)


def late_steps(steps, start, count, speed_a, speed_b, drops, band, image, waiting, one, two, courant, grad, parts):
    smem = pl.BlockSpec(memory_space=pltpu.SMEM)
    vmem = pl.BlockSpec(memory_space=pltpu.VMEM)
    final = jax.ShapeDtypeStruct((1, *image.shape), jnp.float32)
    same = [pltpu.VMEM(array.shape, array.dtype) for array in (one, two, courant, grad, parts)]

    def kernel(*refs):
        late_kernel(steps, *refs)

    results = pl.pallas_call(
        kernel,
        out_shape=(final, final, *same),
        in_specs=[smem] * 2 + [vmem] * 11,
        out_specs=(any_space(), any_space()) + (vmem,) * 5,
        input_output_aliases={8: 2, 9: 3, 10: 4, 11: 5, 12: 6},
        scratch_shapes=[
            pltpu.VMEM((2, *image.shape), jnp.float32),
            pltpu.SemaphoreType.DMA((2 * image.shape[0] // REACH,)),
        ],
        compiler_params=pltpu.CompilerParams(vmem_limit_bytes=8 << 20),
        cost_estimate=pl.CostEstimate(flops=40 << 20, bytes_accessed=6 << 20, transcendentals=0),
    )(start, count, speed_a, speed_b, drops, band, image, waiting, one, two, courant, grad, parts)
    return results[0], results[1], results[6]


def per_device(
    velocity,
    aperture_start,
    aperture_count,
    wave_prev,
    wave_now,
    adjoint_prev,
    adjoint_now,
    source_cells,
    wavelet,
    receiver_cells,
    trace,
):
    steps = wavelet.shape[1]
    deep = steps * REACH
    fields = (wave_now, adjoint_now, wave_prev, adjoint_prev)

    to_a, to_b = pack(fields, deep)
    from_a = swap_pairs(to_a, "slab", 0)
    from_b = swap_pairs(to_b, "slab", 1)
    speeds = lax.all_gather(velocity, "shot")

    cells_w, cells_j = (jnp.transpose(places, (2, 0, 1)) for places in (source_cells, receiver_cells))
    small = (cells_w, cells_j, wavelet, trace)
    to_a, to_b, drops, band, one, two, courant, image, grad = opening(
        aperture_start, aperture_count, small, fields, speeds, steps
    )
    speed_a = swap_pairs(to_a, "slab", 0)
    speed_b = swap_pairs(to_b, "slab", 1)
    one, two, grad, waiting, parts = early_steps(
        steps, aperture_count, from_a, from_b, courant, drops, band, one, two, grad, lax.axis_size("shot")
    )
    final_w, final_j, parts = late_steps(
        steps,
        aperture_start,
        aperture_count,
        speed_a,
        speed_b,
        drops,
        band,
        image,
        waiting,
        one,
        two,
        courant,
        grad,
        parts,
    )
    shares = lax.all_to_all(parts, "shot", 0, 0, tiled=True)
    return final_w, final_j, jnp.sum(shares, axis=0)


def solution(mesh):
    return jax.shard_map(
        per_device,
        mesh=mesh,
        in_specs=(
            P("slab", "shot", None),
            P("shot"),
            P("shot"),
            P("shot", "slab", None, None),
            P("shot", "slab", None, None),
            P("shot", "slab", None, None),
            P("shot", "slab", None, None),
            P("shot", None, None),
            P("shot", None, None),
            P("shot", None, None),
            P("shot", None, None),
        ),
        out_specs=(
            P("shot", "slab", None, None),
            P("shot", "slab", None, None),
            P("slab", "shot", None),
        ),
        check_vma=False,
    )
```

```python
import jax
import jax.numpy as jnp
from jax import lax
from jax.experimental import pallas as pl
from jax.experimental.pallas import tpu as pltpu
from jax.sharding import PartitionSpec as P


SCALE = 5040.0
scaled_weights = (-14350.0, 8064.0, -1008.0, 128.0, -9.0)
time_step = 0.09
REACH = 4
TILE = 8


def swap_pairs(block, axis, first):
    count = lax.axis_size(axis)
    route = []
    for i in range(first, count - 1, 2):
        route += [(i, i + 1), (i + 1, i)]
    return lax.ppermute(block, axis, route)


def any_space():
    return pl.BlockSpec(memory_space=pl.ANY)


def in_hbm(array):
    return pltpu.with_memory_space_constraint(array, pltpu.HBM)


def packing_kernel(now_w, now_j, prev_w, prev_j, to_a, to_b, sems):
    cells = now_w.shape[1]
    deep_now = (to_a.shape[0] // 2 + REACH) // 2
    deep_prev = deep_now - REACH
    odd = lax.axis_index("slab") % 2
    copies, bring = bringing(sems)
    for out, side in ((to_a, 1 - odd), (to_b, odd)):
        at = 0
        for field, deep in ((now_w, deep_now), (now_j, deep_now), (prev_w, deep_prev), (prev_j, deep_prev)):
            bring(field.at[0, pl.ds(side * (cells - deep), deep)], out.at[pl.ds(at, deep)])
            at += deep
    for copy in copies:
        copy.wait()


def pack(fields, deep):
    rows, depth = fields[0].shape[2:]
    out = pltpu.VMEM((4 * deep - 2 * REACH, rows, depth), jnp.float32)
    return pl.pallas_call(
        packing_kernel,
        out_shape=(out, out),
        in_specs=[pl.BlockSpec(memory_space=pltpu.HBM)] * 4,
        out_specs=(any_space(), any_space()),
        scratch_shapes=[pltpu.SemaphoreType.DMA((8,))],
        compiler_params=pltpu.CompilerParams(vmem_limit_bytes=1 << 20),
        cost_estimate=pl.CostEstimate(flops=0, bytes_accessed=4 << 20, transcendentals=0),
    )(*map(in_hbm, fields))


def bringing(sems):
    copies = []

    def bring(source, target):
        copy = pltpu.make_async_copy(source, target, sems.at[len(copies)])
        copy.start()
        copies.append(copy)

    return copies, bring


def opening_kernel(
    start,
    count,
    cells_w_in,
    cells_j_in,
    amps_w_in,
    amps_j_in,
    now_w,
    now_j,
    prev_w,
    prev_j,
    speeds,
    to_a,
    to_b,
    drops,
    band,
    one,
    two,
    courant,
    image,
    grad,
    cells_w,
    cells_j,
    amps_w,
    amps_j,
    sems,
):
    cells, rows, depth = image.shape
    tiles = rows // TILE
    steps = drops.shape[0]
    deep = steps * REACH
    near = deep - 2 * REACH
    wide = drops.shape[2]
    slab = lax.axis_index("slab")
    odd = slab % 2
    start_block = start[0]
    live = count[0]
    copies, bring = bringing(sems)
    for source, target in ((cells_w_in, cells_w), (cells_j_in, cells_j), (amps_w_in, amps_w), (amps_j_in, amps_j)):
        bring(source, target)
    inner = pl.ds(TILE, rows)
    for field, (now, prev) in enumerate(((now_w, prev_w), (now_j, prev_j))):
        bring(now.at[0], one.at[field, pl.ds(deep, cells), inner])
        bring(prev.at[0], two.at[field, pl.ds(deep, cells), inner])

    zero_tile = jnp.zeros((TILE, depth), jnp.float32)

    def clear(x, carry):
        for step in range(steps):
            for field in range(2):
                drops[step, field, x] = zero_tile
        for buffer in (one, two):
            for field in range(2):
                buffer[field, x, pl.ds(0, TILE), :] = zero_tile
                buffer[field, x, pl.ds(TILE + rows, TILE), :] = zero_tile
        return carry

    lax.fori_loop(0, wide, clear, 0)
    away = lax.broadcasted_iota(jnp.int32, (depth, depth), 0) - lax.broadcasted_iota(jnp.int32, (depth, depth), 1)
    matrix = jnp.zeros((depth, depth), jnp.float32)
    for k in range(1, REACH + 1):
        matrix = jnp.where((away == k) | (away == -k), scaled_weights[k], matrix)
    band[pl.ds(0, depth), :] = matrix.astype(jnp.bfloat16)
    band[pl.ds(depth, depth), :] = matrix.astype(jnp.bfloat16)

    def factors(x, carry):
        for tile in range(tiles):
            alive = jnp.where(tile < live, time_step * time_step / SCALE, 0.0)
            speed = speeds[start_block + tile, x]
            at = pl.ds(tile * TILE, TILE)
            courant[deep + x, at, :] = alive * (speed * speed)
            image[x, at, :] = (2.0 * time_step * time_step / SCALE) * speed
        return carry

    lax.fori_loop(0, cells, factors, 0, unroll=4)

    for out, side in ((to_a, 1 - odd), (to_b, odd)):
        for layer in range(near):
            for tile in range(tiles):
                speed = speeds[start_block + tile, side * (cells - near) + layer]
                out[layer, pl.ds(tile * TILE, TILE), :] = speed
    for copy in copies[:4]:
        copy.wait()

    row = lax.broadcasted_iota(jnp.int32, (TILE, depth), 0)
    col = lax.broadcasted_iota(jnp.int32, (TILE, depth), 1)

    def inject(field, places, amps):
        def one_cell(s, carry):
            x = places[0, 0, s] - (slab * cells - deep)

            @pl.when((x >= 0) & (x < wide))
            def _():
                here = (row == places[1, 0, s]) & (col == places[2, 0, s])
                for step in range(steps):
                    drops[step, field, x] = drops[step, field, x] + jnp.where(here, amps[0, step, s], 0.0)

            return carry

        lax.fori_loop(0, places.shape[2], one_cell, 0)

    inject(0, cells_w, amps_w)
    inject(1, cells_j, amps_j)

    for copy in copies[4:]:
        copy.wait()
    clear_dead(one, two, live, deep, deep + cells)

    def core(c, carry):
        advance(one, two, courant, drops, band, 0, deep + REACH + c * REACH, grad, True, deep)
        return carry

    lax.fori_loop(0, cells // REACH - 2, core, 0, unroll=2)
    for out, side in ((to_a, 1 - odd), (to_b, odd)):
        for field in range(2):
            for i in range(REACH):
                x = deep + REACH + (1 - side) * (cells - 3 * REACH) + i
                out[near + field * REACH + i] = two[field, x, inner, :]


def clear_dead(one, two, live, first, last):
    tiles = one.shape[2] // TILE - 2
    for tile in range(1, tiles):

        @pl.when(tile >= live)
        def _():
            def clear(x, carry):
                for buffer in (one, two):
                    for field in range(2):
                        buffer[field, x, pl.ds(TILE + tile * TILE, TILE), :] = jnp.zeros(
                            (TILE, one.shape[3]), jnp.float32
                        )
                return carry

            lax.fori_loop(first, last, clear, 0)


def opening(start, count, small, fields, speeds, steps):
    cells, depth = speeds.shape[1], speeds.shape[3]
    rows = fields[0].shape[2]
    deep = steps * REACH
    wide = cells + 2 * deep
    halo = pltpu.VMEM((deep, rows, depth), jnp.float32)
    drops = pltpu.VMEM((steps, 2, wide, TILE, depth), jnp.float32)
    band = pltpu.VMEM((2 * depth, depth), jnp.bfloat16)
    buffer = pltpu.VMEM((2, wide, rows + 2 * TILE, depth), jnp.float32)
    courant = pltpu.VMEM((wide, rows, depth), jnp.float32)
    layers = pltpu.VMEM((cells, rows, depth), jnp.float32)
    vmem = pl.BlockSpec(memory_space=pltpu.VMEM)
    return pl.pallas_call(
        opening_kernel,
        out_shape=(halo, halo, drops, band, buffer, buffer, courant, layers, layers),
        in_specs=[pl.BlockSpec(memory_space=pltpu.SMEM)] * 2 + [pl.BlockSpec(memory_space=pltpu.HBM)] * 8 + [vmem],
        out_specs=(vmem,) * 9,
        scratch_shapes=[pltpu.SMEM(array.shape, array.dtype) for array in small]
        + [pltpu.SemaphoreType.DMA((8,))],
        compiler_params=pltpu.CompilerParams(vmem_limit_bytes=8 << 20),
        cost_estimate=pl.CostEstimate(flops=4 << 20, bytes_accessed=4 << 20, transcendentals=0),
    )(start, count, *map(in_hbm, small), *map(in_hbm, fields), speeds)


def along_z(now, band, x):
    rows, depth = now.shape[2] - 2 * TILE, now.shape[3]
    inner = pl.ds(TILE, rows)
    fields = [now[field, pl.ds(x, REACH), inner, :].reshape(REACH * rows, depth) for field in range(2)]
    cells = jnp.concatenate(fields, axis=0)
    high = cells.astype(jnp.bfloat16)
    low = (cells - high.astype(jnp.float32)).astype(jnp.bfloat16)
    return jnp.dot(jnp.concatenate([high, low], axis=1), band[...], preferred_element_type=jnp.float32)


def each_tile(now, band, x_first, visit):
    rows = now.shape[2] - 2 * TILE
    spread = along_z(now, band, x_first)
    for tile in range(rows // TILE):
        at = TILE + tile * TILE
        pairs = []
        for field in range(2):
            line = [now[field, x_first + i, pl.ds(at, TILE), :] for i in range(-REACH, 2 * REACH)]
            for i in range(REACH):
                center = line[REACH + i]
                lap = (3.0 * scaled_weights[0]) * center
                for k in range(1, REACH + 1):
                    near = line[REACH + i + k] + line[REACH + i - k]
                    near = near + now[field, x_first + i, pl.ds(at + k, TILE), :]
                    near = near + now[field, x_first + i, pl.ds(at - k, TILE), :]
                    lap = lap + scaled_weights[k] * near
                row = (field * REACH + i) * rows + tile * TILE
                pairs.append((center, lap + spread[row : row + TILE]))
        for i in range(REACH):
            visit(tile, i, (pairs[i], pairs[REACH + i]))


def advance(now, other, courant, drops, band, step, x_first, grad, fresh, deep, finals=None):
    def visit(tile, i, pair):
        x = x_first + i
        own = pl.ds(tile * TILE, TILE)
        padded = pl.ds(TILE + tile * TILE, TILE)
        factor = courant[x, own, :]
        for field, (center, lap) in enumerate(pair):
            ahead = 2.0 * center - other[field, x, padded, :] + factor * lap
            if tile == 0:
                ahead = ahead + drops[step, field, x]
            if finals is None:
                other[field, x, padded, :] = ahead
            else:
                finals[field, x - deep, own, :] = ahead
        if grad is not None:
            term = pair[1][0] * pair[0][1]
            grad[x - deep, own, :] = term if fresh else grad[x - deep, own, :] + term

    each_tile(now, band, x_first, visit)


def early_kernel(steps, count, from_a, from_b, courant, drops, band, one_in, two_in, grad_in, one, two, grad, waiting, parts, sems):
    cells, rows, depth = grad.shape
    deep = steps * REACH
    near = deep - 2 * REACH
    held = near + REACH
    wide = cells + 2 * deep
    odd = lax.axis_index("slab") % 2

    left_of_a = odd
    copies, bring = bringing(sems)
    inner = pl.ds(TILE, rows)
    for field in range(2):
        for buffer, on_left in ((from_a, left_of_a), (from_b, 1 - left_of_a)):
            at = on_left * (deep - held) + (1 - on_left) * (deep + cells)
            bring(buffer.at[pl.ds(field * held, held)], one.at[field, pl.ds(at, held), inner])
            at = on_left * (deep - near) + (1 - on_left) * (deep + cells)
            bring(buffer.at[pl.ds(2 * held + field * near, near)], two.at[field, pl.ds(at, near), inner])
    def clear_parts(b, carry):
        parts[b] = jnp.zeros(parts.shape[1:], jnp.float32)
        return carry

    lax.fori_loop(0, parts.shape[0], clear_parts, 0)
    for copy in copies:
        copy.wait()
    clear_dead(one, two, count[0], 0, deep)
    clear_dead(one, two, count[0], deep + cells, wide)

    half = near // REACH

    def outside(c, carry):
        x_first = deep - near + c * REACH + jnp.where(c >= half, cells, 0)

        def visit(tile, i, pair):
            x = x_first + i
            padded = pl.ds(TILE + tile * TILE, TILE)
            for field, (center, lap) in enumerate(pair):
                waiting[field, c * REACH + i, pl.ds(tile * TILE, TILE), :] = lap
                ahead = 2.0 * center - two[field, x, padded, :]
                two[field, x, padded, :] = ahead + drops[0, field, x] if tile == 0 else ahead

        each_tile(one, band, x_first, visit)
        return carry

    def inside(c, carry):
        advance(one, two, courant, drops, band, 0, deep + c * (cells - REACH), grad, True, deep)
        return carry

    def core(c, carry):
        advance(two, one, courant, drops, band, 1, deep + REACH + c * REACH, grad, False, deep)
        return carry

    lax.fori_loop(0, 2, inside, 0, unroll=2)
    lax.fori_loop(0, 2 * half, outside, 0, unroll=2)
    lax.fori_loop(0, cells // REACH - 2, core, 0, unroll=2)


def late_kernel(
    steps,
    start,
    count,
    next_a,
    next_b,
    drops,
    band,
    image,
    waiting,
    one_in,
    two_in,
    courant_in,
    grad_in,
    parts_in,
    final_w,
    final_j,
    one,
    two,
    courant,
    grad,
    parts,
    finals,
    sems,
):
    cells, rows, depth = image.shape
    deep = steps * REACH
    near = deep - 2 * REACH
    tiles = rows // TILE
    odd = lax.axis_index("slab") % 2
    start_block = start[0]
    live = count[0]

    copies, bring = bringing(sems)

    def finish(h, carry):
        right = h >= near
        layer = jnp.where(right, h - near, h)
        x = jnp.where(right, deep + cells, deep - near) + layer
        use_a = jnp.where(right, 1 - odd, odd) == 1
        for tile in range(tiles):
            alive = jnp.where(tile < live, time_step * time_step / SCALE, 0.0)
            own = pl.ds(tile * TILE, TILE)
            speed = jnp.where(use_a, next_a[layer, own, :], next_b[layer, own, :])
            factor = alive * (speed * speed)
            courant[x, own, :] = factor
            for field in range(2):
                at = pl.ds(TILE + tile * TILE, TILE)
                change = factor * waiting[field, h, own, :]
                two[field, x, at, :] = two[field, x, at, :] + change
        return carry

    lax.fori_loop(0, 2 * near, finish, 0, unroll=4)
    inner = pl.ds(TILE, rows)
    for message, left in ((next_a, odd), (next_b, 1 - odd)):
        for field in range(2):
            for i in range(REACH):
                x = left * (deep - near - REACH) + (1 - left) * (deep + cells + near) + i
                two[field, x, inner, :] = message[near + field * REACH + i]

    now, other = two, one
    for step in range(1, steps):
        margin = REACH * (step + 1)
        half = (deep - margin) // REACH

        def outside(c, carry):
            x = margin + c * REACH + jnp.where(c >= half, cells, 0)
            advance(now, other, courant, drops, band, step, x, None, False, deep)
            return carry

        stride = cells - REACH if step == 1 else REACH

        def inside(c, carry):
            last = finals if step == steps - 1 else None
            advance(now, other, courant, drops, band, step, deep + c * stride, grad, False, deep, last)
            return carry

        if half:
            lax.fori_loop(0, 2 * half, outside, 0, unroll=2)
        groups = 2 if step == 1 else cells // REACH
        for first in range(0, groups, 2):
            lax.fori_loop(first, min(first + 2, groups), inside, 0, unroll=2)
            if step == steps - 1:
                done = pl.ds(first * REACH, min(2, groups - first) * REACH)
                bring(finals.at[0, done], final_w.at[0, done])
                bring(finals.at[1, done], final_j.at[0, done])
        now, other = other, now

    def place(x, carry):
        for tile in range(tiles):
            at = pl.ds(tile * TILE, TILE)
            parts[start_block + tile, x] = image[x, at, :] * grad[x, at, :]
        return carry

    lax.fori_loop(0, cells, place, 0, unroll=4)
    for copy in copies:
        copy.wait()


def early_steps(steps, count, from_a, from_b, courant, drops, band, one, two, grad, groups):
    cells, rows, depth = grad.shape
    waiting = pltpu.VMEM((2, 2 * (steps - 2) * REACH, rows, depth), jnp.float32)
    parts = pltpu.VMEM((groups, cells, TILE, depth), jnp.float32)
    smem = pl.BlockSpec(memory_space=pltpu.SMEM)
    vmem = pl.BlockSpec(memory_space=pltpu.VMEM)
    same = [pltpu.VMEM(array.shape, array.dtype) for array in (one, two, grad)]

    def kernel(*refs):
        early_kernel(steps, *refs)

    return pl.pallas_call(
        kernel,
        out_shape=(*same, waiting, parts),
        in_specs=[smem, any_space(), any_space()] + [vmem] * 6,
        out_specs=(vmem,) * 5,
        input_output_aliases={6: 0, 7: 1, 8: 2},
        scratch_shapes=[pltpu.SemaphoreType.DMA((8,))],
        compiler_params=pltpu.CompilerParams(vmem_limit_bytes=8 << 20),
        cost_estimate=pl.CostEstimate(flops=20 << 20, bytes_accessed=4 << 20, transcendentals=0),
    )(count, from_a, from_b, courant, drops, band, one, two, grad)


def late_steps(steps, start, count, next_a, next_b, drops, band, image, waiting, one, two, courant, grad, parts):
    smem = pl.BlockSpec(memory_space=pltpu.SMEM)
    vmem = pl.BlockSpec(memory_space=pltpu.VMEM)
    final = jax.ShapeDtypeStruct((1, *image.shape), jnp.float32)
    same = [pltpu.VMEM(array.shape, array.dtype) for array in (one, two, courant, grad, parts)]

    def kernel(*refs):
        late_kernel(steps, *refs)

    results = pl.pallas_call(
        kernel,
        out_shape=(final, final, *same),
        in_specs=[smem] * 2 + [vmem] * 11,
        out_specs=(any_space(), any_space()) + (vmem,) * 5,
        input_output_aliases={8: 2, 9: 3, 10: 4, 11: 5, 12: 6},
        scratch_shapes=[
            pltpu.VMEM((2, *image.shape), jnp.float32),
            pltpu.SemaphoreType.DMA((2 * image.shape[0] // REACH,)),
        ],
        compiler_params=pltpu.CompilerParams(vmem_limit_bytes=8 << 20),
        cost_estimate=pl.CostEstimate(flops=40 << 20, bytes_accessed=6 << 20, transcendentals=0),
    )(start, count, next_a, next_b, drops, band, image, waiting, one, two, courant, grad, parts)
    return results[0], results[1], results[6]


def per_device(
    velocity,
    aperture_start,
    aperture_count,
    wave_prev,
    wave_now,
    adjoint_prev,
    adjoint_now,
    source_cells,
    wavelet,
    receiver_cells,
    trace,
):
    steps = wavelet.shape[1]
    deep = steps * REACH
    fields = (wave_now, adjoint_now, wave_prev, adjoint_prev)

    to_a, to_b = pack(fields, deep - REACH)
    from_a = swap_pairs(to_a, "slab", 0)
    from_b = swap_pairs(to_b, "slab", 1)
    speeds = lax.all_gather(velocity, "shot")

    cells_w, cells_j = (jnp.transpose(places, (2, 0, 1)) for places in (source_cells, receiver_cells))
    small = (cells_w, cells_j, wavelet, trace)
    to_a, to_b, drops, band, one, two, courant, image, grad = opening(
        aperture_start, aperture_count, small, fields, speeds, steps
    )
    next_a = swap_pairs(to_a, "slab", 0)
    next_b = swap_pairs(to_b, "slab", 1)
    one, two, grad, waiting, parts = early_steps(
        steps, aperture_count, from_a, from_b, courant, drops, band, one, two, grad, lax.axis_size("shot")
    )
    final_w, final_j, parts = late_steps(
        steps,
        aperture_start,
        aperture_count,
        next_a,
        next_b,
        drops,
        band,
        image,
        waiting,
        one,
        two,
        courant,
        grad,
        parts,
    )
    shares = lax.all_to_all(parts, "shot", 0, 0, tiled=True)
    return final_w, final_j, jnp.sum(shares, axis=0)


def solution(mesh):
    return jax.shard_map(
        per_device,
        mesh=mesh,
        in_specs=(
            P("slab", "shot", None),
            P("shot"),
            P("shot"),
            P("shot", "slab", None, None),
            P("shot", "slab", None, None),
            P("shot", "slab", None, None),
            P("shot", "slab", None, None),
            P("shot", None, None),
            P("shot", None, None),
            P("shot", None, None),
            P("shot", None, None),
        ),
        out_specs=(
            P("shot", "slab", None, None),
            P("shot", "slab", None, None),
            P("slab", "shot", None),
        ),
        check_vma=False,
    )
```

```python
import jax
import jax.numpy as jnp
from jax import lax
from jax.experimental import pallas as pl
from jax.experimental.pallas import tpu as pltpu
from jax.sharding import PartitionSpec as P


SCALE = 5040.0
scaled_weights = (-14350.0, 8064.0, -1008.0, 128.0, -9.0)
time_step = 0.09
REACH = 4
TILE = 8


def swap_pairs(block, axis, first):
    count = lax.axis_size(axis)
    route = []
    for i in range(first, count - 1, 2):
        route += [(i, i + 1), (i + 1, i)]
    return lax.ppermute(block, axis, route)


def any_space():
    return pl.BlockSpec(memory_space=pl.ANY)


def in_hbm(array):
    return pltpu.with_memory_space_constraint(array, pltpu.HBM)


def packing_kernel(now_w, now_j, prev_w, prev_j, to_a, to_b, sems):
    cells = now_w.shape[1]
    deep_now = (to_a.shape[0] // 2 + REACH) // 2
    deep_prev = deep_now - REACH
    odd = lax.axis_index("slab") % 2
    copies, bring = bringing(sems)
    for out, side in ((to_a, 1 - odd), (to_b, odd)):
        at = 0
        for field, deep in ((now_w, deep_now), (now_j, deep_now), (prev_w, deep_prev), (prev_j, deep_prev)):
            bring(field.at[0, pl.ds(side * (cells - deep), deep)], out.at[pl.ds(at, deep)])
            at += deep
    for copy in copies:
        copy.wait()


def pack(fields, deep):
    rows, depth = fields[0].shape[2:]
    out = pltpu.VMEM((4 * deep - 2 * REACH, rows, depth), jnp.float32)
    return pl.pallas_call(
        packing_kernel,
        out_shape=(out, out),
        in_specs=[pl.BlockSpec(memory_space=pltpu.HBM)] * 4,
        out_specs=(any_space(), any_space()),
        scratch_shapes=[pltpu.SemaphoreType.DMA((8,))],
        compiler_params=pltpu.CompilerParams(vmem_limit_bytes=1 << 20),
        cost_estimate=pl.CostEstimate(flops=0, bytes_accessed=4 << 20, transcendentals=0),
    )(*map(in_hbm, fields))


def bringing(sems):
    copies = []

    def bring(source, target):
        copy = pltpu.make_async_copy(source, target, sems.at[len(copies)])
        copy.start()
        copies.append(copy)

    return copies, bring


def opening_kernel(
    start,
    count,
    cells_w_in,
    cells_j_in,
    amps_w_in,
    amps_j_in,
    now_w,
    now_j,
    prev_w,
    prev_j,
    speeds,
    to_a,
    to_b,
    drops,
    band,
    one,
    two,
    courant,
    image,
    grad,
    cells_w,
    cells_j,
    amps_w,
    amps_j,
    sems,
):
    cells, rows, depth = image.shape
    tiles = rows // TILE
    steps = drops.shape[0]
    deep = steps * REACH
    near = deep - 2 * REACH
    wide = drops.shape[2]
    slab = lax.axis_index("slab")
    odd = slab % 2
    start_block = start[0]
    live = count[0]
    copies, bring = bringing(sems)
    for source, target in ((cells_w_in, cells_w), (cells_j_in, cells_j), (amps_w_in, amps_w), (amps_j_in, amps_j)):
        bring(source, target)
    inner = pl.ds(TILE, rows)
    for field, (now, prev) in enumerate(((now_w, prev_w), (now_j, prev_j))):
        bring(now.at[0], one.at[field, pl.ds(deep, cells), inner])
        bring(prev.at[0], two.at[field, pl.ds(deep, cells), inner])

    zero_tile = jnp.zeros((TILE, depth), jnp.float32)

    def clear(x, carry):
        for step in range(steps):
            for field in range(2):
                drops[step, field, x] = zero_tile
        for buffer in (one, two):
            for field in range(2):
                buffer[field, x, pl.ds(0, TILE), :] = zero_tile
                buffer[field, x, pl.ds(TILE + rows, TILE), :] = zero_tile
        return carry

    lax.fori_loop(0, wide, clear, 0)
    away = lax.broadcasted_iota(jnp.int32, (depth, depth), 0) - lax.broadcasted_iota(jnp.int32, (depth, depth), 1)
    matrix = jnp.zeros((depth, depth), jnp.float32)
    for k in range(1, REACH + 1):
        matrix = jnp.where((away == k) | (away == -k), scaled_weights[k], matrix)
    band[pl.ds(0, depth), :] = matrix.astype(jnp.bfloat16)
    band[pl.ds(depth, depth), :] = matrix.astype(jnp.bfloat16)

    def factors(x, carry):
        for tile in range(tiles):
            alive = jnp.where(tile < live, time_step * time_step / SCALE, 0.0)
            speed = speeds[start_block + tile, x]
            at = pl.ds(tile * TILE, TILE)
            courant[deep + x, at, :] = alive * (speed * speed)
            image[x, at, :] = (2.0 * time_step * time_step / SCALE) * speed
        return carry

    lax.fori_loop(0, cells, factors, 0, unroll=4)

    for out, side in ((to_a, 1 - odd), (to_b, odd)):
        for layer in range(near):
            for tile in range(tiles):
                speed = speeds[start_block + tile, side * (cells - near) + layer]
                out[layer, pl.ds(tile * TILE, TILE), :] = speed
    for copy in copies[:4]:
        copy.wait()

    row = lax.broadcasted_iota(jnp.int32, (TILE, depth), 0)
    col = lax.broadcasted_iota(jnp.int32, (TILE, depth), 1)

    def inject(field, places, amps):
        def one_cell(s, carry):
            x = places[0, 0, s] - (slab * cells - deep)

            @pl.when((x >= 0) & (x < wide))
            def _():
                here = (row == places[1, 0, s]) & (col == places[2, 0, s])
                for step in range(steps):
                    drops[step, field, x] = drops[step, field, x] + jnp.where(here, amps[0, step, s], 0.0)

            return carry

        lax.fori_loop(0, places.shape[2], one_cell, 0)

    inject(0, cells_w, amps_w)
    inject(1, cells_j, amps_j)

    for copy in copies[4:]:
        copy.wait()
    clear_dead(one, two, live, deep, deep + cells)

    for groups in paired(range(deep + REACH, deep + cells - REACH, REACH)):
        advance(one, two, courant, drops, band, 0, groups, grad, True, deep)
    for out, side in ((to_a, 1 - odd), (to_b, odd)):
        for field in range(2):
            for i in range(REACH):
                x = deep + REACH + (1 - side) * (cells - 3 * REACH) + i
                out[near + field * REACH + i] = two[field, x, inner, :]


def clear_dead(one, two, live, first, last):
    tiles = one.shape[2] // TILE - 2
    for tile in range(1, tiles):

        @pl.when(tile >= live)
        def _():
            def clear(x, carry):
                for buffer in (one, two):
                    for field in range(2):
                        buffer[field, x, pl.ds(TILE + tile * TILE, TILE), :] = jnp.zeros(
                            (TILE, one.shape[3]), jnp.float32
                        )
                return carry

            lax.fori_loop(first, last, clear, 0)


def opening(start, count, small, fields, speeds, steps):
    cells, depth = speeds.shape[1], speeds.shape[3]
    rows = fields[0].shape[2]
    deep = steps * REACH
    wide = cells + 2 * deep
    halo = pltpu.VMEM((deep, rows, depth), jnp.float32)
    drops = pltpu.VMEM((steps, 2, wide, TILE, depth), jnp.float32)
    band = pltpu.VMEM((2 * depth, depth), jnp.bfloat16)
    buffer = pltpu.VMEM((2, wide, rows + 2 * TILE, depth), jnp.float32)
    courant = pltpu.VMEM((wide, rows, depth), jnp.float32)
    layers = pltpu.VMEM((cells, rows, depth), jnp.float32)
    vmem = pl.BlockSpec(memory_space=pltpu.VMEM)
    return pl.pallas_call(
        opening_kernel,
        out_shape=(halo, halo, drops, band, buffer, buffer, courant, layers, layers),
        in_specs=[pl.BlockSpec(memory_space=pltpu.SMEM)] * 2 + [pl.BlockSpec(memory_space=pltpu.HBM)] * 8 + [vmem],
        out_specs=(vmem,) * 9,
        scratch_shapes=[pltpu.SMEM(array.shape, array.dtype) for array in small]
        + [pltpu.SemaphoreType.DMA((8,))],
        compiler_params=pltpu.CompilerParams(vmem_limit_bytes=8 << 20),
        cost_estimate=pl.CostEstimate(flops=4 << 20, bytes_accessed=4 << 20, transcendentals=0),
    )(start, count, *map(in_hbm, small), *map(in_hbm, fields), speeds)


def along_z(now, band, field, x):
    rows, depth = now.shape[2] - 2 * TILE, now.shape[3]
    cells = now[field, pl.ds(x, REACH), pl.ds(TILE, rows), :].reshape(REACH * rows, depth)
    high = cells.astype(jnp.bfloat16)
    low = (cells - high.astype(jnp.float32)).astype(jnp.bfloat16)
    return jnp.dot(jnp.concatenate([high, low], axis=1), band[...], preferred_element_type=jnp.float32)


def each_tile(now, band, groups, visit):
    rows = now.shape[2] - 2 * TILE
    spreads = [[along_z(now, band, field, x_first) for field in range(2)] for x_first in groups]
    for g, x_first in enumerate(groups):
        for tile in range(rows // TILE):
            at = TILE + tile * TILE
            pairs = []
            for field in range(2):
                line = [now[field, x_first + i, pl.ds(at, TILE), :] for i in range(-REACH, 2 * REACH)]
                for i in range(REACH):
                    center = line[REACH + i]
                    lap = (3.0 * scaled_weights[0]) * center
                    for k in range(1, REACH + 1):
                        near = line[REACH + i + k] + line[REACH + i - k]
                        near = near + now[field, x_first + i, pl.ds(at + k, TILE), :]
                        near = near + now[field, x_first + i, pl.ds(at - k, TILE), :]
                        lap = lap + scaled_weights[k] * near
                    row = i * rows + tile * TILE
                    pairs.append((center, lap + spreads[g][field][row : row + TILE]))
            for i in range(REACH):
                visit(g, tile, i, (pairs[i], pairs[REACH + i]))


def advance(now, other, courant, drops, band, step, groups, grad, fresh, deep, finals=None):
    def visit(g, tile, i, pair):
        x = groups[g] + i
        own = pl.ds(tile * TILE, TILE)
        padded = pl.ds(TILE + tile * TILE, TILE)
        factor = courant[x, own, :]
        for field, (center, lap) in enumerate(pair):
            ahead = 2.0 * center - other[field, x, padded, :] + factor * lap
            if tile == 0:
                ahead = ahead + drops[step, field, x]
            if finals is None:
                other[field, x, padded, :] = ahead
            else:
                finals[field, x - deep, own, :] = ahead
        if grad is not None:
            term = pair[1][0] * pair[0][1]
            grad[x - deep, own, :] = term if fresh else grad[x - deep, own, :] + term

    each_tile(now, band, groups, visit)


def early_kernel(steps, count, from_a, from_b, courant, drops, band, one_in, two_in, grad_in, one, two, grad, waiting, parts, sems):
    cells, rows, depth = grad.shape
    deep = steps * REACH
    near = deep - 2 * REACH
    held = near + REACH
    wide = cells + 2 * deep
    odd = lax.axis_index("slab") % 2

    left_of_a = odd
    copies, bring = bringing(sems)
    inner = pl.ds(TILE, rows)
    for field in range(2):
        for buffer, on_left in ((from_a, left_of_a), (from_b, 1 - left_of_a)):
            at = on_left * (deep - held) + (1 - on_left) * (deep + cells)
            bring(buffer.at[pl.ds(field * held, held)], one.at[field, pl.ds(at, held), inner])
            at = on_left * (deep - near) + (1 - on_left) * (deep + cells)
            bring(buffer.at[pl.ds(2 * held + field * near, near)], two.at[field, pl.ds(at, near), inner])
    def clear_parts(b, carry):
        parts[b] = jnp.zeros(parts.shape[1:], jnp.float32)
        return carry

    lax.fori_loop(0, parts.shape[0], clear_parts, 0)
    for copy in copies:
        copy.wait()
    clear_dead(one, two, count[0], 0, deep)
    clear_dead(one, two, count[0], deep + cells, wide)

    def outside(c, carry):
        groups = [deep - near + c * (near + cells) + i for i in range(0, near, REACH)]

        def visit(g, tile, i, pair):
            x = groups[g] + i
            padded = pl.ds(TILE + tile * TILE, TILE)
            for field, (center, lap) in enumerate(pair):
                waiting[field, c * near + g * REACH + i, pl.ds(tile * TILE, TILE), :] = lap
                ahead = 2.0 * center - two[field, x, padded, :]
                two[field, x, padded, :] = ahead + drops[0, field, x] if tile == 0 else ahead

        each_tile(one, band, groups, visit)
        return carry

    advance(one, two, courant, drops, band, 0, [deep, deep + cells - REACH], grad, True, deep)
    lax.fori_loop(0, 2, outside, 0)
    for groups in paired(range(deep + REACH, deep + cells - REACH, REACH)):
        advance(two, one, courant, drops, band, 1, groups, grad, False, deep)


def paired(starts):
    starts = list(starts)
    return [starts[i : i + 2] for i in range(0, len(starts), 2)]


def late_kernel(
    steps,
    start,
    count,
    next_a,
    next_b,
    drops,
    band,
    image,
    waiting,
    one_in,
    two_in,
    courant_in,
    grad_in,
    parts_in,
    final_w,
    final_j,
    one,
    two,
    courant,
    grad,
    parts,
    finals,
    sems,
):
    cells, rows, depth = image.shape
    deep = steps * REACH
    near = deep - 2 * REACH
    tiles = rows // TILE
    odd = lax.axis_index("slab") % 2
    start_block = start[0]
    live = count[0]

    copies, bring = bringing(sems)

    def finish(h, carry):
        right = h >= near
        layer = jnp.where(right, h - near, h)
        x = jnp.where(right, deep + cells, deep - near) + layer
        use_a = jnp.where(right, 1 - odd, odd) == 1
        for tile in range(tiles):
            alive = jnp.where(tile < live, time_step * time_step / SCALE, 0.0)
            own = pl.ds(tile * TILE, TILE)
            speed = jnp.where(use_a, next_a[layer, own, :], next_b[layer, own, :])
            factor = alive * (speed * speed)
            courant[x, own, :] = factor
            for field in range(2):
                at = pl.ds(TILE + tile * TILE, TILE)
                change = factor * waiting[field, h, own, :]
                two[field, x, at, :] = two[field, x, at, :] + change
        return carry

    lax.fori_loop(0, 2 * near, finish, 0, unroll=4)
    inner = pl.ds(TILE, rows)
    for message, left in ((next_a, odd), (next_b, 1 - odd)):
        for field in range(2):
            for i in range(REACH):
                x = left * (deep - near - REACH) + (1 - left) * (deep + cells + near) + i
                two[field, x, inner, :] = message[near + field * REACH + i]

    now, other = two, one
    for step in range(1, steps):
        edge = range(REACH * (step + 1), deep, REACH)
        groups = list(edge) + [x + cells + deep - REACH * (step + 1) for x in edge]
        for pair in paired(groups):
            advance(now, other, courant, drops, band, step, pair, None, False, deep)
        own = range(deep, deep + cells, REACH)
        groups = [own[0], own[-1]] if step == 1 else own
        last = finals if step == steps - 1 else None
        for pair in paired(groups):
            advance(now, other, courant, drops, band, step, pair, grad, False, deep, last)
            if last is not None:
                done = pl.ds(pair[0] - deep, len(pair) * REACH)
                bring(finals.at[0, done], final_w.at[0, done])
                bring(finals.at[1, done], final_j.at[0, done])
        now, other = other, now

    def place(x, carry):
        for tile in range(tiles):
            at = pl.ds(tile * TILE, TILE)
            parts[start_block + tile, x] = image[x, at, :] * grad[x, at, :]
        return carry

    lax.fori_loop(0, cells, place, 0, unroll=4)
    for copy in copies:
        copy.wait()


def early_steps(steps, count, from_a, from_b, courant, drops, band, one, two, grad, groups):
    cells, rows, depth = grad.shape
    waiting = pltpu.VMEM((2, 2 * (steps - 2) * REACH, rows, depth), jnp.float32)
    parts = pltpu.VMEM((groups, cells, TILE, depth), jnp.float32)
    smem = pl.BlockSpec(memory_space=pltpu.SMEM)
    vmem = pl.BlockSpec(memory_space=pltpu.VMEM)
    same = [pltpu.VMEM(array.shape, array.dtype) for array in (one, two, grad)]

    def kernel(*refs):
        early_kernel(steps, *refs)

    return pl.pallas_call(
        kernel,
        out_shape=(*same, waiting, parts),
        in_specs=[smem, any_space(), any_space()] + [vmem] * 6,
        out_specs=(vmem,) * 5,
        input_output_aliases={6: 0, 7: 1, 8: 2},
        scratch_shapes=[pltpu.SemaphoreType.DMA((8,))],
        compiler_params=pltpu.CompilerParams(vmem_limit_bytes=8 << 20),
        cost_estimate=pl.CostEstimate(flops=20 << 20, bytes_accessed=4 << 20, transcendentals=0),
    )(count, from_a, from_b, courant, drops, band, one, two, grad)


def late_steps(steps, start, count, next_a, next_b, drops, band, image, waiting, one, two, courant, grad, parts):
    smem = pl.BlockSpec(memory_space=pltpu.SMEM)
    vmem = pl.BlockSpec(memory_space=pltpu.VMEM)
    final = jax.ShapeDtypeStruct((1, *image.shape), jnp.float32)
    same = [pltpu.VMEM(array.shape, array.dtype) for array in (one, two, courant, grad, parts)]

    def kernel(*refs):
        late_kernel(steps, *refs)

    results = pl.pallas_call(
        kernel,
        out_shape=(final, final, *same),
        in_specs=[smem] * 2 + [vmem] * 11,
        out_specs=(any_space(), any_space()) + (vmem,) * 5,
        input_output_aliases={8: 2, 9: 3, 10: 4, 11: 5, 12: 6},
        scratch_shapes=[
            pltpu.VMEM((2, *image.shape), jnp.float32),
            pltpu.SemaphoreType.DMA((2 * image.shape[0] // REACH,)),
        ],
        compiler_params=pltpu.CompilerParams(vmem_limit_bytes=8 << 20),
        cost_estimate=pl.CostEstimate(flops=40 << 20, bytes_accessed=6 << 20, transcendentals=0),
    )(start, count, next_a, next_b, drops, band, image, waiting, one, two, courant, grad, parts)
    return results[0], results[1], results[6]


def per_device(
    velocity,
    aperture_start,
    aperture_count,
    wave_prev,
    wave_now,
    adjoint_prev,
    adjoint_now,
    source_cells,
    wavelet,
    receiver_cells,
    trace,
):
    steps = wavelet.shape[1]
    deep = steps * REACH
    fields = (wave_now, adjoint_now, wave_prev, adjoint_prev)

    to_a, to_b = pack(fields, deep - REACH)
    from_a = swap_pairs(to_a, "slab", 0)
    from_b = swap_pairs(to_b, "slab", 1)
    speeds = lax.all_gather(velocity, "shot")

    cells_w, cells_j = (jnp.transpose(places, (2, 0, 1)) for places in (source_cells, receiver_cells))
    small = (cells_w, cells_j, wavelet, trace)
    to_a, to_b, drops, band, one, two, courant, image, grad = opening(
        aperture_start, aperture_count, small, fields, speeds, steps
    )
    next_a = swap_pairs(to_a, "slab", 0)
    next_b = swap_pairs(to_b, "slab", 1)
    one, two, grad, waiting, parts = early_steps(
        steps, aperture_count, from_a, from_b, courant, drops, band, one, two, grad, lax.axis_size("shot")
    )
    final_w, final_j, parts = late_steps(
        steps,
        aperture_start,
        aperture_count,
        next_a,
        next_b,
        drops,
        band,
        image,
        waiting,
        one,
        two,
        courant,
        grad,
        parts,
    )
    shares = lax.all_to_all(parts, "shot", 0, 0, tiled=True)
    return final_w, final_j, jnp.sum(shares, axis=0)


def solution(mesh):
    return jax.shard_map(
        per_device,
        mesh=mesh,
        in_specs=(
            P("slab", "shot", None),
            P("shot"),
            P("shot"),
            P("shot", "slab", None, None),
            P("shot", "slab", None, None),
            P("shot", "slab", None, None),
            P("shot", "slab", None, None),
            P("shot", None, None),
            P("shot", None, None),
            P("shot", None, None),
            P("shot", None, None),
        ),
        out_specs=(
            P("shot", "slab", None, None),
            P("shot", "slab", None, None),
            P("slab", "shot", None),
        ),
        check_vma=False,
    )
```

```python
import jax
import jax.numpy as jnp
from jax import lax
from jax.experimental import pallas as pl
from jax.experimental.pallas import tpu as pltpu
from jax.sharding import PartitionSpec as P


SCALE = 5040.0
scaled_weights = (-14350.0, 8064.0, -1008.0, 128.0, -9.0)
time_step = 0.09
REACH = 4
TILE = 8


def swap_pairs(block, axis, first):
    count = lax.axis_size(axis)
    route = []
    for i in range(first, count - 1, 2):
        route += [(i, i + 1), (i + 1, i)]
    return lax.ppermute(block, axis, route)


def any_space():
    return pl.BlockSpec(memory_space=pl.ANY)


def in_hbm(array):
    return pltpu.with_memory_space_constraint(array, pltpu.HBM)


def packing_kernel(now_w, now_j, prev_w, prev_j, to_a, to_b, drops, band, one, two, sems):
    cells = now_w.shape[1]
    deep_now = (to_a.shape[0] // 2 + REACH) // 2
    deep_prev = deep_now - REACH
    odd = lax.axis_index("slab") % 2
    copies, bring = bringing(sems)
    for out, side in ((to_a, 1 - odd), (to_b, odd)):
        at = 0
        for field, deep in ((now_w, deep_now), (now_j, deep_now), (prev_w, deep_prev), (prev_j, deep_prev)):
            bring(field.at[0, pl.ds(side * (cells - deep), deep)], out.at[pl.ds(at, deep)])
            at += deep
    steps, depth = drops.shape[0], drops.shape[4]
    zero_tile = jnp.zeros((TILE, depth), jnp.float32)

    def clear(x, carry):
        for field in range(2):
            for step in range(steps):
                drops[step, field, x] = zero_tile
            for buffer in (one, two):
                buffer[field, x, pl.ds(0, TILE), :] = zero_tile
                buffer[field, x, pl.ds(buffer.shape[2] - TILE, TILE), :] = zero_tile
        return carry

    lax.fori_loop(0, drops.shape[2], clear, 0)
    away = lax.broadcasted_iota(jnp.int32, (depth, depth), 0) - lax.broadcasted_iota(jnp.int32, (depth, depth), 1)
    matrix = jnp.zeros((depth, depth), jnp.float32)
    for k in range(1, REACH + 1):
        matrix = jnp.where((away == k) | (away == -k), scaled_weights[k], matrix)
    band[pl.ds(0, depth), :] = matrix.astype(jnp.bfloat16)
    band[pl.ds(depth, depth), :] = matrix.astype(jnp.bfloat16)
    for copy in copies:
        copy.wait()


def pack(fields, steps):
    cells, rows, depth = fields[0].shape[1:]
    deep = steps * REACH
    wide = cells + 2 * deep
    message = pltpu.VMEM((4 * (deep - REACH) - 2 * REACH, rows, depth), jnp.float32)
    drops = pltpu.VMEM((steps, 2, wide, TILE, depth), jnp.float32)
    band = pltpu.VMEM((2 * depth, depth), jnp.bfloat16)
    buffer = pltpu.VMEM((2, wide, rows + 2 * TILE, depth), jnp.float32)
    vmem = pl.BlockSpec(memory_space=pltpu.VMEM)
    return pl.pallas_call(
        packing_kernel,
        out_shape=(message, message, drops, band, buffer, buffer),
        in_specs=[pl.BlockSpec(memory_space=pltpu.HBM)] * 4,
        out_specs=(vmem,) * 6,
        scratch_shapes=[pltpu.SemaphoreType.DMA((8,))],
        compiler_params=pltpu.CompilerParams(vmem_limit_bytes=8 << 20),
        cost_estimate=pl.CostEstimate(flops=0, bytes_accessed=4 << 20, transcendentals=0),
    )(*map(in_hbm, fields))


def bringing(sems):
    copies = []

    def bring(source, target):
        copy = pltpu.make_async_copy(source, target, sems.at[len(copies)])
        copy.start()
        copies.append(copy)

    return copies, bring


def inject(drops, slab_first, steps, field, places, amps):
    row = lax.broadcasted_iota(jnp.int32, drops.shape[3:], 0)
    col = lax.broadcasted_iota(jnp.int32, drops.shape[3:], 1)

    def one_cell(s, carry):
        x = places[0, 0, s] - slab_first

        @pl.when((x >= 0) & (x < drops.shape[2]))
        def _():
            here = (row == places[1, 0, s]) & (col == places[2, 0, s])
            for step in steps:
                drops[step, field, x] = drops[step, field, x] + jnp.where(here, amps[0, step, s], 0.0)

        return carry

    lax.fori_loop(0, places.shape[2], one_cell, 0)


def opening_kernel(
    start,
    count,
    cells_w_in,
    cells_j_in,
    amps_w_in,
    amps_j_in,
    sent_a,
    sent_b,
    speeds,
    band,
    drops_in,
    one_in,
    two_in,
    to_a,
    to_b,
    drops,
    one,
    two,
    courant,
    image,
    grad,
    cells_w,
    cells_j,
    amps_w,
    amps_j,
    sems,
):
    cells, rows, depth = image.shape
    tiles = rows // TILE
    steps = drops.shape[0]
    deep = steps * REACH
    near = deep - 2 * REACH
    held = near + REACH
    half = cells // 2
    odd = lax.axis_index("slab") % 2
    start_block = start[0]
    live = count[0]
    copies, bring = bringing(sems)
    for source, target in ((cells_w_in, cells_w), (cells_j_in, cells_j), (amps_w_in, amps_w), (amps_j_in, amps_j)):
        bring(source, target)
    sides = ((sent_a, to_a, 1 - odd), (sent_b, to_b, odd))
    inner = pl.ds(TILE, rows)
    for sent, _, side in sides:
        for field in range(2):
            for layer in range(half):
                x = deep + side * half + layer
                one[field, x, inner, :] = sent[field * held + layer + side * (held - half)]
                two[field, x, inner, :] = sent[2 * held + field * near + layer + side * (near - half)]

    def factors(x, carry):
        for tile in range(tiles):
            alive = jnp.where(tile < live, time_step * time_step / SCALE, 0.0)
            speed = speeds[start_block + tile, x]
            at = pl.ds(tile * TILE, TILE)
            courant[deep + x, at, :] = alive * (speed * speed)
            image[x, at, :] = (2.0 * time_step * time_step / SCALE) * speed
        return carry

    lax.fori_loop(0, cells, factors, 0, unroll=4)
    for _, out, side in sides:
        for layer in range(near):
            for tile in range(tiles):
                speed = speeds[start_block + tile, side * (cells - near) + layer]
                out[layer, pl.ds(tile * TILE, TILE), :] = speed
    clear_dead(one, two, live, deep, deep + cells)
    for copy in copies:
        copy.wait()
    slab_first = lax.axis_index("slab") * cells - deep
    inject(drops, slab_first, range(1), 0, cells_w, amps_w)
    inject(drops, slab_first, range(1), 1, cells_j, amps_j)
    for groups in paired(range(deep + REACH, deep + cells - REACH, REACH)):
        advance(one, two, courant, drops, band, 0, groups, grad, True, deep)
    for _, out, side in sides:
        for field in range(2):
            for i in range(REACH):
                x = deep + REACH + (1 - side) * (cells - 3 * REACH) + i
                out[near + field * REACH + i] = two[field, x, inner, :]


def clear_dead(one, two, live, first, last):
    tiles = one.shape[2] // TILE - 2
    for tile in range(1, tiles):

        @pl.when(tile >= live)
        def _():
            def clear(x, carry):
                for buffer in (one, two):
                    for field in range(2):
                        buffer[field, x, pl.ds(TILE + tile * TILE, TILE), :] = jnp.zeros(
                            (TILE, one.shape[3]), jnp.float32
                        )
                return carry

            lax.fori_loop(first, last, clear, 0)


def opening(start, count, small, sent_a, sent_b, speeds, band, drops, one, two):
    cells, depth = speeds.shape[1], speeds.shape[3]
    rows = sent_a.shape[1]
    deep = drops.shape[0] * REACH
    message = pltpu.VMEM((deep, rows, depth), jnp.float32)
    courant = pltpu.VMEM((cells + 2 * deep, rows, depth), jnp.float32)
    layers = pltpu.VMEM((cells, rows, depth), jnp.float32)
    same = [pltpu.VMEM(array.shape, array.dtype) for array in (drops, one, two)]
    vmem = pl.BlockSpec(memory_space=pltpu.VMEM)
    return pl.pallas_call(
        opening_kernel,
        out_shape=(message, message, *same, courant, layers, layers),
        in_specs=[pl.BlockSpec(memory_space=pltpu.SMEM)] * 2
        + [pl.BlockSpec(memory_space=pltpu.HBM)] * 4
        + [vmem] * 7,
        out_specs=(vmem,) * 8,
        input_output_aliases={10: 2, 11: 3, 12: 4},
        scratch_shapes=[pltpu.SMEM(array.shape, array.dtype) for array in small] + [pltpu.SemaphoreType.DMA((4,))],
        compiler_params=pltpu.CompilerParams(vmem_limit_bytes=8 << 20),
        cost_estimate=pl.CostEstimate(flops=4 << 20, bytes_accessed=4 << 20, transcendentals=0),
    )(start, count, *map(in_hbm, small), sent_a, sent_b, speeds, band, drops, one, two)


def along_z(now, band, field, x):
    rows, depth = now.shape[2] - 2 * TILE, now.shape[3]
    cells = now[field, pl.ds(x, REACH), pl.ds(TILE, rows), :].reshape(REACH * rows, depth)
    high = cells.astype(jnp.bfloat16)
    low = (cells - high.astype(jnp.float32)).astype(jnp.bfloat16)
    return jnp.dot(jnp.concatenate([high, low], axis=1), band[...], preferred_element_type=jnp.float32)


def each_tile(now, band, groups, visit):
    rows = now.shape[2] - 2 * TILE
    spreads = [[along_z(now, band, field, x_first) for field in range(2)] for x_first in groups]
    for g, x_first in enumerate(groups):
        for tile in range(rows // TILE):
            at = TILE + tile * TILE
            pairs = []
            for field in range(2):
                line = [now[field, x_first + i, pl.ds(at, TILE), :] for i in range(-REACH, 2 * REACH)]
                for i in range(REACH):
                    center = line[REACH + i]
                    lap = (3.0 * scaled_weights[0]) * center
                    for k in range(1, REACH + 1):
                        near = line[REACH + i + k] + line[REACH + i - k]
                        near = near + now[field, x_first + i, pl.ds(at + k, TILE), :]
                        near = near + now[field, x_first + i, pl.ds(at - k, TILE), :]
                        lap = lap + scaled_weights[k] * near
                    row = i * rows + tile * TILE
                    pairs.append((center, lap + spreads[g][field][row : row + TILE]))
            for i in range(REACH):
                visit(g, tile, i, (pairs[i], pairs[REACH + i]))


def advance(now, other, courant, drops, band, step, groups, grad, fresh, deep, finals=None):
    def visit(g, tile, i, pair):
        x = groups[g] + i
        own = pl.ds(tile * TILE, TILE)
        padded = pl.ds(TILE + tile * TILE, TILE)
        factor = courant[x, own, :]
        for field, (center, lap) in enumerate(pair):
            ahead = 2.0 * center - other[field, x, padded, :] + factor * lap
            if tile == 0:
                ahead = ahead + drops[step, field, x]
            if finals is None:
                other[field, x, padded, :] = ahead
            else:
                finals[field, x - deep, own, :] = ahead
        if grad is not None:
            term = pair[1][0] * pair[0][1]
            grad[x - deep, own, :] = term if fresh else grad[x - deep, own, :] + term

    each_tile(now, band, groups, visit)


def early_kernel(
    steps,
    count,
    cells_w_in,
    cells_j_in,
    amps_w_in,
    amps_j_in,
    from_a,
    from_b,
    courant,
    band,
    drops_in,
    one_in,
    two_in,
    grad_in,
    drops,
    one,
    two,
    grad,
    waiting,
    parts,
    cells_w,
    cells_j,
    amps_w,
    amps_j,
    sems,
):
    cells, rows, depth = grad.shape
    deep = steps * REACH
    near = deep - 2 * REACH
    held = near + REACH
    wide = cells + 2 * deep
    odd = lax.axis_index("slab") % 2

    left_of_a = odd
    copies, bring = bringing(sems)
    for source, target in ((cells_w_in, cells_w), (cells_j_in, cells_j), (amps_w_in, amps_w), (amps_j_in, amps_j)):
        bring(source, target)
    inner = pl.ds(TILE, rows)
    for field in range(2):
        for buffer, on_left in ((from_a, left_of_a), (from_b, 1 - left_of_a)):
            at = on_left * (deep - held) + (1 - on_left) * (deep + cells)
            bring(buffer.at[pl.ds(field * held, held)], one.at[field, pl.ds(at, held), inner])
            at = on_left * (deep - near) + (1 - on_left) * (deep + cells)
            bring(buffer.at[pl.ds(2 * held + field * near, near)], two.at[field, pl.ds(at, near), inner])
    def clear_parts(b, carry):
        parts[b] = jnp.zeros(parts.shape[1:], jnp.float32)
        return carry

    lax.fori_loop(0, parts.shape[0], clear_parts, 0)
    for copy in copies:
        copy.wait()
    slab_first = lax.axis_index("slab") * cells - deep
    inject(drops, slab_first, range(1, steps), 0, cells_w, amps_w)
    inject(drops, slab_first, range(1, steps), 1, cells_j, amps_j)
    clear_dead(one, two, count[0], 0, deep)
    clear_dead(one, two, count[0], deep + cells, wide)

    def outside(c, carry):
        groups = [deep - near + c * (near + cells) + i for i in range(0, near, REACH)]

        def visit(g, tile, i, pair):
            x = groups[g] + i
            padded = pl.ds(TILE + tile * TILE, TILE)
            for field, (center, lap) in enumerate(pair):
                waiting[field, c * near + g * REACH + i, pl.ds(tile * TILE, TILE), :] = lap
                ahead = 2.0 * center - two[field, x, padded, :]
                two[field, x, padded, :] = ahead + drops[0, field, x] if tile == 0 else ahead

        each_tile(one, band, groups, visit)
        return carry

    advance(one, two, courant, drops, band, 0, [deep, deep + cells - REACH], grad, True, deep)
    lax.fori_loop(0, 2, outside, 0)
    for groups in paired(range(deep + REACH, deep + cells - REACH, REACH)):
        advance(two, one, courant, drops, band, 1, groups, grad, False, deep)


def paired(starts):
    starts = list(starts)
    return [starts[i : i + 2] for i in range(0, len(starts), 2)]


def late_kernel(
    steps,
    start,
    count,
    next_a,
    next_b,
    drops,
    band,
    image,
    waiting,
    one_in,
    two_in,
    courant_in,
    grad_in,
    parts_in,
    final_w,
    final_j,
    one,
    two,
    courant,
    grad,
    parts,
    finals,
    sems,
):
    cells, rows, depth = image.shape
    deep = steps * REACH
    near = deep - 2 * REACH
    tiles = rows // TILE
    odd = lax.axis_index("slab") % 2
    start_block = start[0]
    live = count[0]

    copies, bring = bringing(sems)

    def finish(h, carry):
        right = h >= near
        layer = jnp.where(right, h - near, h)
        x = jnp.where(right, deep + cells, deep - near) + layer
        use_a = jnp.where(right, 1 - odd, odd) == 1
        for tile in range(tiles):
            alive = jnp.where(tile < live, time_step * time_step / SCALE, 0.0)
            own = pl.ds(tile * TILE, TILE)
            speed = jnp.where(use_a, next_a[layer, own, :], next_b[layer, own, :])
            factor = alive * (speed * speed)
            courant[x, own, :] = factor
            for field in range(2):
                at = pl.ds(TILE + tile * TILE, TILE)
                change = factor * waiting[field, h, own, :]
                two[field, x, at, :] = two[field, x, at, :] + change
        return carry

    lax.fori_loop(0, 2 * near, finish, 0, unroll=4)
    inner = pl.ds(TILE, rows)
    for message, left in ((next_a, odd), (next_b, 1 - odd)):
        for field in range(2):
            for i in range(REACH):
                x = left * (deep - near - REACH) + (1 - left) * (deep + cells + near) + i
                two[field, x, inner, :] = message[near + field * REACH + i]

    now, other = two, one
    for step in range(1, steps):
        edge = range(REACH * (step + 1), deep, REACH)
        groups = list(edge) + [x + cells + deep - REACH * (step + 1) for x in edge]
        for pair in paired(groups):
            advance(now, other, courant, drops, band, step, pair, None, False, deep)
        own = range(deep, deep + cells, REACH)
        groups = [own[0], own[-1]] if step == 1 else own
        last = finals if step == steps - 1 else None
        for pair in paired(groups):
            advance(now, other, courant, drops, band, step, pair, grad, False, deep, last)
            if last is not None:
                done = pl.ds(pair[0] - deep, len(pair) * REACH)
                bring(finals.at[0, done], final_w.at[0, done])
                bring(finals.at[1, done], final_j.at[0, done])
        now, other = other, now

    def place(x, carry):
        for tile in range(tiles):
            at = pl.ds(tile * TILE, TILE)
            parts[start_block + tile, x] = image[x, at, :] * grad[x, at, :]
        return carry

    lax.fori_loop(0, cells, place, 0, unroll=4)
    for copy in copies:
        copy.wait()


def early_steps(count, small, from_a, from_b, courant, band, drops, one, two, grad, groups):
    cells, rows, depth = grad.shape
    steps = drops.shape[0]
    waiting = pltpu.VMEM((2, 2 * (steps - 2) * REACH, rows, depth), jnp.float32)
    parts = pltpu.VMEM((groups, cells, TILE, depth), jnp.float32)
    vmem = pl.BlockSpec(memory_space=pltpu.VMEM)
    same = [pltpu.VMEM(array.shape, array.dtype) for array in (drops, one, two, grad)]

    def kernel(*refs):
        early_kernel(steps, *refs)

    return pl.pallas_call(
        kernel,
        out_shape=(*same, waiting, parts),
        in_specs=[pl.BlockSpec(memory_space=pltpu.SMEM)]
        + [pl.BlockSpec(memory_space=pltpu.HBM)] * 4
        + [any_space()] * 2
        + [vmem] * 6,
        out_specs=(vmem,) * 6,
        input_output_aliases={9: 0, 10: 1, 11: 2, 12: 3},
        scratch_shapes=[pltpu.SMEM(array.shape, array.dtype) for array in small] + [pltpu.SemaphoreType.DMA((12,))],
        compiler_params=pltpu.CompilerParams(vmem_limit_bytes=8 << 20),
        cost_estimate=pl.CostEstimate(flops=20 << 20, bytes_accessed=4 << 20, transcendentals=0),
    )(count, *map(in_hbm, small), from_a, from_b, courant, band, drops, one, two, grad)


def late_steps(steps, start, count, next_a, next_b, drops, band, image, waiting, one, two, courant, grad, parts):
    smem = pl.BlockSpec(memory_space=pltpu.SMEM)
    vmem = pl.BlockSpec(memory_space=pltpu.VMEM)
    final = jax.ShapeDtypeStruct((1, *image.shape), jnp.float32)
    same = [pltpu.VMEM(array.shape, array.dtype) for array in (one, two, courant, grad, parts)]

    def kernel(*refs):
        late_kernel(steps, *refs)

    results = pl.pallas_call(
        kernel,
        out_shape=(final, final, *same),
        in_specs=[smem] * 2 + [vmem] * 11,
        out_specs=(any_space(), any_space()) + (vmem,) * 5,
        input_output_aliases={8: 2, 9: 3, 10: 4, 11: 5, 12: 6},
        scratch_shapes=[
            pltpu.VMEM((2, *image.shape), jnp.float32),
            pltpu.SemaphoreType.DMA((2 * image.shape[0] // REACH,)),
        ],
        compiler_params=pltpu.CompilerParams(vmem_limit_bytes=8 << 20),
        cost_estimate=pl.CostEstimate(flops=40 << 20, bytes_accessed=6 << 20, transcendentals=0),
    )(start, count, next_a, next_b, drops, band, image, waiting, one, two, courant, grad, parts)
    return results[0], results[1], results[6]


def per_device(
    velocity,
    aperture_start,
    aperture_count,
    wave_prev,
    wave_now,
    adjoint_prev,
    adjoint_now,
    source_cells,
    wavelet,
    receiver_cells,
    trace,
):
    steps = wavelet.shape[1]
    fields = (wave_now, adjoint_now, wave_prev, adjoint_prev)

    sent_a, sent_b, drops, band, one, two = pack(fields, steps)
    from_a = swap_pairs(sent_a, "slab", 0)
    from_b = swap_pairs(sent_b, "slab", 1)
    speeds = lax.all_gather(velocity, "shot")

    cells_w, cells_j = (jnp.transpose(places, (2, 0, 1)) for places in (source_cells, receiver_cells))
    small = (cells_w, cells_j, wavelet, trace)
    to_a, to_b, drops, one, two, courant, image, grad = opening(
        aperture_start, aperture_count, small, sent_a, sent_b, speeds, band, drops, one, two
    )
    next_a = swap_pairs(to_a, "slab", 0)
    next_b = swap_pairs(to_b, "slab", 1)
    drops, one, two, grad, waiting, parts = early_steps(
        aperture_count, small, from_a, from_b, courant, band, drops, one, two, grad, lax.axis_size("shot")
    )
    final_w, final_j, parts = late_steps(
        steps,
        aperture_start,
        aperture_count,
        next_a,
        next_b,
        drops,
        band,
        image,
        waiting,
        one,
        two,
        courant,
        grad,
        parts,
    )
    shares = lax.all_to_all(parts, "shot", 0, 0, tiled=True)
    return final_w, final_j, jnp.sum(shares, axis=0)


def solution(mesh):
    return jax.shard_map(
        per_device,
        mesh=mesh,
        in_specs=(
            P("slab", "shot", None),
            P("shot"),
            P("shot"),
            P("shot", "slab", None, None),
            P("shot", "slab", None, None),
            P("shot", "slab", None, None),
            P("shot", "slab", None, None),
            P("shot", None, None),
            P("shot", None, None),
            P("shot", None, None),
            P("shot", None, None),
        ),
        out_specs=(
            P("shot", "slab", None, None),
            P("shot", "slab", None, None),
            P("slab", "shot", None),
        ),
        check_vma=False,
    )
```

```python
import jax
import jax.numpy as jnp
from jax import lax
from jax.experimental import pallas as pl
from jax.experimental.pallas import tpu as pltpu
from jax.sharding import PartitionSpec as P


SCALE = 5040.0
scaled_weights = (-14350.0, 8064.0, -1008.0, 128.0, -9.0)
time_step = 0.09
REACH = 4
TILE = 8


def swap_pairs(block, axis, first):
    count = lax.axis_size(axis)
    route = []
    for i in range(first, count - 1, 2):
        route += [(i, i + 1), (i + 1, i)]
    return lax.ppermute(block, axis, route)


def any_space():
    return pl.BlockSpec(memory_space=pl.ANY)


def in_hbm(array):
    return pltpu.with_memory_space_constraint(array, pltpu.HBM)


def packing_kernel(now_w, now_j, prev_w, prev_j, to_a, to_b, drops, band, one, two, sems):
    cells = now_w.shape[1]
    deep_now = (to_a.shape[0] // 2 + REACH) // 2
    deep_prev = deep_now - REACH
    odd = lax.axis_index("slab") % 2
    copies, bring = bringing(sems)
    for out, side in ((to_a, 1 - odd), (to_b, odd)):
        at = 0
        for field, deep in ((now_w, deep_now), (now_j, deep_now), (prev_w, deep_prev), (prev_j, deep_prev)):
            bring(field.at[0, pl.ds(side * (cells - deep), deep)], out.at[pl.ds(at, deep)])
            at += deep
    steps, depth = drops.shape[0], drops.shape[4]
    zero_tile = jnp.zeros((TILE, depth), jnp.float32)

    def clear(x, carry):
        for field in range(2):
            for step in range(steps):
                drops[step, field, x] = zero_tile
            for buffer in (one, two):
                buffer[field, x, pl.ds(0, TILE), :] = zero_tile
                buffer[field, x, pl.ds(buffer.shape[2] - TILE, TILE), :] = zero_tile
        return carry

    lax.fori_loop(0, drops.shape[2], clear, 0)
    away = lax.broadcasted_iota(jnp.int32, (depth, depth), 0) - lax.broadcasted_iota(jnp.int32, (depth, depth), 1)
    matrix = jnp.zeros((depth, depth), jnp.float32)
    for k in range(1, REACH + 1):
        matrix = jnp.where((away == k) | (away == -k), scaled_weights[k], matrix)
    band[pl.ds(0, depth), :] = matrix.astype(jnp.bfloat16)
    band[pl.ds(depth, depth), :] = matrix.astype(jnp.bfloat16)
    for copy in copies:
        copy.wait()


def pack(fields, steps):
    cells, rows, depth = fields[0].shape[1:]
    deep = steps * REACH
    wide = cells + 2 * deep
    message = pltpu.VMEM((4 * (deep - REACH) - 2 * REACH, rows, depth), jnp.float32)
    drops = pltpu.VMEM((steps, 2, wide, TILE, depth), jnp.float32)
    band = pltpu.VMEM((2 * depth, depth), jnp.bfloat16)
    buffer = pltpu.VMEM((2, wide, rows + 2 * TILE, depth), jnp.float32)
    vmem = pl.BlockSpec(memory_space=pltpu.VMEM)
    return pl.pallas_call(
        packing_kernel,
        out_shape=(message, message, drops, band, buffer, buffer),
        in_specs=[pl.BlockSpec(memory_space=pltpu.HBM)] * 4,
        out_specs=(vmem,) * 6,
        scratch_shapes=[pltpu.SemaphoreType.DMA((8,))],
        compiler_params=pltpu.CompilerParams(vmem_limit_bytes=8 << 20),
        cost_estimate=pl.CostEstimate(flops=0, bytes_accessed=4 << 20, transcendentals=0),
    )(*map(in_hbm, fields))


def bringing(sems):
    copies = []

    def bring(source, target):
        copy = pltpu.make_async_copy(source, target, sems.at[len(copies)])
        copy.start()
        copies.append(copy)

    return copies, bring


def inject(drops, slab_first, field, places, amps):
    row = lax.broadcasted_iota(jnp.int32, drops.shape[3:], 0)
    col = lax.broadcasted_iota(jnp.int32, drops.shape[3:], 1)

    def one_cell(s, carry):
        x = places[0, 0, s] - slab_first
        inside = (x >= 0) & (x < drops.shape[2])
        x = jnp.clip(x, 0, drops.shape[2] - 1)
        here = (row == places[1, 0, s]) & (col == places[2, 0, s])
        tiles = [drops[step, field, x] for step in range(drops.shape[0])]
        for step, tile in enumerate(tiles):
            amp = jnp.where(inside, amps[0, step, s], 0.0)
            drops[step, field, x] = tile + jnp.where(here, amp, 0.0)
        return carry

    lax.fori_loop(0, places.shape[2], one_cell, 0, unroll=4)


def opening_kernel(
    start,
    count,
    sent_a,
    sent_b,
    speeds,
    band,
    one_in,
    two_in,
    to_a,
    to_b,
    one,
    two,
    courant,
    image,
    grad,
):
    cells, rows, depth = image.shape
    tiles = rows // TILE
    deep = to_a.shape[0]
    near = deep - 2 * REACH
    held = near + REACH
    half = cells // 2
    odd = lax.axis_index("slab") % 2
    start_block = start[0]
    live = count[0]
    sides = ((sent_a, to_a, 1 - odd), (sent_b, to_b, odd))
    inner = pl.ds(TILE, rows)
    for sent, _, side in sides:
        for field in range(2):
            for layer in range(half):
                x = deep + side * half + layer
                one[field, x, inner, :] = sent[field * held + layer + side * (held - half)]
                two[field, x, inner, :] = sent[2 * held + field * near + layer + side * (near - half)]

    def factors(x, carry):
        for tile in range(tiles):
            alive = jnp.where(tile < live, time_step * time_step / SCALE, 0.0)
            speed = speeds[start_block + tile, x]
            at = pl.ds(tile * TILE, TILE)
            courant[deep + x, at, :] = alive * (speed * speed)
            image[x, at, :] = (2.0 * time_step * time_step / SCALE) * speed
        return carry

    lax.fori_loop(0, cells, factors, 0, unroll=4)
    for _, out, side in sides:
        for layer in range(near):
            for tile in range(tiles):
                speed = speeds[start_block + tile, side * (cells - near) + layer]
                out[layer, pl.ds(tile * TILE, TILE), :] = speed
    clear_dead(one, two, live, deep, deep + cells)
    for groups in paired(range(deep + REACH, deep + cells - REACH, REACH)):
        advance(one, two, courant, None, band, 0, groups, grad, True, deep)
    for _, out, side in sides:
        for field in range(2):
            for i in range(REACH):
                x = deep + REACH + (1 - side) * (cells - 3 * REACH) + i
                out[near + field * REACH + i] = two[field, x, inner, :]


def clear_dead(one, two, live, first, last):
    tiles = one.shape[2] // TILE - 2
    for tile in range(1, tiles):

        @pl.when(tile >= live)
        def _():
            def clear(x, carry):
                for buffer in (one, two):
                    for field in range(2):
                        buffer[field, x, pl.ds(TILE + tile * TILE, TILE), :] = jnp.zeros(
                            (TILE, one.shape[3]), jnp.float32
                        )
                return carry

            lax.fori_loop(first, last, clear, 0)


def opening(start, count, sent_a, sent_b, speeds, band, one, two):
    cells, depth = speeds.shape[1], speeds.shape[3]
    rows = sent_a.shape[1]
    wide = one.shape[1]
    message = pltpu.VMEM(((wide - cells) // 2, rows, depth), jnp.float32)
    courant = pltpu.VMEM((wide, rows, depth), jnp.float32)
    layers = pltpu.VMEM((cells, rows, depth), jnp.float32)
    same = [pltpu.VMEM(array.shape, array.dtype) for array in (one, two)]
    vmem = pl.BlockSpec(memory_space=pltpu.VMEM)
    return pl.pallas_call(
        opening_kernel,
        out_shape=(message, message, *same, courant, layers, layers),
        in_specs=[pl.BlockSpec(memory_space=pltpu.SMEM)] * 2 + [vmem] * 6,
        out_specs=(vmem,) * 7,
        input_output_aliases={6: 2, 7: 3},
        compiler_params=pltpu.CompilerParams(vmem_limit_bytes=8 << 20),
        cost_estimate=pl.CostEstimate(flops=4 << 20, bytes_accessed=4 << 20, transcendentals=0),
    )(start, count, sent_a, sent_b, speeds, band, one, two)


def along_z(now, band, field, x):
    rows, depth = now.shape[2] - 2 * TILE, now.shape[3]
    cells = now[field, pl.ds(x, REACH), pl.ds(TILE, rows), :].reshape(REACH * rows, depth)
    high = cells.astype(jnp.bfloat16)
    low = (cells - high.astype(jnp.float32)).astype(jnp.bfloat16)
    return jnp.dot(jnp.concatenate([high, low], axis=1), band[...], preferred_element_type=jnp.float32)


def each_tile(now, band, groups, visit):
    rows = now.shape[2] - 2 * TILE
    spreads = [[along_z(now, band, field, x_first) for field in range(2)] for x_first in groups]
    for g, x_first in enumerate(groups):
        for tile in range(rows // TILE):
            at = TILE + tile * TILE
            pairs = []
            for field in range(2):
                line = [now[field, x_first + i, pl.ds(at, TILE), :] for i in range(-REACH, 2 * REACH)]
                for i in range(REACH):
                    center = line[REACH + i]
                    lap = (3.0 * scaled_weights[0]) * center
                    for k in range(1, REACH + 1):
                        near = line[REACH + i + k] + line[REACH + i - k]
                        near = near + now[field, x_first + i, pl.ds(at + k, TILE), :]
                        near = near + now[field, x_first + i, pl.ds(at - k, TILE), :]
                        lap = lap + scaled_weights[k] * near
                    row = i * rows + tile * TILE
                    pairs.append((center, lap + spreads[g][field][row : row + TILE]))
            for i in range(REACH):
                visit(g, tile, i, (pairs[i], pairs[REACH + i]))


def advance(now, other, courant, drops, band, step, groups, grad, fresh, deep, finals=None):
    def visit(g, tile, i, pair):
        x = groups[g] + i
        own = pl.ds(tile * TILE, TILE)
        padded = pl.ds(TILE + tile * TILE, TILE)
        factor = courant[x, own, :]
        for field, (center, lap) in enumerate(pair):
            ahead = 2.0 * center - other[field, x, padded, :] + factor * lap
            if tile == 0 and drops is not None:
                ahead = ahead + drops[step, field, x]
            if finals is None:
                other[field, x, padded, :] = ahead
            else:
                finals[field, x - deep, own, :] = ahead
        if grad is not None:
            term = pair[1][0] * pair[0][1]
            grad[x - deep, own, :] = term if fresh else grad[x - deep, own, :] + term

    each_tile(now, band, groups, visit)


def add_drops(buffer, drops, layers):
    for field in range(2):
        for x in layers:
            tile = buffer[field, x, pl.ds(TILE, TILE), :]
            buffer[field, x, pl.ds(TILE, TILE), :] = tile + drops[0, field, x]


def early_kernel(
    steps,
    count,
    cells_w_in,
    cells_j_in,
    amps_w_in,
    amps_j_in,
    from_a,
    from_b,
    courant,
    band,
    drops_in,
    one_in,
    two_in,
    grad_in,
    drops,
    one,
    two,
    grad,
    waiting,
    parts,
    cells_w,
    cells_j,
    amps_w,
    amps_j,
    sems,
):
    cells, rows, depth = grad.shape
    deep = steps * REACH
    near = deep - 2 * REACH
    held = near + REACH
    wide = cells + 2 * deep
    odd = lax.axis_index("slab") % 2

    left_of_a = odd
    copies, bring = bringing(sems)
    for source, target in ((cells_w_in, cells_w), (cells_j_in, cells_j), (amps_w_in, amps_w), (amps_j_in, amps_j)):
        bring(source, target)
    inner = pl.ds(TILE, rows)
    for field in range(2):
        for buffer, on_left in ((from_a, left_of_a), (from_b, 1 - left_of_a)):
            at = on_left * (deep - held) + (1 - on_left) * (deep + cells)
            bring(buffer.at[pl.ds(field * held, held)], one.at[field, pl.ds(at, held), inner])
            at = on_left * (deep - near) + (1 - on_left) * (deep + cells)
            bring(buffer.at[pl.ds(2 * held + field * near, near)], two.at[field, pl.ds(at, near), inner])
    def clear_parts(b, carry):
        parts[b] = jnp.zeros(parts.shape[1:], jnp.float32)
        return carry

    lax.fori_loop(0, parts.shape[0], clear_parts, 0)
    for copy in copies:
        copy.wait()
    slab_first = lax.axis_index("slab") * cells - deep
    inject(drops, slab_first, 0, cells_w, amps_w)
    inject(drops, slab_first, 1, cells_j, amps_j)
    add_drops(two, drops, range(deep + REACH, deep + cells - REACH))
    clear_dead(one, two, count[0], 0, deep)
    clear_dead(one, two, count[0], deep + cells, wide)

    def outside(c, carry):
        groups = [deep - near + c * (near + cells) + i for i in range(0, near, REACH)]

        def visit(g, tile, i, pair):
            x = groups[g] + i
            padded = pl.ds(TILE + tile * TILE, TILE)
            for field, (center, lap) in enumerate(pair):
                waiting[field, c * near + g * REACH + i, pl.ds(tile * TILE, TILE), :] = lap
                ahead = 2.0 * center - two[field, x, padded, :]
                two[field, x, padded, :] = ahead + drops[0, field, x] if tile == 0 else ahead

        each_tile(one, band, groups, visit)
        return carry

    advance(one, two, courant, drops, band, 0, [deep, deep + cells - REACH], grad, True, deep)
    lax.fori_loop(0, 2, outside, 0)
    for groups in paired(range(deep + REACH, deep + cells - REACH, REACH)):
        advance(two, one, courant, drops, band, 1, groups, grad, False, deep)


def paired(starts):
    starts = list(starts)
    return [starts[i : i + 2] for i in range(0, len(starts), 2)]


def late_kernel(
    steps,
    start,
    count,
    next_a,
    next_b,
    drops,
    band,
    image,
    waiting,
    one_in,
    two_in,
    courant_in,
    grad_in,
    parts_in,
    final_w,
    final_j,
    one,
    two,
    courant,
    grad,
    parts,
    finals,
    sems,
):
    cells, rows, depth = image.shape
    deep = steps * REACH
    near = deep - 2 * REACH
    tiles = rows // TILE
    odd = lax.axis_index("slab") % 2
    start_block = start[0]
    live = count[0]

    copies, bring = bringing(sems)

    def finish(h, carry):
        right = h >= near
        layer = jnp.where(right, h - near, h)
        x = jnp.where(right, deep + cells, deep - near) + layer
        use_a = jnp.where(right, 1 - odd, odd) == 1
        for tile in range(tiles):
            alive = jnp.where(tile < live, time_step * time_step / SCALE, 0.0)
            own = pl.ds(tile * TILE, TILE)
            speed = jnp.where(use_a, next_a[layer, own, :], next_b[layer, own, :])
            factor = alive * (speed * speed)
            courant[x, own, :] = factor
            for field in range(2):
                at = pl.ds(TILE + tile * TILE, TILE)
                change = factor * waiting[field, h, own, :]
                two[field, x, at, :] = two[field, x, at, :] + change
        return carry

    lax.fori_loop(0, 2 * near, finish, 0, unroll=4)
    inner = pl.ds(TILE, rows)
    for message, left in ((next_a, odd), (next_b, 1 - odd)):
        for field in range(2):
            for i in range(REACH):
                x = left * (deep - near - REACH) + (1 - left) * (deep + cells + near) + i
                two[field, x, inner, :] = message[near + field * REACH + i]
    add_drops(two, drops, range(deep - near - REACH, deep - near))
    add_drops(two, drops, range(deep + cells + near, deep + cells + near + REACH))

    now, other = two, one
    for step in range(1, steps):
        edge = range(REACH * (step + 1), deep, REACH)
        groups = list(edge) + [x + cells + deep - REACH * (step + 1) for x in edge]
        for pair in paired(groups):
            advance(now, other, courant, drops, band, step, pair, None, False, deep)
        own = range(deep, deep + cells, REACH)
        groups = [own[0], own[-1]] if step == 1 else own
        last = finals if step == steps - 1 else None
        for pair in paired(groups):
            advance(now, other, courant, drops, band, step, pair, grad, False, deep, last)
            if last is not None:
                done = pl.ds(pair[0] - deep, len(pair) * REACH)
                bring(finals.at[0, done], final_w.at[0, done])
                bring(finals.at[1, done], final_j.at[0, done])
        now, other = other, now

    def place(x, carry):
        for tile in range(tiles):
            at = pl.ds(tile * TILE, TILE)
            parts[start_block + tile, x] = image[x, at, :] * grad[x, at, :]
        return carry

    lax.fori_loop(0, cells, place, 0, unroll=4)
    for copy in copies:
        copy.wait()


def early_steps(count, small, from_a, from_b, courant, band, drops, one, two, grad, groups):
    cells, rows, depth = grad.shape
    steps = drops.shape[0]
    waiting = pltpu.VMEM((2, 2 * (steps - 2) * REACH, rows, depth), jnp.float32)
    parts = pltpu.VMEM((groups, cells, TILE, depth), jnp.float32)
    vmem = pl.BlockSpec(memory_space=pltpu.VMEM)
    same = [pltpu.VMEM(array.shape, array.dtype) for array in (drops, one, two, grad)]

    def kernel(*refs):
        early_kernel(steps, *refs)

    return pl.pallas_call(
        kernel,
        out_shape=(*same, waiting, parts),
        in_specs=[pl.BlockSpec(memory_space=pltpu.SMEM)]
        + [pl.BlockSpec(memory_space=pltpu.HBM)] * 4
        + [any_space()] * 2
        + [vmem] * 6,
        out_specs=(vmem,) * 6,
        input_output_aliases={9: 0, 10: 1, 11: 2, 12: 3},
        scratch_shapes=[pltpu.SMEM(array.shape, array.dtype) for array in small] + [pltpu.SemaphoreType.DMA((12,))],
        compiler_params=pltpu.CompilerParams(vmem_limit_bytes=8 << 20),
        cost_estimate=pl.CostEstimate(flops=20 << 20, bytes_accessed=4 << 20, transcendentals=0),
    )(count, *map(in_hbm, small), from_a, from_b, courant, band, drops, one, two, grad)


def late_steps(steps, start, count, next_a, next_b, drops, band, image, waiting, one, two, courant, grad, parts):
    smem = pl.BlockSpec(memory_space=pltpu.SMEM)
    vmem = pl.BlockSpec(memory_space=pltpu.VMEM)
    final = jax.ShapeDtypeStruct((1, *image.shape), jnp.float32)
    same = [pltpu.VMEM(array.shape, array.dtype) for array in (one, two, courant, grad, parts)]

    def kernel(*refs):
        late_kernel(steps, *refs)

    results = pl.pallas_call(
        kernel,
        out_shape=(final, final, *same),
        in_specs=[smem] * 2 + [vmem] * 11,
        out_specs=(any_space(), any_space()) + (vmem,) * 5,
        input_output_aliases={8: 2, 9: 3, 10: 4, 11: 5, 12: 6},
        scratch_shapes=[
            pltpu.VMEM((2, *image.shape), jnp.float32),
            pltpu.SemaphoreType.DMA((2 * image.shape[0] // REACH,)),
        ],
        compiler_params=pltpu.CompilerParams(vmem_limit_bytes=8 << 20),
        cost_estimate=pl.CostEstimate(flops=40 << 20, bytes_accessed=6 << 20, transcendentals=0),
    )(start, count, next_a, next_b, drops, band, image, waiting, one, two, courant, grad, parts)
    return results[0], results[1], results[6]


def per_device(
    velocity,
    aperture_start,
    aperture_count,
    wave_prev,
    wave_now,
    adjoint_prev,
    adjoint_now,
    source_cells,
    wavelet,
    receiver_cells,
    trace,
):
    steps = wavelet.shape[1]
    fields = (wave_now, adjoint_now, wave_prev, adjoint_prev)

    sent_a, sent_b, drops, band, one, two = pack(fields, steps)
    from_a = swap_pairs(sent_a, "slab", 0)
    from_b = swap_pairs(sent_b, "slab", 1)
    speeds = lax.all_gather(velocity, "shot")

    cells_w, cells_j = (jnp.transpose(places, (2, 0, 1)) for places in (source_cells, receiver_cells))
    small = (cells_w, cells_j, wavelet, trace)
    to_a, to_b, one, two, courant, image, grad = opening(
        aperture_start, aperture_count, sent_a, sent_b, speeds, band, one, two
    )
    next_a = swap_pairs(to_a, "slab", 0)
    next_b = swap_pairs(to_b, "slab", 1)
    drops, one, two, grad, waiting, parts = early_steps(
        aperture_count, small, from_a, from_b, courant, band, drops, one, two, grad, lax.axis_size("shot")
    )
    final_w, final_j, parts = late_steps(
        steps,
        aperture_start,
        aperture_count,
        next_a,
        next_b,
        drops,
        band,
        image,
        waiting,
        one,
        two,
        courant,
        grad,
        parts,
    )
    shares = lax.all_to_all(parts, "shot", 0, 0, tiled=True)
    return final_w, final_j, jnp.sum(shares, axis=0)


def solution(mesh):
    return jax.shard_map(
        per_device,
        mesh=mesh,
        in_specs=(
            P("slab", "shot", None),
            P("shot"),
            P("shot"),
            P("shot", "slab", None, None),
            P("shot", "slab", None, None),
            P("shot", "slab", None, None),
            P("shot", "slab", None, None),
            P("shot", None, None),
            P("shot", None, None),
            P("shot", None, None),
            P("shot", None, None),
        ),
        out_specs=(
            P("shot", "slab", None, None),
            P("shot", "slab", None, None),
            P("slab", "shot", None),
        ),
        check_vma=False,
    )
```

```python
import jax
import jax.numpy as jnp
from jax import lax
from jax.experimental import pallas as pl
from jax.experimental.pallas import tpu as pltpu
from jax.sharding import PartitionSpec as P


SCALE = 5040.0
scaled_weights = (-14350.0, 8064.0, -1008.0, 128.0, -9.0)
time_step = 0.09
REACH = 4
TILE = 8


def swap_pairs(block, axis, first):
    count = lax.axis_size(axis)
    route = []
    for i in range(first, count - 1, 2):
        route += [(i, i + 1), (i + 1, i)]
    return lax.ppermute(block, axis, route)


def any_space():
    return pl.BlockSpec(memory_space=pl.ANY)


def in_hbm(array):
    return pltpu.with_memory_space_constraint(array, pltpu.HBM)


def packing_kernel(now_w, now_j, prev_w, prev_j, to_a, to_b, drops, band, one, two, sems):
    cells = now_w.shape[1]
    deep_now = (to_a.shape[0] // 2 + REACH) // 2
    deep_prev = deep_now - REACH
    odd = lax.axis_index("slab") % 2
    copies, bring = bringing(sems)
    for out, side in ((to_a, 1 - odd), (to_b, odd)):
        at = 0
        for field, deep in ((now_w, deep_now), (now_j, deep_now), (prev_w, deep_prev), (prev_j, deep_prev)):
            bring(field.at[0, pl.ds(side * (cells - deep), deep)], out.at[pl.ds(at, deep)])
            at += deep
    steps, depth = drops.shape[0], drops.shape[4]
    zero_tile = jnp.zeros((TILE, depth), jnp.float32)

    def clear(x, carry):
        for field in range(2):
            for step in range(steps):
                drops[step, field, x] = zero_tile
            for buffer in (one, two):
                buffer[field, x, pl.ds(0, TILE), :] = zero_tile
                buffer[field, x, pl.ds(buffer.shape[2] - TILE, TILE), :] = zero_tile
        return carry

    lax.fori_loop(0, drops.shape[2], clear, 0)
    away = lax.broadcasted_iota(jnp.int32, (depth, depth), 0) - lax.broadcasted_iota(jnp.int32, (depth, depth), 1)
    matrix = jnp.zeros((depth, depth), jnp.float32)
    for k in range(1, REACH + 1):
        matrix = jnp.where((away == k) | (away == -k), scaled_weights[k], matrix)
    band[pl.ds(0, depth), :] = matrix.astype(jnp.bfloat16)
    band[pl.ds(depth, depth), :] = matrix.astype(jnp.bfloat16)
    for copy in copies:
        copy.wait()


def pack(fields, steps):
    cells, rows, depth = fields[0].shape[1:]
    deep = steps * REACH
    wide = cells + 2 * deep
    message = pltpu.VMEM((4 * (deep - REACH) - 2 * REACH, rows, depth), jnp.float32)
    drops = pltpu.VMEM((steps, 2, wide, TILE, depth), jnp.float32)
    band = pltpu.VMEM((2 * depth, depth), jnp.bfloat16)
    buffer = pltpu.VMEM((2, wide, rows + 2 * TILE, depth), jnp.float32)
    vmem = pl.BlockSpec(memory_space=pltpu.VMEM)
    return pl.pallas_call(
        packing_kernel,
        out_shape=(message, message, drops, band, buffer, buffer),
        in_specs=[pl.BlockSpec(memory_space=pltpu.HBM)] * 4,
        out_specs=(vmem,) * 6,
        scratch_shapes=[pltpu.SemaphoreType.DMA((8,))],
        compiler_params=pltpu.CompilerParams(vmem_limit_bytes=8 << 20),
        cost_estimate=pl.CostEstimate(flops=0, bytes_accessed=4 << 20, transcendentals=0),
    )(*map(in_hbm, fields))


def bringing(sems):
    copies = []

    def bring(source, target):
        copy = pltpu.make_async_copy(source, target, sems.at[len(copies)])
        copy.start()
        copies.append(copy)

    return copies, bring


def inject(drops, slab_first, field, places, amps):
    row = lax.broadcasted_iota(jnp.int32, drops.shape[3:], 0)
    col = lax.broadcasted_iota(jnp.int32, drops.shape[3:], 1)

    def one_cell(s, carry):
        x = places[0, 0, s] - slab_first
        inside = (x >= 0) & (x < drops.shape[2])
        x = jnp.clip(x, 0, drops.shape[2] - 1)
        here = (row == places[1, 0, s]) & (col == places[2, 0, s])
        tiles = [drops[step, field, x] for step in range(drops.shape[0])]
        for step, tile in enumerate(tiles):
            amp = jnp.where(inside, amps[0, step, s], 0.0)
            drops[step, field, x] = tile + jnp.where(here, amp, 0.0)
        return carry

    lax.fori_loop(0, places.shape[2], one_cell, 0, unroll=4)


def opening_kernel(
    start,
    count,
    sent_a,
    sent_b,
    speeds,
    band,
    one_in,
    two_in,
    to_a,
    to_b,
    one,
    two,
    courant,
    image,
    grad,
):
    cells, rows, depth = image.shape
    tiles = rows // TILE
    deep = to_a.shape[0]
    near = deep - 2 * REACH
    held = near + REACH
    half = cells // 2
    odd = lax.axis_index("slab") % 2
    start_block = start[0]
    live = count[0]
    sides = ((sent_a, to_a, 1 - odd), (sent_b, to_b, odd))
    inner = pl.ds(TILE, rows)
    for sent, _, side in sides:
        for field in range(2):
            for layer in range(half):
                x = deep + side * half + layer
                one[field, x, inner, :] = sent[field * held + layer + side * (held - half)]
                two[field, x, inner, :] = sent[2 * held + field * near + layer + side * (near - half)]

    def factors(x, carry):
        for tile in range(tiles):
            alive = jnp.where(tile < live, time_step * time_step / SCALE, 0.0)
            speed = speeds[start_block + tile, x]
            at = pl.ds(tile * TILE, TILE)
            courant[deep + x, at, :] = alive * (speed * speed)
            image[x, at, :] = (2.0 * time_step * time_step / SCALE) * speed
        return carry

    lax.fori_loop(0, cells, factors, 0, unroll=4)
    for _, out, side in sides:
        for layer in range(near):
            for tile in range(tiles):
                speed = speeds[start_block + tile, side * (cells - near) + layer]
                out[layer, pl.ds(tile * TILE, TILE), :] = speed
    clear_dead(one, two, live, deep, deep + cells)
    for groups in paired(range(deep + REACH, deep + cells - REACH, REACH)):
        advance(one, two, courant, None, band, 0, groups, grad, True, deep)
    for _, out, side in sides:
        for field in range(2):
            for i in range(REACH):
                x = deep + REACH + (1 - side) * (cells - 3 * REACH) + i
                out[near + field * REACH + i] = two[field, x, inner, :]


def clear_dead(one, two, live, first, last):
    tiles = one.shape[2] // TILE - 2
    for tile in range(1, tiles):

        @pl.when(tile >= live)
        def _():
            def clear(x, carry):
                for buffer in (one, two):
                    for field in range(2):
                        buffer[field, x, pl.ds(TILE + tile * TILE, TILE), :] = jnp.zeros(
                            (TILE, one.shape[3]), jnp.float32
                        )
                return carry

            lax.fori_loop(first, last, clear, 0)


def opening(start, count, sent_a, sent_b, speeds, band, one, two):
    cells, depth = speeds.shape[1], speeds.shape[3]
    rows = sent_a.shape[1]
    wide = one.shape[1]
    message = pltpu.VMEM(((wide - cells) // 2, rows, depth), jnp.float32)
    courant = pltpu.VMEM((wide, rows, depth), jnp.float32)
    layers = pltpu.VMEM((cells, rows, depth), jnp.float32)
    same = [pltpu.VMEM(array.shape, array.dtype) for array in (one, two)]
    vmem = pl.BlockSpec(memory_space=pltpu.VMEM)
    return pl.pallas_call(
        opening_kernel,
        out_shape=(message, message, *same, courant, layers, layers),
        in_specs=[pl.BlockSpec(memory_space=pltpu.SMEM)] * 2 + [vmem] * 6,
        out_specs=(vmem,) * 7,
        input_output_aliases={6: 2, 7: 3},
        compiler_params=pltpu.CompilerParams(vmem_limit_bytes=8 << 20),
        cost_estimate=pl.CostEstimate(flops=4 << 20, bytes_accessed=4 << 20, transcendentals=0),
    )(start, count, sent_a, sent_b, speeds, band, one, two)


def along_z(now, band, field, x):
    rows, depth = now.shape[2] - 2 * TILE, now.shape[3]
    cells = now[field, pl.ds(x, REACH), pl.ds(TILE, rows), :].reshape(REACH * rows, depth)
    high = cells.astype(jnp.bfloat16)
    low = (cells - high.astype(jnp.float32)).astype(jnp.bfloat16)
    return jnp.dot(jnp.concatenate([high, low], axis=1), band[...], preferred_element_type=jnp.float32)


def each_tile(now, band, groups, visit):
    rows = now.shape[2] - 2 * TILE
    spreads = [[along_z(now, band, field, x_first) for field in range(2)] for x_first in groups]
    for g, x_first in enumerate(groups):
        for tile in range(rows // TILE):
            at = TILE + tile * TILE
            pairs = []
            for field in range(2):
                line = [now[field, x_first + i, pl.ds(at, TILE), :] for i in range(-REACH, 2 * REACH)]
                for i in range(REACH):
                    center = line[REACH + i]
                    lap = (3.0 * scaled_weights[0]) * center
                    for k in range(1, REACH + 1):
                        near = line[REACH + i + k] + line[REACH + i - k]
                        near = near + now[field, x_first + i, pl.ds(at + k, TILE), :]
                        near = near + now[field, x_first + i, pl.ds(at - k, TILE), :]
                        lap = lap + scaled_weights[k] * near
                    row = i * rows + tile * TILE
                    pairs.append((center, lap + spreads[g][field][row : row + TILE]))
            for i in range(REACH):
                visit(g, tile, i, (pairs[i], pairs[REACH + i]))


def advance(now, other, courant, drops, band, step, groups, grad, fresh, deep, finals=None):
    def visit(g, tile, i, pair):
        x = groups[g] + i
        own = pl.ds(tile * TILE, TILE)
        padded = pl.ds(TILE + tile * TILE, TILE)
        factor = courant[x, own, :]
        for field, (center, lap) in enumerate(pair):
            ahead = 2.0 * center - other[field, x, padded, :] + factor * lap
            if tile == 0 and drops is not None:
                ahead = ahead + drops[step, field, x]
            if finals is None:
                other[field, x, padded, :] = ahead
            else:
                finals[field, x - deep, own, :] = ahead
        if grad is not None:
            term = pair[1][0] * pair[0][1]
            grad[x - deep, own, :] = term if fresh else grad[x - deep, own, :] + term

    each_tile(now, band, groups, visit)


def add_drops(buffer, drops, layers):
    for field in range(2):
        for x in layers:
            tile = buffer[field, x, pl.ds(TILE, TILE), :]
            buffer[field, x, pl.ds(TILE, TILE), :] = tile + drops[0, field, x]


def early_kernel(
    steps,
    count,
    cells_w_in,
    cells_j_in,
    amps_w_in,
    amps_j_in,
    from_a,
    from_b,
    courant,
    band,
    drops_in,
    one_in,
    two_in,
    grad_in,
    drops,
    one,
    two,
    grad,
    waiting,
    parts,
    cells_w,
    cells_j,
    amps_w,
    amps_j,
    sems,
):
    cells, rows, depth = grad.shape
    deep = steps * REACH
    near = deep - 2 * REACH
    held = near + REACH
    wide = cells + 2 * deep
    odd = lax.axis_index("slab") % 2

    left_of_a = odd
    copies, bring = bringing(sems)
    for source, target in ((cells_w_in, cells_w), (cells_j_in, cells_j), (amps_w_in, amps_w), (amps_j_in, amps_j)):
        bring(source, target)
    inner = pl.ds(TILE, rows)
    for field in range(2):
        for buffer, on_left in ((from_a, left_of_a), (from_b, 1 - left_of_a)):
            at = on_left * (deep - held) + (1 - on_left) * (deep + cells)
            bring(buffer.at[pl.ds(field * held, held)], one.at[field, pl.ds(at, held), inner])
            at = on_left * (deep - near) + (1 - on_left) * (deep + cells)
            bring(buffer.at[pl.ds(2 * held + field * near, near)], two.at[field, pl.ds(at, near), inner])
    def clear_parts(b, carry):
        parts[b] = jnp.zeros(parts.shape[1:], jnp.float32)
        return carry

    lax.fori_loop(0, parts.shape[0], clear_parts, 0)
    for copy in copies:
        copy.wait()
    slab_first = lax.axis_index("slab") * cells - deep
    inject(drops, slab_first, 0, cells_w, amps_w)
    inject(drops, slab_first, 1, cells_j, amps_j)
    add_drops(two, drops, range(deep + REACH, deep + cells - REACH))
    clear_dead(one, two, count[0], 0, deep)
    clear_dead(one, two, count[0], deep + cells, wide)

    def outside(c, carry):
        groups = [deep - near + c * (near + cells) + i for i in range(0, near, REACH)]

        def visit(g, tile, i, pair):
            x = groups[g] + i
            padded = pl.ds(TILE + tile * TILE, TILE)
            for field, (center, lap) in enumerate(pair):
                waiting[field, c * near + g * REACH + i, pl.ds(tile * TILE, TILE), :] = lap
                ahead = 2.0 * center - two[field, x, padded, :]
                two[field, x, padded, :] = ahead + drops[0, field, x] if tile == 0 else ahead

        each_tile(one, band, groups, visit)
        return carry

    advance(one, two, courant, drops, band, 0, [deep, deep + cells - REACH], grad, True, deep)
    lax.fori_loop(0, 2, outside, 0)
    for groups in paired(range(deep + REACH, deep + cells - REACH, REACH)):
        advance(two, one, courant, drops, band, 1, groups, grad, False, deep)


def paired(starts):
    starts = list(starts)
    return [starts[i : i + 2] for i in range(0, len(starts), 2)]


def late_kernel(
    steps,
    start,
    count,
    next_a,
    next_b,
    drops,
    band,
    image,
    waiting,
    one_in,
    two_in,
    courant_in,
    grad_in,
    parts_in,
    finals,
    one,
    two,
    courant,
    grad,
    parts,
):
    cells, rows, depth = image.shape
    deep = steps * REACH
    near = deep - 2 * REACH
    tiles = rows // TILE
    odd = lax.axis_index("slab") % 2
    start_block = start[0]
    live = count[0]

    def finish(h, carry):
        right = h >= near
        layer = jnp.where(right, h - near, h)
        x = jnp.where(right, deep + cells, deep - near) + layer
        use_a = jnp.where(right, 1 - odd, odd) == 1
        for tile in range(tiles):
            alive = jnp.where(tile < live, time_step * time_step / SCALE, 0.0)
            own = pl.ds(tile * TILE, TILE)
            speed = jnp.where(use_a, next_a[layer, own, :], next_b[layer, own, :])
            factor = alive * (speed * speed)
            courant[x, own, :] = factor
            for field in range(2):
                at = pl.ds(TILE + tile * TILE, TILE)
                change = factor * waiting[field, h, own, :]
                two[field, x, at, :] = two[field, x, at, :] + change
        return carry

    lax.fori_loop(0, 2 * near, finish, 0, unroll=4)
    inner = pl.ds(TILE, rows)
    for message, left in ((next_a, odd), (next_b, 1 - odd)):
        for field in range(2):
            for i in range(REACH):
                x = left * (deep - near - REACH) + (1 - left) * (deep + cells + near) + i
                two[field, x, inner, :] = message[near + field * REACH + i]
    add_drops(two, drops, range(deep - near - REACH, deep - near))
    add_drops(two, drops, range(deep + cells + near, deep + cells + near + REACH))

    now, other = two, one
    for step in range(1, steps):
        edge = range(REACH * (step + 1), deep, REACH)
        groups = list(edge) + [x + cells + deep - REACH * (step + 1) for x in edge]
        for pair in paired(groups):
            advance(now, other, courant, drops, band, step, pair, None, False, deep)
        own = range(deep, deep + cells, REACH)
        groups = [own[0], own[-1]] if step == 1 else own
        last = finals if step == steps - 1 else None
        for pair in paired(groups):
            advance(now, other, courant, drops, band, step, pair, grad, False, deep, last)
        now, other = other, now

    def place(x, carry):
        for tile in range(tiles):
            at = pl.ds(tile * TILE, TILE)
            parts[start_block + tile, x] = image[x, at, :] * grad[x, at, :]
        return carry

    lax.fori_loop(0, cells, place, 0, unroll=4)


def early_steps(count, small, from_a, from_b, courant, band, drops, one, two, grad, groups):
    cells, rows, depth = grad.shape
    steps = drops.shape[0]
    waiting = pltpu.VMEM((2, 2 * (steps - 2) * REACH, rows, depth), jnp.float32)
    parts = pltpu.VMEM((groups, cells, TILE, depth), jnp.float32)
    vmem = pl.BlockSpec(memory_space=pltpu.VMEM)
    same = [pltpu.VMEM(array.shape, array.dtype) for array in (drops, one, two, grad)]

    def kernel(*refs):
        early_kernel(steps, *refs)

    return pl.pallas_call(
        kernel,
        out_shape=(*same, waiting, parts),
        in_specs=[pl.BlockSpec(memory_space=pltpu.SMEM)]
        + [pl.BlockSpec(memory_space=pltpu.HBM)] * 4
        + [any_space()] * 2
        + [vmem] * 6,
        out_specs=(vmem,) * 6,
        input_output_aliases={9: 0, 10: 1, 11: 2, 12: 3},
        scratch_shapes=[pltpu.SMEM(array.shape, array.dtype) for array in small] + [pltpu.SemaphoreType.DMA((12,))],
        compiler_params=pltpu.CompilerParams(vmem_limit_bytes=8 << 20),
        cost_estimate=pl.CostEstimate(flops=20 << 20, bytes_accessed=4 << 20, transcendentals=0),
    )(count, *map(in_hbm, small), from_a, from_b, courant, band, drops, one, two, grad)


def late_steps(steps, start, count, next_a, next_b, drops, band, image, waiting, one, two, courant, grad, parts):
    smem = pl.BlockSpec(memory_space=pltpu.SMEM)
    vmem = pl.BlockSpec(memory_space=pltpu.VMEM)
    finals = pltpu.VMEM((2, *image.shape), jnp.float32)
    same = [pltpu.VMEM(array.shape, array.dtype) for array in (one, two, courant, grad, parts)]

    def kernel(*refs):
        late_kernel(steps, *refs)

    results = pl.pallas_call(
        kernel,
        out_shape=(finals, *same),
        in_specs=[smem] * 2 + [vmem] * 11,
        out_specs=(vmem,) * 6,
        input_output_aliases={8: 1, 9: 2, 10: 3, 11: 4, 12: 5},
        compiler_params=pltpu.CompilerParams(vmem_limit_bytes=8 << 20),
        cost_estimate=pl.CostEstimate(flops=40 << 20, bytes_accessed=6 << 20, transcendentals=0),
    )(start, count, next_a, next_b, drops, band, image, waiting, one, two, courant, grad, parts)
    return results[0], results[5]


def closing_kernel(finals, shares, final_w, final_j, gradient, total, sems):
    copies, bring = bringing(sems)
    bring(finals.at[0], final_w.at[0])
    bring(finals.at[1], final_j.at[0])
    value = shares[0]
    for group in range(1, shares.shape[0]):
        value = value + shares[group]
    total[...] = value
    bring(total, gradient)
    for copy in copies:
        copy.wait()


def closing(finals, shares):
    final = jax.ShapeDtypeStruct((1, *finals.shape[1:]), jnp.float32)
    block = shares.shape[1:]
    return pl.pallas_call(
        closing_kernel,
        out_shape=(final, final, jax.ShapeDtypeStruct(block, jnp.float32)),
        in_specs=[pl.BlockSpec(memory_space=pltpu.VMEM)] * 2,
        out_specs=(any_space(),) * 3,
        scratch_shapes=[pltpu.VMEM(block, jnp.float32), pltpu.SemaphoreType.DMA((3,))],
        compiler_params=pltpu.CompilerParams(vmem_limit_bytes=8 << 20),
        cost_estimate=pl.CostEstimate(flops=1 << 20, bytes_accessed=2 << 20, transcendentals=0),
    )(finals, shares)


def per_device(
    velocity,
    aperture_start,
    aperture_count,
    wave_prev,
    wave_now,
    adjoint_prev,
    adjoint_now,
    source_cells,
    wavelet,
    receiver_cells,
    trace,
):
    steps = wavelet.shape[1]
    fields = (wave_now, adjoint_now, wave_prev, adjoint_prev)

    sent_a, sent_b, drops, band, one, two = pack(fields, steps)
    from_a = swap_pairs(sent_a, "slab", 0)
    from_b = swap_pairs(sent_b, "slab", 1)
    speeds = lax.all_gather(velocity, "shot")

    cells_w, cells_j = (jnp.transpose(places, (2, 0, 1)) for places in (source_cells, receiver_cells))
    small = (cells_w, cells_j, wavelet, trace)
    to_a, to_b, one, two, courant, image, grad = opening(
        aperture_start, aperture_count, sent_a, sent_b, speeds, band, one, two
    )
    next_a = swap_pairs(to_a, "slab", 0)
    next_b = swap_pairs(to_b, "slab", 1)
    drops, one, two, grad, waiting, parts = early_steps(
        aperture_count, small, from_a, from_b, courant, band, drops, one, two, grad, lax.axis_size("shot")
    )
    finals, parts = late_steps(
        steps,
        aperture_start,
        aperture_count,
        next_a,
        next_b,
        drops,
        band,
        image,
        waiting,
        one,
        two,
        courant,
        grad,
        parts,
    )
    shares = lax.all_to_all(parts, "shot", 0, 0, tiled=True)
    return closing(finals, shares)


def solution(mesh):
    return jax.shard_map(
        per_device,
        mesh=mesh,
        in_specs=(
            P("slab", "shot", None),
            P("shot"),
            P("shot"),
            P("shot", "slab", None, None),
            P("shot", "slab", None, None),
            P("shot", "slab", None, None),
            P("shot", "slab", None, None),
            P("shot", None, None),
            P("shot", None, None),
            P("shot", None, None),
            P("shot", None, None),
        ),
        out_specs=(
            P("shot", "slab", None, None),
            P("shot", "slab", None, None),
            P("slab", "shot", None),
        ),
        check_vma=False,
    )
```

```python
import jax
import jax.numpy as jnp
from jax import lax
from jax.experimental import pallas as pl
from jax.experimental.pallas import tpu as pltpu
from jax.sharding import PartitionSpec as P


SCALE = 5040.0
scaled_weights = (-14350.0, 8064.0, -1008.0, 128.0, -9.0)
time_step = 0.09
REACH = 4
TILE = 8


def swap_pairs(block, axis, first):
    count = lax.axis_size(axis)
    route = []
    for i in range(first, count - 1, 2):
        route += [(i, i + 1), (i + 1, i)]
    return lax.ppermute(block, axis, route)


def any_space():
    return pl.BlockSpec(memory_space=pl.ANY)


def in_hbm(array):
    return pltpu.with_memory_space_constraint(array, pltpu.HBM)


def packing_kernel(now_w, now_j, prev_w, prev_j, to_a, to_b, drops, band, one, two, sems):
    cells = now_w.shape[1]
    deep_now = (to_a.shape[0] // 2 + REACH) // 2
    deep_prev = deep_now - REACH
    odd = lax.axis_index("slab") % 2
    copies, bring = bringing(sems)
    for out, side in ((to_a, 1 - odd), (to_b, odd)):
        at = 0
        for field, deep in ((now_w, deep_now), (now_j, deep_now), (prev_w, deep_prev), (prev_j, deep_prev)):
            bring(field.at[0, pl.ds(side * (cells - deep), deep)], out.at[pl.ds(at, deep)])
            at += deep
    steps, depth = drops.shape[0], drops.shape[4]
    zero_tile = jnp.zeros((TILE, depth), jnp.float32)

    def clear(x, carry):
        for field in range(2):
            for step in range(steps):
                drops[step, field, x] = zero_tile
            for buffer in (one, two):
                buffer[field, x, pl.ds(0, TILE), :] = zero_tile
                buffer[field, x, pl.ds(buffer.shape[2] - TILE, TILE), :] = zero_tile
        return carry

    lax.fori_loop(0, drops.shape[2], clear, 0)
    away = lax.broadcasted_iota(jnp.int32, (depth, depth), 0) - lax.broadcasted_iota(jnp.int32, (depth, depth), 1)
    matrix = jnp.zeros((depth, depth), jnp.float32)
    for k in range(1, REACH + 1):
        matrix = jnp.where((away == k) | (away == -k), scaled_weights[k], matrix)
    band[pl.ds(0, depth), :] = matrix.astype(jnp.bfloat16)
    band[pl.ds(depth, depth), :] = matrix.astype(jnp.bfloat16)
    for copy in copies:
        copy.wait()


def pack(fields, steps):
    cells, rows, depth = fields[0].shape[1:]
    deep = steps * REACH
    wide = cells + 2 * deep
    message = pltpu.VMEM((4 * (deep - REACH) - 2 * REACH, rows, depth), jnp.float32)
    drops = pltpu.VMEM((steps, 2, wide, TILE, depth), jnp.float32)
    band = pltpu.VMEM((2 * depth, depth), jnp.bfloat16)
    buffer = pltpu.VMEM((2, wide, rows + 2 * TILE, depth), jnp.float32)
    vmem = pl.BlockSpec(memory_space=pltpu.VMEM)
    return pl.pallas_call(
        packing_kernel,
        out_shape=(message, message, drops, band, buffer, buffer),
        in_specs=[pl.BlockSpec(memory_space=pltpu.HBM)] * 4,
        out_specs=(vmem,) * 6,
        scratch_shapes=[pltpu.SemaphoreType.DMA((8,))],
        compiler_params=pltpu.CompilerParams(vmem_limit_bytes=8 << 20),
        cost_estimate=pl.CostEstimate(flops=0, bytes_accessed=4 << 20, transcendentals=0),
    )(*map(in_hbm, fields))


def bringing(sems):
    copies = []

    def bring(source, target):
        copy = pltpu.make_async_copy(source, target, sems.at[len(copies)])
        copy.start()
        copies.append(copy)

    return copies, bring


def inject(drops, slab_first, field, places, amps):
    row = lax.broadcasted_iota(jnp.int32, drops.shape[3:], 0)
    col = lax.broadcasted_iota(jnp.int32, drops.shape[3:], 1)

    def one_cell(s, carry):
        x = places[0, 0, s] - slab_first
        inside = (x >= 0) & (x < drops.shape[2])
        x = jnp.clip(x, 0, drops.shape[2] - 1)
        here = (row == places[1, 0, s]) & (col == places[2, 0, s])
        tiles = [drops[step, field, x] for step in range(drops.shape[0])]
        for step, tile in enumerate(tiles):
            amp = jnp.where(inside, amps[0, step, s], 0.0)
            drops[step, field, x] = tile + jnp.where(here, amp, 0.0)
        return carry

    lax.fori_loop(0, places.shape[2], one_cell, 0, unroll=4)


def opening_kernel(
    start,
    count,
    sent_a,
    sent_b,
    speeds,
    band,
    one_in,
    two_in,
    to_a,
    to_b,
    one,
    two,
    courant,
    image,
    grad,
):
    cells, rows, depth = image.shape
    tiles = rows // TILE
    deep = to_a.shape[0]
    near = deep - 2 * REACH
    held = near + REACH
    half = cells // 2
    odd = lax.axis_index("slab") % 2
    start_block = start[0]
    live = count[0]
    sides = ((sent_a, to_a, 1 - odd), (sent_b, to_b, odd))
    inner = pl.ds(TILE, rows)
    for sent, _, side in sides:
        for field in range(2):
            for layer in range(half):
                x = deep + side * half + layer
                one[field, x, inner, :] = sent[field * held + layer + side * (held - half)]
                two[field, x, inner, :] = sent[2 * held + field * near + layer + side * (near - half)]

    def factors(x, carry):
        for tile in range(tiles):
            alive = jnp.where(tile < live, time_step * time_step / SCALE, 0.0)
            speed = speeds[start_block + tile, x]
            at = pl.ds(tile * TILE, TILE)
            courant[deep + x, at, :] = alive * (speed * speed)
            image[x, at, :] = (2.0 * time_step * time_step / SCALE) * speed
        return carry

    lax.fori_loop(0, cells, factors, 0, unroll=4)
    for _, out, side in sides:
        for layer in range(near):
            for tile in range(tiles):
                speed = speeds[start_block + tile, side * (cells - near) + layer]
                out[layer, pl.ds(tile * TILE, TILE), :] = speed
    clear_dead(one, two, live, deep, deep + cells)
    for groups in paired(range(deep + REACH, deep + cells - REACH, REACH)):
        advance(one, two, courant, None, band, 0, groups, grad, True, deep)
    for _, out, side in sides:
        for field in range(2):
            for i in range(REACH):
                x = deep + REACH + (1 - side) * (cells - 3 * REACH) + i
                out[near + field * REACH + i] = two[field, x, inner, :]


def clear_dead(one, two, live, first, last):
    tiles = one.shape[2] // TILE - 2
    for tile in range(1, tiles):

        @pl.when(tile >= live)
        def _():
            def clear(x, carry):
                for buffer in (one, two):
                    for field in range(2):
                        buffer[field, x, pl.ds(TILE + tile * TILE, TILE), :] = jnp.zeros(
                            (TILE, one.shape[3]), jnp.float32
                        )
                return carry

            lax.fori_loop(first, last, clear, 0)


def opening(start, count, sent_a, sent_b, speeds, band, one, two):
    cells, depth = speeds.shape[1], speeds.shape[3]
    rows = sent_a.shape[1]
    wide = one.shape[1]
    message = pltpu.VMEM(((wide - cells) // 2, rows, depth), jnp.float32)
    courant = pltpu.VMEM((wide, rows, depth), jnp.float32)
    layers = pltpu.VMEM((cells, rows, depth), jnp.float32)
    same = [pltpu.VMEM(array.shape, array.dtype) for array in (one, two)]
    vmem = pl.BlockSpec(memory_space=pltpu.VMEM)
    return pl.pallas_call(
        opening_kernel,
        out_shape=(message, message, *same, courant, layers, layers),
        in_specs=[pl.BlockSpec(memory_space=pltpu.SMEM)] * 2 + [vmem] * 6,
        out_specs=(vmem,) * 7,
        input_output_aliases={6: 2, 7: 3},
        compiler_params=pltpu.CompilerParams(vmem_limit_bytes=8 << 20),
        cost_estimate=pl.CostEstimate(flops=4 << 20, bytes_accessed=4 << 20, transcendentals=0),
    )(start, count, sent_a, sent_b, speeds, band, one, two)


def along_z(now, band, field, x):
    rows, depth = now.shape[2] - 2 * TILE, now.shape[3]
    cells = now[field, pl.ds(x, REACH), pl.ds(TILE, rows), :].reshape(REACH * rows, depth)
    high = cells.astype(jnp.bfloat16)
    low = (cells - high.astype(jnp.float32)).astype(jnp.bfloat16)
    return jnp.dot(jnp.concatenate([high, low], axis=1), band[...], preferred_element_type=jnp.float32)


def each_tile(now, band, groups, visit):
    rows = now.shape[2] - 2 * TILE
    spreads = [[along_z(now, band, field, x_first) for field in range(2)] for x_first in groups]
    for g, x_first in enumerate(groups):
        for tile in range(rows // TILE):
            at = TILE + tile * TILE
            pairs = []
            for field in range(2):
                line = [now[field, x_first + i, pl.ds(at, TILE), :] for i in range(-REACH, 2 * REACH)]
                for i in range(REACH):
                    center = line[REACH + i]
                    lap = (3.0 * scaled_weights[0]) * center
                    for k in range(1, REACH + 1):
                        near = line[REACH + i + k] + line[REACH + i - k]
                        near = near + now[field, x_first + i, pl.ds(at + k, TILE), :]
                        near = near + now[field, x_first + i, pl.ds(at - k, TILE), :]
                        lap = lap + scaled_weights[k] * near
                    row = i * rows + tile * TILE
                    pairs.append((center, lap + spreads[g][field][row : row + TILE]))
            for i in range(REACH):
                visit(g, tile, i, (pairs[i], pairs[REACH + i]))


def advance(now, other, courant, drops, band, step, groups, grad, fresh, deep, finals=None):
    def visit(g, tile, i, pair):
        x = groups[g] + i
        own = pl.ds(tile * TILE, TILE)
        padded = pl.ds(TILE + tile * TILE, TILE)
        factor = courant[x, own, :]
        for field, (center, lap) in enumerate(pair):
            ahead = 2.0 * center - other[field, x, padded, :] + factor * lap
            if tile == 0 and drops is not None:
                ahead = ahead + drops[step, field, x]
            if finals is None:
                other[field, x, padded, :] = ahead
            else:
                finals[field, x - deep, own, :] = ahead
        if grad is not None:
            term = pair[1][0] * pair[0][1]
            grad[x - deep, own, :] = term if fresh else grad[x - deep, own, :] + term

    each_tile(now, band, groups, visit)


def add_drops(buffer, drops, layers):
    for field in range(2):
        for x in layers:
            tile = buffer[field, x, pl.ds(TILE, TILE), :]
            buffer[field, x, pl.ds(TILE, TILE), :] = tile + drops[0, field, x]


def early_kernel(
    steps,
    count,
    cells_w_in,
    cells_j_in,
    amps_w_in,
    amps_j_in,
    from_a,
    from_b,
    courant,
    band,
    drops_in,
    one_in,
    two_in,
    grad_in,
    drops,
    one,
    two,
    grad,
    waiting,
    parts,
    cells_w,
    cells_j,
    amps_w,
    amps_j,
    sems,
):
    cells, rows, depth = grad.shape
    deep = steps * REACH
    near = deep - 2 * REACH
    held = near + REACH
    wide = cells + 2 * deep
    odd = lax.axis_index("slab") % 2

    left_of_a = odd
    copies, bring = bringing(sems)
    for source, target in ((cells_w_in, cells_w), (cells_j_in, cells_j), (amps_w_in, amps_w), (amps_j_in, amps_j)):
        bring(source, target)
    inner = pl.ds(TILE, rows)
    for field in range(2):
        for buffer, on_left in ((from_a, left_of_a), (from_b, 1 - left_of_a)):
            at = on_left * (deep - held) + (1 - on_left) * (deep + cells)
            bring(buffer.at[pl.ds(field * held, held)], one.at[field, pl.ds(at, held), inner])
            at = on_left * (deep - near) + (1 - on_left) * (deep + cells)
            bring(buffer.at[pl.ds(2 * held + field * near, near)], two.at[field, pl.ds(at, near), inner])
    def clear_parts(b, carry):
        parts[b] = jnp.zeros(parts.shape[1:], jnp.float32)
        return carry

    lax.fori_loop(0, parts.shape[0], clear_parts, 0)
    for copy in copies:
        copy.wait()
    slab_first = lax.axis_index("slab") * cells - deep
    inject(drops, slab_first, 0, cells_w, amps_w)
    inject(drops, slab_first, 1, cells_j, amps_j)
    add_drops(two, drops, range(deep + REACH, deep + cells - REACH))
    clear_dead(one, two, count[0], 0, deep)
    clear_dead(one, two, count[0], deep + cells, wide)

    def outside(c, carry):
        groups = [deep - near + c * (near + cells) + i for i in range(0, near, REACH)]

        def visit(g, tile, i, pair):
            x = groups[g] + i
            padded = pl.ds(TILE + tile * TILE, TILE)
            for field, (center, lap) in enumerate(pair):
                waiting[field, c * near + g * REACH + i, pl.ds(tile * TILE, TILE), :] = lap
                ahead = 2.0 * center - two[field, x, padded, :]
                two[field, x, padded, :] = ahead + drops[0, field, x] if tile == 0 else ahead

        each_tile(one, band, groups, visit)
        return carry

    advance(one, two, courant, drops, band, 0, [deep, deep + cells - REACH], grad, True, deep)
    lax.fori_loop(0, 2, outside, 0)
    for groups in paired(range(deep + REACH, deep + cells - REACH, REACH)):
        advance(two, one, courant, drops, band, 1, groups, grad, False, deep)


def paired(starts):
    starts = list(starts)
    return [starts[i : i + 2] for i in range(0, len(starts), 2)]


def take_side(on_left, live, message, drops, band, waiting, finals, one, two, courant, grad):
    cells = grad.shape[0]
    rows = grad.shape[1]
    deep = message.shape[0]
    near = deep - 2 * REACH
    steps = deep // REACH

    def place(left, right):
        return on_left * left + (1 - on_left) * right

    def finish(layer, carry):
        x = place(deep - near, deep + cells) + layer
        h = place(0, near) + layer
        for tile in range(rows // TILE):
            alive = jnp.where(tile < live, time_step * time_step / SCALE, 0.0)
            own = pl.ds(tile * TILE, TILE)
            padded = pl.ds(TILE + tile * TILE, TILE)
            speed = message[layer, own, :]
            factor = alive * (speed * speed)
            courant[x, own, :] = factor
            for field in range(2):
                change = factor * waiting[field, h, own, :]
                two[field, x, padded, :] = two[field, x, padded, :] + change
        return carry

    lax.fori_loop(0, near, finish, 0, unroll=4)
    first = place(deep - near - REACH, deep + cells + near)
    for field in range(2):
        for i in range(REACH):
            two[field, first + i, pl.ds(TILE, rows), :] = message[near + field * REACH + i]
    add_drops(two, drops, [first + i for i in range(REACH)])

    now, other = two, one
    for step in range(1, steps):
        inner = REACH if step == 1 else cells // 2 - REACH * (step - 2)
        depths = range(REACH * (step + 1) - deep, inner, REACH)
        halo = [place(deep + d, deep + cells - REACH - d) for d in depths if d < 0]
        own = [place(deep + d, deep + cells - REACH - d) for d in depths if d >= 0]
        last = finals if step == steps - 1 else None
        if halo:
            advance(now, other, courant, drops, band, step, halo, None, False, deep)
        advance(now, other, courant, drops, band, step, own, grad, False, deep, last)
        now, other = other, now


def first_side_kernel(
    count,
    message,
    drops,
    band,
    waiting,
    one_in,
    two_in,
    courant_in,
    grad_in,
    finals,
    one,
    two,
    courant,
    grad,
):
    odd = lax.axis_index("slab") % 2
    take_side(odd, count[0], message, drops, band, waiting, finals, one, two, courant, grad)


def second_side_kernel(
    start,
    count,
    message,
    drops,
    band,
    waiting,
    image,
    finals_in,
    one_in,
    two_in,
    courant_in,
    grad_in,
    parts_in,
    finals,
    one,
    two,
    courant,
    grad,
    parts,
):
    cells, rows, _ = image.shape
    deep = message.shape[0]
    steps = deep // REACH
    odd = lax.axis_index("slab") % 2
    start_block = start[0]
    take_side(1 - odd, count[0], message, drops, band, waiting, finals, one, two, courant, grad)
    now, other = (one, two) if steps % 2 else (two, one)
    for step in range(3, steps):
        reach = cells // 2 - REACH * (step - 2)
        for groups in paired(range(deep + reach, deep + cells - reach, REACH)):
            advance(now, other, courant, drops, band, step, groups, grad, False, deep, finals)

    def place(x, carry):
        for tile in range(rows // TILE):
            at = pl.ds(tile * TILE, TILE)
            parts[start_block + tile, x] = image[x, at, :] * grad[x, at, :]
        return carry

    lax.fori_loop(0, cells, place, 0, unroll=4)


def early_steps(count, small, from_a, from_b, courant, band, drops, one, two, grad, groups):
    cells, rows, depth = grad.shape
    steps = drops.shape[0]
    waiting = pltpu.VMEM((2, 2 * (steps - 2) * REACH, rows, depth), jnp.float32)
    parts = pltpu.VMEM((groups, cells, TILE, depth), jnp.float32)
    vmem = pl.BlockSpec(memory_space=pltpu.VMEM)
    same = [pltpu.VMEM(array.shape, array.dtype) for array in (drops, one, two, grad)]

    def kernel(*refs):
        early_kernel(steps, *refs)

    return pl.pallas_call(
        kernel,
        out_shape=(*same, waiting, parts),
        in_specs=[pl.BlockSpec(memory_space=pltpu.SMEM)]
        + [pl.BlockSpec(memory_space=pltpu.HBM)] * 4
        + [any_space()] * 2
        + [vmem] * 6,
        out_specs=(vmem,) * 6,
        input_output_aliases={9: 0, 10: 1, 11: 2, 12: 3},
        scratch_shapes=[pltpu.SMEM(array.shape, array.dtype) for array in small] + [pltpu.SemaphoreType.DMA((12,))],
        compiler_params=pltpu.CompilerParams(vmem_limit_bytes=8 << 20),
        cost_estimate=pl.CostEstimate(flops=20 << 20, bytes_accessed=4 << 20, transcendentals=0),
    )(count, *map(in_hbm, small), from_a, from_b, courant, band, drops, one, two, grad)


def first_side(count, message, drops, band, waiting, one, two, courant, grad):
    vmem = pl.BlockSpec(memory_space=pltpu.VMEM)
    finals = pltpu.VMEM((2, *grad.shape), jnp.float32)
    same = [pltpu.VMEM(array.shape, array.dtype) for array in (one, two, courant, grad)]
    return pl.pallas_call(
        first_side_kernel,
        out_shape=(finals, *same),
        in_specs=[pl.BlockSpec(memory_space=pltpu.SMEM)] + [vmem] * 8,
        out_specs=(vmem,) * 5,
        input_output_aliases={5: 1, 6: 2, 7: 3, 8: 4},
        compiler_params=pltpu.CompilerParams(vmem_limit_bytes=8 << 20),
        cost_estimate=pl.CostEstimate(flops=20 << 20, bytes_accessed=3 << 20, transcendentals=0),
    )(count, message, drops, band, waiting, one, two, courant, grad)


def second_side(start, count, message, drops, band, waiting, image, finals, one, two, courant, grad, parts):
    vmem = pl.BlockSpec(memory_space=pltpu.VMEM)
    same = [pltpu.VMEM(array.shape, array.dtype) for array in (finals, one, two, courant, grad, parts)]
    results = pl.pallas_call(
        second_side_kernel,
        out_shape=tuple(same),
        in_specs=[pl.BlockSpec(memory_space=pltpu.SMEM)] * 2 + [vmem] * 11,
        out_specs=(vmem,) * 6,
        input_output_aliases={7: 0, 8: 1, 9: 2, 10: 3, 11: 4, 12: 5},
        compiler_params=pltpu.CompilerParams(vmem_limit_bytes=8 << 20),
        cost_estimate=pl.CostEstimate(flops=20 << 20, bytes_accessed=3 << 20, transcendentals=0),
    )(start, count, message, drops, band, waiting, image, finals, one, two, courant, grad, parts)
    return results[0], results[5]


def closing_kernel(finals, shares, final_w, final_j, gradient, total, sems):
    copies, bring = bringing(sems)
    bring(finals.at[0], final_w.at[0])
    bring(finals.at[1], final_j.at[0])
    value = shares[0]
    for group in range(1, shares.shape[0]):
        value = value + shares[group]
    total[...] = value
    bring(total, gradient)
    for copy in copies:
        copy.wait()


def closing(finals, shares):
    final = jax.ShapeDtypeStruct((1, *finals.shape[1:]), jnp.float32)
    block = shares.shape[1:]
    return pl.pallas_call(
        closing_kernel,
        out_shape=(final, final, jax.ShapeDtypeStruct(block, jnp.float32)),
        in_specs=[pl.BlockSpec(memory_space=pltpu.VMEM)] * 2,
        out_specs=(any_space(),) * 3,
        scratch_shapes=[pltpu.VMEM(block, jnp.float32), pltpu.SemaphoreType.DMA((3,))],
        compiler_params=pltpu.CompilerParams(vmem_limit_bytes=8 << 20),
        cost_estimate=pl.CostEstimate(flops=1 << 20, bytes_accessed=2 << 20, transcendentals=0),
    )(finals, shares)


def per_device(
    velocity,
    aperture_start,
    aperture_count,
    wave_prev,
    wave_now,
    adjoint_prev,
    adjoint_now,
    source_cells,
    wavelet,
    receiver_cells,
    trace,
):
    steps = wavelet.shape[1]
    fields = (wave_now, adjoint_now, wave_prev, adjoint_prev)

    sent_a, sent_b, drops, band, one, two = pack(fields, steps)
    from_a = swap_pairs(sent_a, "slab", 0)
    from_b = swap_pairs(sent_b, "slab", 1)
    speeds = lax.all_gather(velocity, "shot")

    cells_w, cells_j = (jnp.transpose(places, (2, 0, 1)) for places in (source_cells, receiver_cells))
    small = (cells_w, cells_j, wavelet, trace)
    to_a, to_b, one, two, courant, image, grad = opening(
        aperture_start, aperture_count, sent_a, sent_b, speeds, band, one, two
    )
    next_a = swap_pairs(to_a, "slab", 0)
    next_b = swap_pairs(to_b, "slab", 1)
    drops, one, two, grad, waiting, parts = early_steps(
        aperture_count, small, from_a, from_b, courant, band, drops, one, two, grad, lax.axis_size("shot")
    )
    finals, one, two, courant, grad = first_side(
        aperture_count, next_a, drops, band, waiting, one, two, courant, grad
    )
    finals, parts = second_side(
        aperture_start,
        aperture_count,
        next_b,
        drops,
        band,
        waiting,
        image,
        finals,
        one,
        two,
        courant,
        grad,
        parts,
    )
    shares = lax.all_to_all(parts, "shot", 0, 0, tiled=True)
    return closing(finals, shares)


def solution(mesh):
    return jax.shard_map(
        per_device,
        mesh=mesh,
        in_specs=(
            P("slab", "shot", None),
            P("shot"),
            P("shot"),
            P("shot", "slab", None, None),
            P("shot", "slab", None, None),
            P("shot", "slab", None, None),
            P("shot", "slab", None, None),
            P("shot", None, None),
            P("shot", None, None),
            P("shot", None, None),
            P("shot", None, None),
        ),
        out_specs=(
            P("shot", "slab", None, None),
            P("shot", "slab", None, None),
            P("slab", "shot", None),
        ),
        check_vma=False,
    )
```

```python
import jax
import jax.numpy as jnp
from jax import lax
from jax.experimental import pallas as pl
from jax.experimental.pallas import tpu as pltpu
from jax.sharding import PartitionSpec as P


SCALE = 5040.0
scaled_weights = (-14350.0, 8064.0, -1008.0, 128.0, -9.0)
time_step = 0.09
REACH = 4
TILE = 8


def swap_pairs(block, axis, first):
    count = lax.axis_size(axis)
    route = []
    for i in range(first, count - 1, 2):
        route += [(i, i + 1), (i + 1, i)]
    return lax.ppermute(block, axis, route)


def any_space():
    return pl.BlockSpec(memory_space=pl.ANY)


def in_hbm(array):
    return pltpu.with_memory_space_constraint(array, pltpu.HBM)


def packing_kernel(now_w, now_j, prev_w, prev_j, to_a, to_b, drops, band, one, two, sems):
    cells = now_w.shape[1]
    deep_now = (to_a.shape[0] // 2 + REACH) // 2
    deep_prev = deep_now - REACH
    odd = lax.axis_index("slab") % 2
    copies, bring = bringing(sems)
    for out, side in ((to_a, 1 - odd), (to_b, odd)):
        at = 0
        for field, deep in ((now_w, deep_now), (now_j, deep_now), (prev_w, deep_prev), (prev_j, deep_prev)):
            bring(field.at[0, pl.ds(side * (cells - deep), deep)], out.at[pl.ds(at, deep)])
            at += deep
    steps, depth = drops.shape[0], drops.shape[4]
    zero_tile = jnp.zeros((TILE, depth), jnp.float32)

    def clear(x, carry):
        for field in range(2):
            for step in range(steps):
                drops[step, field, x] = zero_tile
            for buffer in (one, two):
                buffer[field, x, pl.ds(0, TILE), :] = zero_tile
                buffer[field, x, pl.ds(buffer.shape[2] - TILE, TILE), :] = zero_tile
        return carry

    lax.fori_loop(0, drops.shape[2], clear, 0)
    away = lax.broadcasted_iota(jnp.int32, (depth, depth), 0) - lax.broadcasted_iota(jnp.int32, (depth, depth), 1)
    matrix = jnp.zeros((depth, depth), jnp.float32)
    for k in range(1, REACH + 1):
        matrix = jnp.where((away == k) | (away == -k), scaled_weights[k], matrix)
    band[pl.ds(0, depth), :] = matrix.astype(jnp.bfloat16)
    band[pl.ds(depth, depth), :] = matrix.astype(jnp.bfloat16)
    for copy in copies:
        copy.wait()


def pack(fields, steps):
    cells, rows, depth = fields[0].shape[1:]
    deep = steps * REACH
    wide = cells + 2 * deep
    message = pltpu.VMEM((4 * (deep - REACH) - 2 * REACH, rows, depth), jnp.float32)
    drops = pltpu.VMEM((steps, 2, wide, TILE, depth), jnp.float32)
    band = pltpu.VMEM((2 * depth, depth), jnp.bfloat16)
    buffer = pltpu.VMEM((2, wide, rows + 2 * TILE, depth), jnp.float32)
    vmem = pl.BlockSpec(memory_space=pltpu.VMEM)
    return pl.pallas_call(
        packing_kernel,
        out_shape=(message, message, drops, band, buffer, buffer),
        in_specs=[pl.BlockSpec(memory_space=pltpu.HBM)] * 4,
        out_specs=(vmem,) * 6,
        scratch_shapes=[pltpu.SemaphoreType.DMA((8,))],
        compiler_params=pltpu.CompilerParams(vmem_limit_bytes=8 << 20),
        cost_estimate=pl.CostEstimate(flops=0, bytes_accessed=4 << 20, transcendentals=0),
    )(*map(in_hbm, fields))


def bringing(sems):
    copies = []

    def bring(source, target):
        copy = pltpu.make_async_copy(source, target, sems.at[len(copies)])
        copy.start()
        copies.append(copy)

    return copies, bring


def inject(drops, slab_first, field, places, amps):
    row = lax.broadcasted_iota(jnp.int32, drops.shape[3:], 0)
    col = lax.broadcasted_iota(jnp.int32, drops.shape[3:], 1)

    def one_cell(s, carry):
        x = places[0, 0, s] - slab_first
        inside = (x >= 0) & (x < drops.shape[2])
        x = jnp.clip(x, 0, drops.shape[2] - 1)
        here = (row == places[1, 0, s]) & (col == places[2, 0, s])
        tiles = [drops[step, field, x] for step in range(drops.shape[0])]
        for step, tile in enumerate(tiles):
            amp = jnp.where(inside, amps[0, step, s], 0.0)
            drops[step, field, x] = tile + jnp.where(here, amp, 0.0)
        return carry

    lax.fori_loop(0, places.shape[2], one_cell, 0, unroll=4)


def opening_kernel(
    start,
    count,
    sent_a,
    sent_b,
    speeds,
    band,
    one_in,
    two_in,
    to_a,
    to_b,
    one,
    two,
    courant,
    image,
    grad,
):
    cells, rows, depth = image.shape
    tiles = rows // TILE
    deep = to_a.shape[0]
    near = deep - 2 * REACH
    held = near + REACH
    half = cells // 2
    odd = lax.axis_index("slab") % 2
    start_block = start[0]
    live = count[0]
    sides = ((sent_a, to_a, 1 - odd), (sent_b, to_b, odd))
    inner = pl.ds(TILE, rows)
    for sent, _, side in sides:
        for field in range(2):
            for layer in range(half):
                x = deep + side * half + layer
                one[field, x, inner, :] = sent[field * held + layer + side * (held - half)]
                two[field, x, inner, :] = sent[2 * held + field * near + layer + side * (near - half)]

    def factors(x, carry):
        for tile in range(tiles):
            alive = jnp.where(tile < live, time_step * time_step / SCALE, 0.0)
            speed = speeds[start_block + tile, x]
            at = pl.ds(tile * TILE, TILE)
            courant[deep + x, at, :] = alive * (speed * speed)
            image[x, at, :] = (2.0 * time_step * time_step / SCALE) * speed
        return carry

    lax.fori_loop(0, cells, factors, 0, unroll=4)
    for _, out, side in sides:
        for layer in range(near):
            for tile in range(tiles):
                speed = speeds[start_block + tile, side * (cells - near) + layer]
                out[layer, pl.ds(tile * TILE, TILE), :] = speed
    clear_dead(one, two, live, deep, deep + cells)
    for groups in paired(range(deep + REACH, deep + cells - REACH, REACH)):
        advance(one, two, courant, None, band, 0, groups, grad, True, deep)
    for _, out, side in sides:
        for field in range(2):
            for i in range(REACH):
                x = deep + REACH + (1 - side) * (cells - 3 * REACH) + i
                out[near + field * REACH + i] = two[field, x, inner, :]


def clear_dead(one, two, live, first, last):
    tiles = one.shape[2] // TILE - 2
    for tile in range(1, tiles):

        @pl.when(tile >= live)
        def _():
            def clear(x, carry):
                for buffer in (one, two):
                    for field in range(2):
                        buffer[field, x, pl.ds(TILE + tile * TILE, TILE), :] = jnp.zeros(
                            (TILE, one.shape[3]), jnp.float32
                        )
                return carry

            lax.fori_loop(first, last, clear, 0)


def opening(start, count, sent_a, sent_b, speeds, band, one, two):
    cells, depth = speeds.shape[1], speeds.shape[3]
    rows = sent_a.shape[1]
    wide = one.shape[1]
    message = pltpu.VMEM(((wide - cells) // 2, rows, depth), jnp.float32)
    courant = pltpu.VMEM((wide, rows, depth), jnp.float32)
    layers = pltpu.VMEM((cells, rows, depth), jnp.float32)
    same = [pltpu.VMEM(array.shape, array.dtype) for array in (one, two)]
    vmem = pl.BlockSpec(memory_space=pltpu.VMEM)
    return pl.pallas_call(
        opening_kernel,
        out_shape=(message, message, *same, courant, layers, layers),
        in_specs=[pl.BlockSpec(memory_space=pltpu.SMEM)] * 2 + [vmem] * 6,
        out_specs=(vmem,) * 7,
        input_output_aliases={6: 2, 7: 3},
        compiler_params=pltpu.CompilerParams(vmem_limit_bytes=8 << 20),
        cost_estimate=pl.CostEstimate(flops=4 << 20, bytes_accessed=4 << 20, transcendentals=0),
    )(start, count, sent_a, sent_b, speeds, band, one, two)


def along_z(now, band, field, x):
    rows, depth = now.shape[2] - 2 * TILE, now.shape[3]
    cells = now[field, pl.ds(x, REACH), pl.ds(TILE, rows), :].reshape(REACH * rows, depth)
    high = cells.astype(jnp.bfloat16)
    low = (cells - high.astype(jnp.float32)).astype(jnp.bfloat16)
    return jnp.dot(jnp.concatenate([high, low], axis=1), band[...], preferred_element_type=jnp.float32)


def each_tile(now, band, groups, visit):
    rows = now.shape[2] - 2 * TILE
    spreads = [[along_z(now, band, field, x_first) for field in range(2)] for x_first in groups]
    for g, x_first in enumerate(groups):
        for tile in range(rows // TILE):
            at = TILE + tile * TILE
            pairs = []
            for field in range(2):
                line = [now[field, x_first + i, pl.ds(at, TILE), :] for i in range(-REACH, 2 * REACH)]
                for i in range(REACH):
                    center = line[REACH + i]
                    lap = (3.0 * scaled_weights[0]) * center
                    for k in range(1, REACH + 1):
                        near = line[REACH + i + k] + line[REACH + i - k]
                        near = near + now[field, x_first + i, pl.ds(at + k, TILE), :]
                        near = near + now[field, x_first + i, pl.ds(at - k, TILE), :]
                        lap = lap + scaled_weights[k] * near
                    row = i * rows + tile * TILE
                    pairs.append((center, lap + spreads[g][field][row : row + TILE]))
            for i in range(REACH):
                visit(g, tile, i, (pairs[i], pairs[REACH + i]))


def advance(now, other, courant, drops, band, step, groups, grad, fresh, deep, finals=None):
    def visit(g, tile, i, pair):
        x = groups[g] + i
        own = pl.ds(tile * TILE, TILE)
        padded = pl.ds(TILE + tile * TILE, TILE)
        factor = courant[x, own, :]
        for field, (center, lap) in enumerate(pair):
            ahead = 2.0 * center - other[field, x, padded, :] + factor * lap
            if tile == 0 and drops is not None:
                ahead = ahead + drops[step, field, x]
            if finals is None:
                other[field, x, padded, :] = ahead
            else:
                finals[field, x - deep, own, :] = ahead
        if grad is not None:
            term = pair[1][0] * pair[0][1]
            grad[x - deep, own, :] = term if fresh else grad[x - deep, own, :] + term

    each_tile(now, band, groups, visit)


def add_drops(buffer, drops, layers):
    for field in range(2):
        for x in layers:
            tile = buffer[field, x, pl.ds(TILE, TILE), :]
            buffer[field, x, pl.ds(TILE, TILE), :] = tile + drops[0, field, x]


def early_kernel(
    steps,
    count,
    cells_w_in,
    cells_j_in,
    amps_w_in,
    amps_j_in,
    from_a,
    from_b,
    band,
    drops_in,
    one_in,
    two_in,
    courant_in,
    grad_in,
    drops,
    one,
    two,
    courant,
    grad,
    waiting,
    parts,
    finals,
    cells_w,
    cells_j,
    amps_w,
    amps_j,
    sems,
):
    cells, rows, depth = grad.shape
    deep = steps * REACH
    near = deep - 2 * REACH
    held = near + REACH
    wide = cells + 2 * deep
    odd = lax.axis_index("slab") % 2

    left_of_a = odd
    copies, bring = bringing(sems)
    for source, target in ((cells_w_in, cells_w), (cells_j_in, cells_j), (amps_w_in, amps_w), (amps_j_in, amps_j)):
        bring(source, target)
    inner = pl.ds(TILE, rows)
    for field in range(2):
        for buffer, on_left in ((from_a, left_of_a), (from_b, 1 - left_of_a)):
            at = on_left * (deep - held) + (1 - on_left) * (deep + cells)
            bring(buffer.at[pl.ds(field * held, held)], one.at[field, pl.ds(at, held), inner])
            at = on_left * (deep - near) + (1 - on_left) * (deep + cells)
            bring(buffer.at[pl.ds(2 * held + field * near, near)], two.at[field, pl.ds(at, near), inner])
    def clear_parts(b, carry):
        parts[b] = jnp.zeros(parts.shape[1:], jnp.float32)
        return carry

    lax.fori_loop(0, parts.shape[0], clear_parts, 0)
    for copy in copies:
        copy.wait()
    slab_first = lax.axis_index("slab") * cells - deep
    inject(drops, slab_first, 0, cells_w, amps_w)
    inject(drops, slab_first, 1, cells_j, amps_j)
    add_drops(two, drops, range(deep + REACH, deep + cells - REACH))
    clear_dead(one, two, count[0], 0, deep)
    clear_dead(one, two, count[0], deep + cells, wide)

    def outside(c, carry):
        groups = [deep - near + c * (near + cells) + i for i in range(0, near, REACH)]

        def visit(g, tile, i, pair):
            x = groups[g] + i
            padded = pl.ds(TILE + tile * TILE, TILE)
            for field, (center, lap) in enumerate(pair):
                waiting[field, c * near + g * REACH + i, pl.ds(tile * TILE, TILE), :] = lap
                ahead = 2.0 * center - two[field, x, padded, :]
                two[field, x, padded, :] = ahead + drops[0, field, x] if tile == 0 else ahead

        each_tile(one, band, groups, visit)
        return carry

    advance(one, two, courant, drops, band, 0, [deep, deep + cells - REACH], grad, True, deep)
    lax.fori_loop(0, 2, outside, 0)
    for groups in paired(range(deep + REACH, deep + cells - REACH, REACH)):
        advance(two, one, courant, drops, band, 1, groups, grad, False, deep)

    @pl.when(no_second_partner())
    def _():
        nothing = from_b.at[pl.ds(0, deep)]
        take_side(1 - odd, count[0], nothing, drops, band, waiting, finals, one, two, courant, grad)


def paired(starts):
    starts = list(starts)
    return [starts[i : i + 2] for i in range(0, len(starts), 2)]


def no_second_partner():
    slab = lax.axis_index("slab")
    return (slab == 0) | ((slab % 2 == 1) & (slab == lax.axis_size("slab") - 1))


def take_side(on_left, live, message, drops, band, waiting, finals, one, two, courant, grad):
    cells = grad.shape[0]
    rows = grad.shape[1]
    deep = message.shape[0]
    near = deep - 2 * REACH
    steps = deep // REACH

    def place(left, right):
        return on_left * left + (1 - on_left) * right

    def finish(layer, carry):
        x = place(deep - near, deep + cells) + layer
        h = place(0, near) + layer
        for tile in range(rows // TILE):
            alive = jnp.where(tile < live, time_step * time_step / SCALE, 0.0)
            own = pl.ds(tile * TILE, TILE)
            padded = pl.ds(TILE + tile * TILE, TILE)
            speed = message[layer, own, :]
            factor = alive * (speed * speed)
            courant[x, own, :] = factor
            for field in range(2):
                change = factor * waiting[field, h, own, :]
                two[field, x, padded, :] = two[field, x, padded, :] + change
        return carry

    lax.fori_loop(0, near, finish, 0, unroll=4)
    first = place(deep - near - REACH, deep + cells + near)
    for field in range(2):
        for i in range(REACH):
            two[field, first + i, pl.ds(TILE, rows), :] = message[near + field * REACH + i]
    add_drops(two, drops, [first + i for i in range(REACH)])

    now, other = two, one
    for step in range(1, steps):
        inner = REACH if step == 1 else cells // 2 - REACH * (step - 2)
        depths = range(REACH * (step + 1) - deep, inner, REACH)
        halo = [place(deep + d, deep + cells - REACH - d) for d in depths if d < 0]
        own = [place(deep + d, deep + cells - REACH - d) for d in depths if d >= 0]
        last = finals if step == steps - 1 else None
        if halo:
            advance(now, other, courant, drops, band, step, halo, None, False, deep)
        advance(now, other, courant, drops, band, step, own, grad, False, deep, last)
        now, other = other, now


def first_side_kernel(
    count,
    message,
    drops,
    band,
    waiting,
    finals_in,
    one_in,
    two_in,
    courant_in,
    grad_in,
    finals,
    one,
    two,
    courant,
    grad,
):
    odd = lax.axis_index("slab") % 2
    take_side(odd, count[0], message, drops, band, waiting, finals, one, two, courant, grad)


def second_side_kernel(
    start,
    count,
    message,
    drops,
    band,
    waiting,
    image,
    finals_in,
    one_in,
    two_in,
    courant_in,
    grad_in,
    parts_in,
    finals,
    one,
    two,
    courant,
    grad,
    parts,
):
    cells, rows, _ = image.shape
    deep = message.shape[0]
    steps = deep // REACH
    odd = lax.axis_index("slab") % 2
    start_block = start[0]

    @pl.when(jnp.logical_not(no_second_partner()))
    def _():
        take_side(1 - odd, count[0], message, drops, band, waiting, finals, one, two, courant, grad)

    now, other = (one, two) if steps % 2 else (two, one)
    for step in range(3, steps):
        reach = cells // 2 - REACH * (step - 2)
        for groups in paired(range(deep + reach, deep + cells - reach, REACH)):
            advance(now, other, courant, drops, band, step, groups, grad, False, deep, finals)

    def place(x, carry):
        for tile in range(rows // TILE):
            at = pl.ds(tile * TILE, TILE)
            parts[start_block + tile, x] = image[x, at, :] * grad[x, at, :]
        return carry

    lax.fori_loop(0, cells, place, 0, unroll=4)


def early_steps(count, small, from_a, from_b, courant, band, drops, one, two, grad, groups):
    cells, rows, depth = grad.shape
    steps = drops.shape[0]
    waiting = pltpu.VMEM((2, 2 * (steps - 2) * REACH, rows, depth), jnp.float32)
    parts = pltpu.VMEM((groups, cells, TILE, depth), jnp.float32)
    finals = pltpu.VMEM((2, *grad.shape), jnp.float32)
    vmem = pl.BlockSpec(memory_space=pltpu.VMEM)
    same = [pltpu.VMEM(array.shape, array.dtype) for array in (drops, one, two, courant, grad)]

    def kernel(*refs):
        early_kernel(steps, *refs)

    return pl.pallas_call(
        kernel,
        out_shape=(*same, waiting, parts, finals),
        in_specs=[pl.BlockSpec(memory_space=pltpu.SMEM)]
        + [pl.BlockSpec(memory_space=pltpu.HBM)] * 4
        + [vmem] * 8,
        out_specs=(vmem,) * 8,
        input_output_aliases={8: 0, 9: 1, 10: 2, 11: 3, 12: 4},
        scratch_shapes=[pltpu.SMEM(array.shape, array.dtype) for array in small] + [pltpu.SemaphoreType.DMA((12,))],
        compiler_params=pltpu.CompilerParams(vmem_limit_bytes=8 << 20),
        cost_estimate=pl.CostEstimate(flops=20 << 20, bytes_accessed=4 << 20, transcendentals=0),
    )(count, *map(in_hbm, small), from_a, from_b, band, drops, one, two, courant, grad)


def first_side(count, message, drops, band, waiting, finals, one, two, courant, grad):
    vmem = pl.BlockSpec(memory_space=pltpu.VMEM)
    same = [pltpu.VMEM(array.shape, array.dtype) for array in (finals, one, two, courant, grad)]
    return pl.pallas_call(
        first_side_kernel,
        out_shape=tuple(same),
        in_specs=[pl.BlockSpec(memory_space=pltpu.SMEM)] + [vmem] * 9,
        out_specs=(vmem,) * 5,
        input_output_aliases={5: 0, 6: 1, 7: 2, 8: 3, 9: 4},
        compiler_params=pltpu.CompilerParams(vmem_limit_bytes=8 << 20),
        cost_estimate=pl.CostEstimate(flops=20 << 20, bytes_accessed=3 << 20, transcendentals=0),
    )(count, message, drops, band, waiting, finals, one, two, courant, grad)


def second_side(start, count, message, drops, band, waiting, image, finals, one, two, courant, grad, parts):
    vmem = pl.BlockSpec(memory_space=pltpu.VMEM)
    same = [pltpu.VMEM(array.shape, array.dtype) for array in (finals, one, two, courant, grad, parts)]
    results = pl.pallas_call(
        second_side_kernel,
        out_shape=tuple(same),
        in_specs=[pl.BlockSpec(memory_space=pltpu.SMEM)] * 2 + [vmem] * 11,
        out_specs=(vmem,) * 6,
        input_output_aliases={7: 0, 8: 1, 9: 2, 10: 3, 11: 4, 12: 5},
        compiler_params=pltpu.CompilerParams(vmem_limit_bytes=8 << 20),
        cost_estimate=pl.CostEstimate(flops=20 << 20, bytes_accessed=3 << 20, transcendentals=0),
    )(start, count, message, drops, band, waiting, image, finals, one, two, courant, grad, parts)
    return results[0], results[5]


def closing_kernel(finals, shares, final_w, final_j, gradient, total, sems):
    copies, bring = bringing(sems)
    bring(finals.at[0], final_w.at[0])
    bring(finals.at[1], final_j.at[0])
    value = shares[0]
    for group in range(1, shares.shape[0]):
        value = value + shares[group]
    total[...] = value
    bring(total, gradient)
    for copy in copies:
        copy.wait()


def closing(finals, shares):
    final = jax.ShapeDtypeStruct((1, *finals.shape[1:]), jnp.float32)
    block = shares.shape[1:]
    return pl.pallas_call(
        closing_kernel,
        out_shape=(final, final, jax.ShapeDtypeStruct(block, jnp.float32)),
        in_specs=[pl.BlockSpec(memory_space=pltpu.VMEM)] * 2,
        out_specs=(any_space(),) * 3,
        scratch_shapes=[pltpu.VMEM(block, jnp.float32), pltpu.SemaphoreType.DMA((3,))],
        compiler_params=pltpu.CompilerParams(vmem_limit_bytes=8 << 20),
        cost_estimate=pl.CostEstimate(flops=1 << 20, bytes_accessed=2 << 20, transcendentals=0),
    )(finals, shares)


def per_device(
    velocity,
    aperture_start,
    aperture_count,
    wave_prev,
    wave_now,
    adjoint_prev,
    adjoint_now,
    source_cells,
    wavelet,
    receiver_cells,
    trace,
):
    steps = wavelet.shape[1]
    fields = (wave_now, adjoint_now, wave_prev, adjoint_prev)

    sent_a, sent_b, drops, band, one, two = pack(fields, steps)
    from_a = swap_pairs(sent_a, "slab", 0)
    from_b = swap_pairs(sent_b, "slab", 1)
    speeds = lax.all_gather(velocity, "shot")

    cells_w, cells_j = (jnp.transpose(places, (2, 0, 1)) for places in (source_cells, receiver_cells))
    small = (cells_w, cells_j, wavelet, trace)
    to_a, to_b, one, two, courant, image, grad = opening(
        aperture_start, aperture_count, sent_a, sent_b, speeds, band, one, two
    )
    next_a = swap_pairs(to_a, "slab", 0)
    next_b = swap_pairs(to_b, "slab", 1)
    drops, one, two, courant, grad, waiting, parts, finals = early_steps(
        aperture_count, small, from_a, from_b, courant, band, drops, one, two, grad, lax.axis_size("shot")
    )
    finals, one, two, courant, grad = first_side(
        aperture_count, next_a, drops, band, waiting, finals, one, two, courant, grad
    )
    finals, parts = second_side(
        aperture_start,
        aperture_count,
        next_b,
        drops,
        band,
        waiting,
        image,
        finals,
        one,
        two,
        courant,
        grad,
        parts,
    )
    shares = lax.all_to_all(parts, "shot", 0, 0, tiled=True)
    return closing(finals, shares)


def solution(mesh):
    return jax.shard_map(
        per_device,
        mesh=mesh,
        in_specs=(
            P("slab", "shot", None),
            P("shot"),
            P("shot"),
            P("shot", "slab", None, None),
            P("shot", "slab", None, None),
            P("shot", "slab", None, None),
            P("shot", "slab", None, None),
            P("shot", None, None),
            P("shot", None, None),
            P("shot", None, None),
            P("shot", None, None),
        ),
        out_specs=(
            P("shot", "slab", None, None),
            P("shot", "slab", None, None),
            P("slab", "shot", None),
        ),
        check_vma=False,
    )
```
